512 devices in a mesh: shot: 16 (over z), row: 8 (over y, core), col: 4 (over x).
Axes of the slice: x: 4, y: 4, z: 16, core: 2. Of those that a mesh axis runs over, the one named last changes fastest.
Arguments:
- soft: bfloat16 [12288, 32768], P('shot', ('row', 'col')), may hold values from 0.1 to 0.9, as said below
- partners: int32 [128, 4], P(('row', 'col')), may hold values from -1 to 127, as said below
- incidence: int32 [3, 128, 512], P(None, ('row', 'col')), may hold values from 0 to 255, as said below
- edge_prob: float32 [128, 512], P(('row', 'col')), may hold values from 0.002 to 0.05
Outputs:
- pair_prob: bfloat16 [128, 4, 256, 256], P(('row', 'col'), None, 'shot')
- gradient: float32 [128, 512], P(('row', 'col'))
The draws below stay inside these ranges and needn't reach their ends.
Inputs may be any that keep to these rules, and one draw needn't show every extreme that they name: Slot 0 of block b holds b itself; a live partner lies within 2 blocks of b and the live partners of a block differ. `soft`: each entry lies between 0 and 1 - 0.2 / 2, so gram / 12288 exceeds 0.01. incidence[0] and incidence[2] lie in 0 to 255, incidence[1] in 0 to 3.
All inputs are finite; a program needn't handle non-finite values.
Results may differ from the reference program's by a relative error of at most 0.001.
Values may be sent and summed in bfloat16 or wider, within the bound.
No kernel may reach another device: no remote copies, remote signals or barrier semaphores. Data moves between devices by JAX's collectives and lax.ppermute only.
A program may use at most 64 MiB of HBM per device.

```python
import math
import jax
import jax.numpy as jnp
from jax import lax

BS = 256
K = 4
HALO = 2
EPB = 512
NBLK = 128
DETS = 32768
TOTAL_SHOTS = 12288


def draw_soft(key, part):
    key = jax.random.fold_in(key, 3)
    key_noise, key_shared, key_load = jax.random.split(key, 3)
    noise = jax.random.normal(key_noise, (TOTAL_SHOTS, DETS), jnp.float32)
    loading = jax.random.uniform(key_load, (1, DETS), jnp.float32, -0.8, 0.8)
    shared = jax.random.normal(key_shared, (TOTAL_SHOTS, 1), jnp.float32)
    field = noise + 0.7 * jnp.roll(noise, 1, axis=1) + loading * shared
    return (0.5 + 0.39 * jnp.tanh(0.6 * field)).astype(jnp.bfloat16)


def draw_partners(key, part):
    key = jax.random.fold_in(key, 7)
    key_order, key_keep = jax.random.split(key, 2)
    offsets = jnp.concatenate([jnp.arange(-HALO, 0, dtype=jnp.int32), jnp.arange(1, HALO + 1, dtype=jnp.int32)])
    scores = jax.random.randint(key_order, (NBLK, 2 * HALO), 0, 1 << 20) * (2 * HALO) + jnp.arange(2 * HALO, dtype=jnp.int32)[None, :]
    order = jnp.argsort(scores, axis=1)
    picks = offsets[order[:, :K - 1]]
    block_ids = jnp.arange(NBLK, dtype=jnp.int32)[:, None]
    candidate = block_ids + picks
    keeper = (jax.random.randint(key_keep, (NBLK, K - 1), 0, 3) > 0) & (candidate >= 0) & (candidate < NBLK)
    others = jnp.where(keeper, candidate, -1)
    return jnp.concatenate([block_ids, others], axis=1).astype(jnp.int32)


def draw_incidence(key, part):
    key = jax.random.fold_in(key, 11)
    key_rows, key_slot, key_cols = jax.random.split(key, 3)
    rows_x = jax.random.randint(key_rows, (1, NBLK, EPB), 0, BS)
    slot_x = jax.random.randint(key_slot, (1, NBLK, EPB), 0, K)
    cols_x = jax.random.randint(key_cols, (1, NBLK, EPB), 0, BS)
    return jnp.concatenate([rows_x, slot_x, cols_x], axis=0).astype(jnp.int32)


def steps_of(stream_key, extent, cuts, least, largest):
    loudness = 1.0
    for position, parts in cuts:
        draws = jax.random.uniform(jax.random.fold_in(jax.random.fold_in(stream_key, 6), position), (parts,), jnp.float32, least / len(cuts), largest / len(cuts))
        loudness = loudness * jnp.repeat(jnp.exp(draws), extent[position] // parts).reshape((-1,) + (1,) * (len(extent) - 1 - position))
    return loudness


def setup_inputs(seed: int = 0) -> dict:
    arg_keys = jax.random.split(jax.random.key(seed), 5)
    soft = draw_soft(jax.random.fold_in(arg_keys[4], 71), 0)
    partners = draw_partners(jax.random.fold_in(arg_keys[4], 71), 0)
    incidence = draw_incidence(jax.random.fold_in(arg_keys[4], 71), 0)
    edge_prob = jnp.clip(jnp.exp(math.log(0.05) - 3.218876 * jax.random.uniform(arg_keys[3], (NBLK, EPB), jnp.float32) ** steps_of(arg_keys[3], (NBLK, EPB), ((0, 32),), -0.2, 0.2)), 0.002, 0.05)
    return {"soft": soft, "partners": partners, "incidence": incidence, "edge_prob": edge_prob}


NOISE_SPREAD = 0.05

def pairwise_probability(summed_gram, row_average, column_average, activity_mask, count_of_shots):
    quotient_value = row_average[..., :, None] * column_average[..., None, :] * count_of_shots / summed_gram
    return (0.5 - 0.5 * jnp.sqrt(quotient_value)) * activity_mask[:, :, None, None]

def reference(soft, partners, incidence, edge_prob):
    means = lax.optimization_barrier(jnp.sum(soft, axis=0, dtype=jnp.float32)) / TOTAL_SHOTS
    block_ids = jnp.arange(NBLK, dtype=jnp.int32)
    active_flags = partners >= 0
    chosen = jnp.where(active_flags, partners, block_ids[:, None]).astype(jnp.int32)

    def one_block(pieces):
        index, chosen_row, active_row, rows_x, slot_x, cols_x, probs = pieces
        own_cols = lax.dynamic_slice_in_dim(soft, (index * BS).astype(jnp.int32), BS, 1).astype(jnp.float32)

        def one_slot(partner):
            part_cols = lax.dynamic_slice_in_dim(soft, (partner * BS).astype(jnp.int32), BS, 1).astype(jnp.float32)
            return jnp.dot(own_cols.T, part_cols, precision=lax.Precision.HIGHEST, preferred_element_type=jnp.float32)
        summed_gram = lax.map(one_slot, chosen_row)
        local_average = lax.dynamic_slice_in_dim(means, (index * BS).astype(jnp.int32), BS, 0)
        partial_average = lax.map(lambda partner: lax.dynamic_slice_in_dim(means, (partner * BS).astype(jnp.int32), BS, 0), chosen_row)
        activity_mask = active_row.astype(jnp.float32)
        pairwise_entry = pairwise_probability(summed_gram[None], local_average[None, None, :], partial_average[None], activity_mask[None], float(TOTAL_SHOTS))[0]
        fitted_values = jnp.zeros((K, BS, BS), jnp.float32).at[slot_x, rows_x, cols_x].add(probs)
        fit_residual = activity_mask[:, None, None] * (pairwise_entry - fitted_values) / NOISE_SPREAD
        grads = -fit_residual[slot_x, rows_x, cols_x] / NOISE_SPREAD
        return (pairwise_entry.astype(jnp.bfloat16), grads)
    pairs, grads = lax.map(one_block, (block_ids, chosen, active_flags, incidence[0], incidence[1], incidence[2], edge_prob))
    return (pairs, grads)
```

```python
import functools

import jax
import jax.numpy as jnp
from jax import lax
from jax.experimental import pallas as pl
from jax.experimental.pallas import tpu as pltpu
from jax.sharding import PartitionSpec as P

HALO = 2
NOISE_SPREAD = 0.05


def gram_kernel(
    blocks, slots, width, local_ref, left_ref, own_ref, right_ref, inc_ref, keyt_ref, probt_ref,
    gram_ref, small_ref, fit_ref, ext, sems,
):
    shots = own_ref.shape[0]
    halo = left_ref.shape[1]
    own_width = own_ref.shape[1]
    parts = (
        (left_ref, 0, halo),
        (own_ref, halo, own_width),
        (right_ref, halo + own_width, halo),
    )
    copies = [
        pltpu.make_async_copy(ref, ext.at[:, pl.ds(start, size)], sems.at[n])
        for n, (ref, start, size) in enumerate(parts)
    ]
    for copy in copies:
        copy.start()
    edges = inc_ref.shape[2]
    groups = gram_ref.shape[0]
    share = width // groups
    for b in range(blocks):
        key = inc_ref[1, b : b + 1, :] * (width * width) + inc_ref[0, b : b + 1, :] * width + inc_ref[2, b : b + 1, :]
        same = keyt_ref[:, b : b + 1] == key
        fit_ref[b : b + 1, :] = jnp.sum(jnp.where(same, probt_ref[:, b : b + 1], 0.0), axis=0, keepdims=True)
    for copy in copies:
        copy.wait()
    ones = jnp.ones((8, shots), jnp.bfloat16)
    small_ref[0:1, :] = jnp.dot(ones, ext[...], preferred_element_type=jnp.float32)[0:1, :]
    for b in range(blocks):
        own = ext[:, halo + b * width : halo + (b + 1) * width]
        chosen = []
        for k in range(slots):
            start = pl.multiple_of(local_ref[b * slots + k] * width, width)
            chosen.append(ext[:, pl.ds(start, width)])
        chosen = jnp.concatenate(chosen, axis=1)
        tile = lax.dot_general(own, chosen, (((0,), (0,)), ((), ())), preferred_element_type=jnp.float32)
        for k in range(slots):
            gram_ref[:, b, k] = tile[:, k * width : (k + 1) * width].reshape(groups, share, width)
        row_hot = lax.broadcasted_iota(jnp.int32, (width, edges), 0) == inc_ref[0, b : b + 1, :]
        col_hot = lax.broadcasted_iota(jnp.int32, (slots * width, edges), 0) == (
            inc_ref[1, b : b + 1, :] * width + inc_ref[2, b : b + 1, :]
        )
        row_vals = jnp.dot(own, row_hot.astype(jnp.bfloat16), preferred_element_type=jnp.float32)
        col_vals = jnp.dot(chosen, col_hot.astype(jnp.bfloat16), preferred_element_type=jnp.float32)
        at = slice(b * edges, (b + 1) * edges)
        small_ref[1:2, at] = jnp.sum(row_vals, axis=0, keepdims=True)
        small_ref[2:3, at] = jnp.sum(col_vals, axis=0, keepdims=True)
        small_ref[3:4, at] = jnp.sum(row_vals * col_vals, axis=0, keepdims=True)


def gram_call(local_index, left, own, right, incidence, keys_t, prob_t, groups, slots, width):
    shots, own_width = own.shape
    blocks = own_width // width
    edges = incidence.shape[2]
    any_spec = pl.BlockSpec(memory_space=pl.ANY)
    vmem = pl.BlockSpec(memory_space=pltpu.VMEM)
    ext_width = own_width + 2 * left.shape[1]
    return pl.pallas_call(
        functools.partial(gram_kernel, blocks, slots, width),
        out_shape=(
            jax.ShapeDtypeStruct((groups, blocks, slots, width // groups, width), jnp.float32),
            jax.ShapeDtypeStruct((4, max(ext_width, blocks * edges)), jnp.float32),
            jax.ShapeDtypeStruct((blocks, edges), jnp.float32),
        ),
        in_specs=[pl.BlockSpec(memory_space=pltpu.SMEM), any_spec, any_spec, any_spec, vmem, vmem, vmem],
        out_specs=(vmem, vmem, vmem),
        scratch_shapes=[pltpu.VMEM((shots, ext_width), jnp.bfloat16), pltpu.SemaphoreType.DMA((3,))],
        compiler_params=pltpu.CompilerParams(vmem_limit_bytes=40 * 1024 * 1024),
        cost_estimate=pl.CostEstimate(flops=6_500_000_000, bytes_accessed=8_000_000, transcendentals=0),
    )(local_index, left, own, right, incidence, keys_t, prob_t)


def local(soft, partners, incidence, edge_prob):
    shots, own_width = soft.shape
    blocks, slots = partners.shape
    width = own_width // blocks
    groups = lax.axis_size("shot")
    count = float(shots * groups)
    first = lax.axis_index(("row", "col")) * blocks
    sides = lax.axis_size(("row", "col"))
    reach = HALO * width

    left = lax.ppermute(soft[:, own_width - reach :], ("row", "col"), [(i, (i + 1) % sides) for i in range(sides)])
    right = lax.ppermute(soft[:, :reach], ("row", "col"), [((i + 1) % sides, i) for i in range(sides)])

    own_ids = first + jnp.arange(blocks, dtype=jnp.int32)
    live = partners >= 0
    local_index = (jnp.where(live, partners, own_ids[:, None]) - first + HALO).reshape(-1)
    keys = incidence[1] * (width * width) + incidence[0] * width + incidence[2]
    gram, small, fitted = gram_call(
        local_index, left, soft, right, incidence, keys.T, edge_prob.T, groups, slots, width
    )
    small = lax.psum(small, "shot")
    total = lax.psum_scatter(gram, "shot", scatter_dimension=0, tiled=False)

    mean_blocks = small[0].reshape(blocks + 2 * HALO, width) / count
    share = width // groups
    row_mean = lax.dynamic_slice_in_dim(
        mean_blocks[HALO : HALO + blocks], lax.axis_index("shot") * share, share, 1
    )
    col_mean = jnp.take(mean_blocks, local_index, axis=0).reshape(blocks, slots, width)
    mask = live.astype(jnp.float32)
    quotient = row_mean[:, None, :, None] * col_mean[:, :, None, :] * count / total
    pair = ((0.5 - 0.5 * jnp.sqrt(quotient)) * mask[:, :, None, None]).astype(jnp.bfloat16)

    edge = small[1:].reshape(3, blocks, -1)
    at_edge = (edge[0] / count) * (edge[1] / count) * count / edge[2]
    edge_live = jnp.zeros(edge_prob.shape, jnp.float32)
    for k in range(slots):
        edge_live = edge_live + jnp.where(incidence[1] == k, mask[:, k : k + 1], 0.0)
    residual = edge_live * ((0.5 - 0.5 * jnp.sqrt(at_edge)) * edge_live - fitted) / NOISE_SPREAD
    return (pair, -residual / NOISE_SPREAD)


def solution(mesh):
    placed = (
        P("shot", ("row", "col")),
        P(("row", "col"), None),
        P(None, ("row", "col"), None),
        P(("row", "col"), None),
    )
    return jax.shard_map(
        local,
        mesh=mesh,
        in_specs=placed,
        out_specs=(P(("row", "col"), None, "shot", None), P(("row", "col"), None)),
        check_vma=False,
    )
```

```python
import functools

import jax
import jax.numpy as jnp
from jax import lax
from jax.experimental import pallas as pl
from jax.experimental.pallas import tpu as pltpu
from jax.sharding import PartitionSpec as P

HALO = 2
NOISE_SPREAD = 0.05


def gram_kernel(
    blocks, slots, width, local_ref, left_ref, own_ref, right_ref, inc_ref, keyt_ref, probt_ref,
    gram_ref, small_ref, fit_ref, ext, sems,
):
    shots = own_ref.shape[0]
    halo = left_ref.shape[1]
    own_width = own_ref.shape[1]
    parts = (
        (left_ref, 0, halo),
        (own_ref, halo, own_width),
        (right_ref, halo + own_width, halo),
    )
    copies = [
        pltpu.make_async_copy(ref, ext.at[:, pl.ds(start, size)], sems.at[n])
        for n, (ref, start, size) in enumerate(parts)
    ]
    for copy in copies:
        copy.start()
    edges = inc_ref.shape[2]
    groups = gram_ref.shape[0]
    share = width // groups
    for b in range(blocks):
        key = inc_ref[1, b : b + 1, :] * (width * width) + inc_ref[0, b : b + 1, :] * width + inc_ref[2, b : b + 1, :]
        same = keyt_ref[:, b : b + 1] == key
        fit_ref[b : b + 1, :] = jnp.sum(jnp.where(same, probt_ref[:, b : b + 1], 0.0), axis=0, keepdims=True)
    for copy in copies:
        copy.wait()
    ones = jnp.ones((8, shots), jnp.bfloat16)
    small_ref[0:1, :] = jnp.dot(ones, ext[...], preferred_element_type=jnp.float32)[0:1, :]
    for b in range(blocks):
        own = ext[:, halo + b * width : halo + (b + 1) * width]
        chosen = []
        for k in range(slots):
            start = pl.multiple_of(local_ref[b * slots + k] * width, width)
            chosen.append(ext[:, pl.ds(start, width)])
        chosen = jnp.concatenate(chosen, axis=1)
        tile = lax.dot_general(own, chosen, (((0,), (0,)), ((), ())), preferred_element_type=jnp.float32)
        for k in range(slots):
            gram_ref[:, b, k] = tile[:, k * width : (k + 1) * width].reshape(groups, share, width)
        row_hot = lax.broadcasted_iota(jnp.int32, (width, edges), 0) == inc_ref[0, b : b + 1, :]
        col_hot = lax.broadcasted_iota(jnp.int32, (slots * width, edges), 0) == (
            inc_ref[1, b : b + 1, :] * width + inc_ref[2, b : b + 1, :]
        )
        row_vals = jnp.dot(own, row_hot.astype(jnp.bfloat16), preferred_element_type=jnp.float32)
        col_vals = jnp.dot(chosen, col_hot.astype(jnp.bfloat16), preferred_element_type=jnp.float32)
        at = slice(b * edges, (b + 1) * edges)
        small_ref[1:2, at] = jnp.sum(row_vals, axis=0, keepdims=True)
        small_ref[2:3, at] = jnp.sum(col_vals, axis=0, keepdims=True)
        small_ref[3:4, at] = jnp.sum(row_vals * col_vals, axis=0, keepdims=True)


def gram_call(local_index, left, own, right, incidence, keys_t, prob_t, groups, slots, width):
    shots, own_width = own.shape
    blocks = own_width // width
    edges = incidence.shape[2]
    any_spec = pl.BlockSpec(memory_space=pl.ANY)
    vmem = pl.BlockSpec(memory_space=pltpu.VMEM)
    ext_width = own_width + 2 * left.shape[1]
    return pl.pallas_call(
        functools.partial(gram_kernel, blocks, slots, width),
        out_shape=(
            jax.ShapeDtypeStruct((groups, blocks, slots, width // groups, width), jnp.float32),
            jax.ShapeDtypeStruct((4, max(ext_width, blocks * edges)), jnp.float32),
            jax.ShapeDtypeStruct((blocks, edges), jnp.float32),
        ),
        in_specs=[pl.BlockSpec(memory_space=pltpu.SMEM), any_spec, any_spec, any_spec, vmem, vmem, vmem],
        out_specs=(vmem, vmem, vmem),
        scratch_shapes=[pltpu.VMEM((shots, ext_width), jnp.bfloat16), pltpu.SemaphoreType.DMA((3,))],
        compiler_params=pltpu.CompilerParams(vmem_limit_bytes=40 * 1024 * 1024),
        cost_estimate=pl.CostEstimate(flops=6_500_000_000, bytes_accessed=8_000_000, transcendentals=0),
    )(local_index, left, own, right, incidence, keys_t, prob_t)


def arcs_sum(parts, axis, count):
    me = lax.axis_index(axis)

    def mine(shift):
        return lax.dynamic_index_in_dim(parts, lax.rem(me + shift + count, count), 0, keepdims=False)

    lower = [((i + 1) % count, i) for i in range(count)]
    upper = [(i, (i + 1) % count) for i in range(count)]
    half = count // 2
    down, up = mine(-half), mine(half - 1)
    for step in range(half):
        down = lax.ppermute(down, axis, lower)
        if step < half - 1:
            down = down + mine(step + 1 - half)
            up = lax.ppermute(up, axis, upper)
            if step < half - 2:
                up = up + mine(half - 2 - step)
    return mine(0) + down + up


def local(soft, partners, incidence, edge_prob):
    shots, own_width = soft.shape
    blocks, slots = partners.shape
    width = own_width // blocks
    groups = lax.axis_size("shot")
    count = float(shots * groups)
    first = lax.axis_index(("row", "col")) * blocks
    sides = lax.axis_size(("row", "col"))
    reach = HALO * width

    left = lax.ppermute(soft[:, own_width - reach :], ("row", "col"), [(i, (i + 1) % sides) for i in range(sides)])
    right = lax.ppermute(soft[:, :reach], ("row", "col"), [((i + 1) % sides, i) for i in range(sides)])

    own_ids = first + jnp.arange(blocks, dtype=jnp.int32)
    live = partners >= 0
    local_index = (jnp.where(live, partners, own_ids[:, None]) - first + HALO).reshape(-1)
    keys = incidence[1] * (width * width) + incidence[0] * width + incidence[2]
    gram, small, fitted = gram_call(
        local_index, left, soft, right, incidence, keys.T, edge_prob.T, groups, slots, width
    )
    small = jnp.sum(lax.all_gather(small, "shot"), axis=0)
    total = arcs_sum(gram, "shot", groups)

    mean_blocks = small[0].reshape(blocks + 2 * HALO, width) / count
    share = width // groups
    row_mean = lax.dynamic_slice_in_dim(
        mean_blocks[HALO : HALO + blocks], lax.axis_index("shot") * share, share, 1
    )
    col_mean = jnp.take(mean_blocks, local_index, axis=0).reshape(blocks, slots, width)
    mask = live.astype(jnp.float32)
    quotient = row_mean[:, None, :, None] * col_mean[:, :, None, :] * count / total
    pair = ((0.5 - 0.5 * jnp.sqrt(quotient)) * mask[:, :, None, None]).astype(jnp.bfloat16)

    edge = small[1:].reshape(3, blocks, -1)
    at_edge = (edge[0] / count) * (edge[1] / count) * count / edge[2]
    edge_live = jnp.zeros(edge_prob.shape, jnp.float32)
    for k in range(slots):
        edge_live = edge_live + jnp.where(incidence[1] == k, mask[:, k : k + 1], 0.0)
    residual = edge_live * ((0.5 - 0.5 * jnp.sqrt(at_edge)) * edge_live - fitted) / NOISE_SPREAD
    return (pair, -residual / NOISE_SPREAD)


def solution(mesh):
    placed = (
        P("shot", ("row", "col")),
        P(("row", "col"), None),
        P(None, ("row", "col"), None),
        P(("row", "col"), None),
    )
    return jax.shard_map(
        local,
        mesh=mesh,
        in_specs=placed,
        out_specs=(P(("row", "col"), None, "shot", None), P(("row", "col"), None)),
        check_vma=False,
    )
```

```python
import functools

import jax
import jax.numpy as jnp
from jax import lax
from jax.experimental import pallas as pl
from jax.experimental.pallas import tpu as pltpu
from jax.sharding import PartitionSpec as P

HALO = 2
NOISE_SPREAD = 0.05
SCALE = 131072.0
VMEM = pl.BlockSpec(memory_space=pltpu.VMEM)
ANY = pl.BlockSpec(memory_space=pl.ANY)
SMEM = pl.BlockSpec(memory_space=pltpu.SMEM)
PARAMS = pltpu.CompilerParams(vmem_limit_bytes=40 * 1024 * 1024)


def fixed(values):
    return jnp.floor(values * SCALE + 0.5).astype(jnp.int32)


def place():
    me = lax.axis_index("shot")
    way = 1 - 2 * lax.rem(lax.axis_index("row"), 2)
    first = (lax.axis_index("row") * lax.axis_size("col") + lax.axis_index("col"))
    return me, way, first


def spread(tile, slot, stage, first_ref, keep_ref, give_ref, me, way, groups):
    share = tile.shape[0] // groups
    stage[...] = tile.reshape(groups, share, tile.shape[1])
    half = groups // 2

    def rows(hop):
        return fixed(stage[lax.rem(me + way * hop + 2 * groups, groups)])

    for hop in range(half):
        keep_ref[hop, slot] = rows(hop)
    first_ref[slot] = rows(half)
    for hop in range(1, half):
        give_ref[hop - 1, slot] = rows(-hop)


def self_kernel(width, groups, own_ref, _, first_ref, keep_ref, give_ref, stage):
    me, way, _ = place()
    for b in range(own_ref.shape[1] // width):
        own = own_ref[:, b * width : (b + 1) * width]
        tile = lax.dot_general(own, own, (((0,), (0,)), ((), ())), preferred_element_type=jnp.float32)
        spread(tile, b, stage, first_ref, keep_ref, give_ref, me, way, groups)


def pair_kernel(
    upper, width, groups, partners_ref, halo_ref, own_ref, inc_ref, keyt_ref, probt_ref, _,
    first_ref, keep_ref, give_ref, fit_ref, win, stage,
):
    blocks, slots = partners_ref.shape
    mine = blocks // 2
    low = mine * upper
    edges = inc_ref.shape[2]
    reach = HALO * width
    own_width = own_ref.shape[1]
    me, way, group = place()
    base = group * blocks
    if upper:
        win[:, 0:own_width] = own_ref[...]
        win[:, own_width:] = halo_ref[...]
        window_first = base + low - HALO
    else:
        win[:, 0:reach] = halo_ref[...]
        win[:, reach:] = own_ref[...]
        window_first = base - HALO
    at_own = HALO * width
    share = width // groups
    pieces = edges // width
    small = [[], [], [], []]
    for b in range(mine):
        block = low + b
        own = win[:, at_own + b * width : at_own + (b + 1) * width]
        chosen = [own]
        for k in range(1, slots):
            partner = partners_ref[block, k]
            partner = jnp.where(partner >= 0, partner, base + block)
            start = pl.multiple_of((partner - window_first) * width, width)
            chosen.append(win[:, pl.ds(start, width)])
        chosen = jnp.concatenate(chosen, axis=1)
        tiles = lax.dot_general(
            own, chosen[:, width:], (((0,), (0,)), ((), ())), preferred_element_type=jnp.float32
        )
        for k in range(1, slots):
            spread(
                tiles[:, (k - 1) * width : k * width], b * (slots - 1) + k - 1, stage,
                first_ref, keep_ref, give_ref, me, way, groups,
            )
        rows_x = inc_ref[0, block : block + 1, :]
        slot_x = inc_ref[1, block : block + 1, :]
        cols_x = inc_ref[2, block : block + 1, :]
        row_hot = lax.broadcasted_iota(jnp.int32, (width, edges), 0) == rows_x
        col_hot = lax.broadcasted_iota(jnp.int32, (slots * width, edges), 0) == slot_x * width + cols_x
        row_vals = jnp.dot(own, row_hot.astype(jnp.bfloat16), preferred_element_type=jnp.float32)
        col_vals = jnp.dot(chosen, col_hot.astype(jnp.bfloat16), preferred_element_type=jnp.float32)
        sums = (row_vals * col_vals, row_vals, col_vals)
        for n, values in enumerate(sums):
            total = jnp.sum(values, axis=0, keepdims=True)
            small[n] += [total[:, p * width : (p + 1) * width] for p in range(pieces)]
        key = slot_x * (width * width) + rows_x * width + cols_x
        same = keyt_ref[:, block : block + 1] == key
        fit_ref[b : b + 1, :] = jnp.sum(jnp.where(same, probt_ref[:, block : block + 1], 0.0), axis=0, keepdims=True)
    ones = jnp.ones((8, win.shape[0]), jnp.bfloat16)
    low_col = reach if upper else 0
    columns = jnp.dot(ones, win[:, low_col : low_col + 4 * width], preferred_element_type=jnp.float32)
    small[3] = [columns[0:1, p * width : (p + 1) * width] for p in range(4)]
    rest = fixed(jnp.concatenate(small[0] + small[1] + small[2] + small[3], axis=0))
    last = mine * (slots - 1)
    first_ref[last] = rest
    for hop in range(groups // 2):
        keep_ref[hop, last] = rest
    for hop in range(1, groups // 2):
        give_ref[hop - 1, last] = rest


def pieces_of(slots, groups, share, width):
    shape = (slots, share, width)
    return [
        jax.ShapeDtypeStruct(shape, jnp.int32),
        jax.ShapeDtypeStruct((groups // 2,) + shape, jnp.int32),
        jax.ShapeDtypeStruct((groups // 2 - 1,) + shape, jnp.int32),
    ]


def self_call(soft, after, width, groups):
    blocks = soft.shape[1] // width
    share = width // groups
    return pl.pallas_call(
        functools.partial(self_kernel, width, groups),
        out_shape=pieces_of(blocks, groups, share, width),
        in_specs=[VMEM, ANY],
        out_specs=[VMEM] * 3,
        scratch_shapes=[pltpu.VMEM((groups, share, width), jnp.float32)],
        compiler_params=PARAMS,
        cost_estimate=pl.CostEstimate(flops=400_000_000, bytes_accessed=3_000_000, transcendentals=0),
    )(soft, after)


def pair_call(upper, partners, halo, after, soft, incidence, keys_t, prob_t, width, groups):
    blocks, slots = partners.shape
    share = width // groups
    edges = incidence.shape[2]
    return pl.pallas_call(
        functools.partial(pair_kernel, upper, width, groups),
        out_shape=pieces_of((blocks // 2) * (slots - 1) + 1, groups, share, width)
        + [jax.ShapeDtypeStruct((blocks // 2, edges), jnp.float32)],
        in_specs=[SMEM] + [VMEM] * 5 + [ANY],
        out_specs=[VMEM] * 4,
        scratch_shapes=[
            pltpu.VMEM((soft.shape[0], soft.shape[1] + halo.shape[1]), jnp.bfloat16),
            pltpu.VMEM((groups, share, width), jnp.float32),
        ],
        compiler_params=PARAMS,
        cost_estimate=pl.CostEstimate(flops=3_200_000_000, bytes_accessed=4_000_000, transcendentals=0),
    )(partners, halo, soft, incidence, keys_t, prob_t, after)


def hop_kernel(hop, came_ref, keep_ref, got_ref, *refs):
    out_ref = refs[-1]
    if len(came_ref.shape) == 3:
        out_ref[0] = came_ref[...] + keep_ref[hop]
        out_ref[1] = got_ref[hop - 1]
    else:
        out_ref[0] = came_ref[0] + keep_ref[hop]
        out_ref[1] = came_ref[1] + got_ref[hop - 1]


def hop_call(hop, came, keep, got, after):
    return pl.pallas_call(
        functools.partial(hop_kernel, hop),
        out_shape=jax.ShapeDtypeStruct((2,) + keep.shape[1:], jnp.int32),
        in_specs=[VMEM] * 3 + [ANY] * len(after),
        out_specs=VMEM,
        compiler_params=PARAMS,
        cost_estimate=pl.CostEstimate(flops=100_000, bytes_accessed=600_000, transcendentals=0),
    )(came, keep, got, *after)


def swap(values):
    rows = lax.axis_size("row")
    return lax.ppermute(values, "row", [(r, r ^ 1) for r in range(rows)])


def onward(values):
    groups, rows = lax.axis_size("shot"), lax.axis_size("row")
    pairs = []
    for z in range(groups):
        for r in range(rows):
            pairs.append((z * rows + r, ((z + 1 - 2 * (r % 2)) % groups) * rows + r))
    return lax.ppermute(values, ("shot", "row"), pairs)


def final_kernel(
    width, groups, count, partners_ref, inc_ref, *refs,
):
    (keep_a, came_a, back_a, keep_l, came_l, back_l, keep_u, came_u, back_u, fit_l, fit_u,
     pair_ref, grad_ref, total_l, total_u, means) = refs
    blocks, slots = partners_ref.shape
    mine = blocks // 2
    share = width // groups
    me, _, group = place()
    base = group * blocks
    total_l[...] = (keep_l[0] + came_l[0] + back_l[...]).astype(jnp.float32) * (1.0 / SCALE)
    total_u[...] = (keep_u[0] + came_u[0] + back_u[...]).astype(jnp.float32) * (1.0 / SCALE)
    last = mine * (slots - 1)
    means[0:4, :] = total_l[last, 12:16, :] / count
    means[4:8, :] = total_u[last, 12:16, :] / count
    spot = lax.broadcasted_iota(jnp.int32, (share, width), 1) == (
        lax.broadcasted_iota(jnp.int32, (share, width), 0) + me * share
    )
    for block in range(blocks):
        b = block % mine
        total, fit = (total_l, fit_l) if block < mine else (total_u, fit_u)
        row_mean = jnp.sum(
            jnp.where(spot, means[block + HALO : block + HALO + 1, :], 0.0), axis=1, keepdims=True
        )
        for k in range(slots):
            if k == 0:
                gram = (keep_a[0, block] + came_a[0, block] + back_a[block]).astype(jnp.float32) * (1.0 / SCALE)
                at = block + HALO
                live = jnp.float32(1.0)
            else:
                gram = total[b * (slots - 1) + k - 1]
                partner = partners_ref[block, k]
                live = jnp.where(partner >= 0, 1.0, 0.0)
                at = jnp.where(partner >= 0, partner - base + HALO, block + HALO)
            quotient = row_mean * means[pl.ds(at, 1), :] * count / gram
            pair_ref[block, k] = ((0.5 - 0.5 * jnp.sqrt(quotient)) * live).astype(jnp.bfloat16)
        pieces = inc_ref.shape[2] // width
        for p in range(pieces):
            n = b * pieces + p
            gram = total[last, n : n + 1, :]
            row_mean_x = total[last, 4 + n : 5 + n, :] / count
            col_mean_x = total[last, 8 + n : 9 + n, :] / count
            at = slice(p * width, (p + 1) * width)
            slot_x = inc_ref[1, block : block + 1, at]
            live = jnp.where(slot_x == 0, 1.0, 0.0)
            for k in range(1, slots):
                live = live + jnp.where((slot_x == k) & (partners_ref[block, k] >= 0), 1.0, 0.0)
            quotient = row_mean_x * col_mean_x * count / gram
            entry = (0.5 - 0.5 * jnp.sqrt(quotient)) * live
            residual = live * (entry - fit[b : b + 1, at]) / NOISE_SPREAD
            grad_ref[block : block + 1, at] = -residual / NOISE_SPREAD


def final_call(partners, incidence, sums, fits, width, groups, count):
    blocks, slots = partners.shape
    share = width // groups
    rows = (blocks // 2) * (slots - 1) + 1
    flat = [array for triple in sums for array in triple]
    return pl.pallas_call(
        functools.partial(final_kernel, width, groups, count),
        out_shape=[
            jax.ShapeDtypeStruct((blocks, slots, share, width), jnp.bfloat16),
            jax.ShapeDtypeStruct((blocks, incidence.shape[2]), jnp.float32),
        ],
        in_specs=[SMEM] + [VMEM] * (1 + len(flat) + len(fits)),
        out_specs=[VMEM] * 2,
        scratch_shapes=[
            pltpu.VMEM((rows, share, width), jnp.float32),
            pltpu.VMEM((rows, share, width), jnp.float32),
            pltpu.VMEM((blocks + 2 * HALO, width), jnp.float32),
        ],
        compiler_params=PARAMS,
        cost_estimate=pl.CostEstimate(flops=1_000_000, bytes_accessed=2_000_000, transcendentals=100_000),
    )(partners, incidence, *flat, *fits)


def local(soft, partners, incidence, edge_prob):
    shots, own_width = soft.shape
    blocks, slots = partners.shape
    width = own_width // blocks
    groups = lax.axis_size("shot")
    count = float(shots * groups)
    sides = lax.axis_size(("row", "col"))
    reach = HALO * width

    tail, head = soft[:, own_width - reach :], soft[:, :reach]
    left = lax.ppermute(tail, ("row", "col"), [(i, (i + 1) % sides) for i in range(sides)])
    right = lax.ppermute(head, ("row", "col"), [((i + 1) % sides, i) for i in range(sides)])

    keys = incidence[1] * (width * width) + incidence[0] * width + incidence[2]
    args = (soft, incidence, keys.T, edge_prob.T, width, groups)
    half = groups // 2

    def around(first, keep, give, order):
        steps = [onward(first)]
        got = swap(give)
        for hop in range(half - 1, 0, -1):
            steps.append(onward(hop_call(hop, steps[-1], keep, got, order.get(hop, ()))))
        return steps, (keep, steps[-1], swap(steps[-1][1]))

    early, alone = around(*self_call(soft, tail, width, groups), {})
    lower = pair_call(0, partners, left, early[4], *args)
    upper = pair_call(1, partners, right, early[5], *args)
    order = {half - 2: (early[6],), half - 3: (early[7],), half - 4: (alone[2],)}
    sums = (alone, around(*lower[:3], order)[1], around(*upper[:3], {})[1])
    return final_call(partners, incidence, sums, (lower[3], upper[3]), width, groups, count)


def solution(mesh):
    placed = (
        P("shot", ("row", "col")),
        P(("row", "col"), None),
        P(None, ("row", "col"), None),
        P(("row", "col"), None),
    )
    return jax.shard_map(
        local,
        mesh=mesh,
        in_specs=placed,
        out_specs=(P(("row", "col"), None, "shot", None), P(("row", "col"), None)),
        check_vma=False,
    )
```

```python
import functools

import jax
import jax.numpy as jnp
from jax import lax
from jax.experimental import pallas as pl
from jax.experimental.pallas import tpu as pltpu
from jax.sharding import PartitionSpec as P

HALO = 2
NOISE_SPREAD = 0.05
SCALE = 131072.0
PAIR_SCALE = 1638.0
LOW = (1 << 24) - 1
ANY = pl.BlockSpec(memory_space=pl.ANY)
VMEM = pl.BlockSpec(memory_space=pltpu.VMEM)
SMEM = pl.BlockSpec(memory_space=pltpu.SMEM)
PARAMS = pltpu.CompilerParams(vmem_limit_bytes=48 * 1024 * 1024)


def fixed(values, scale):
    return jnp.floor(values * scale + 0.5).astype(jnp.int32)


def packed(parts):
    a, b, c, d = parts
    return (
        a | ((d & 255) << 24),
        b | (((d >> 8) & 255) << 24),
        c | ((d >> 16) << 24),
    )


def unpacked(words):
    tops = [lax.shift_right_logical(word, 24) for word in words]
    return [word & LOW for word in words] + [tops[0] | (tops[1] << 8) | (tops[2] << 16)]


def group_index():
    return lax.axis_index("row") * lax.axis_size("col") + lax.axis_index("col")


def cut_kernel(soft_ref, head_ref, tail_ref, sems):
    width = soft_ref.shape[1]
    reach = head_ref.shape[1]
    copies = [
        pltpu.make_async_copy(soft_ref.at[:, pl.ds(width - reach, reach)], tail_ref, sems.at[0]),
        pltpu.make_async_copy(soft_ref.at[:, pl.ds(0, reach)], head_ref, sems.at[1]),
    ]
    for copy in copies:
        copy.start()
    for copy in copies:
        copy.wait()


def cut_call(soft, reach):
    shape = jax.ShapeDtypeStruct((soft.shape[0], reach), soft.dtype)
    return pl.pallas_call(
        cut_kernel,
        out_shape=[shape, shape],
        in_specs=[ANY],
        out_specs=[VMEM, VMEM],
        scratch_shapes=[pltpu.SemaphoreType.DMA((2,))],
        compiler_params=PARAMS,
        cost_estimate=pl.CostEstimate(flops=0, bytes_accessed=3_000_000, transcendentals=0),
    )(soft)


def ready_kernel(
    width, slots, own_ref, inc_ref, keyt_ref, probt_ref, _,
    fit_ref, vals_ref, hot_ref, self_ref, small_ref,
):
    blocks = own_ref.shape[1] // width
    edges = inc_ref.shape[2]
    pieces = edges // width
    for b in range(blocks):
        own = own_ref[:, b * width : (b + 1) * width]
        tile = lax.dot_general(own, own, (((0,), (0,)), ((), ())), preferred_element_type=jnp.float32)
        self_ref[b] = fixed(tile, PAIR_SCALE)
        rows_x = inc_ref[0, b : b + 1, :]
        slot_x = inc_ref[1, b : b + 1, :]
        cols_x = inc_ref[2, b : b + 1, :]
        lines = lax.broadcasted_iota(jnp.int32, (width, edges), 0)
        row_hot = (lines == rows_x).astype(jnp.bfloat16)
        for k in range(slots):
            hot_ref[b, k * width : (k + 1) * width, :] = (
                lines == jnp.where(slot_x == k, cols_x, -1)
            ).astype(jnp.bfloat16)
        vals = jnp.dot(own, row_hot, preferred_element_type=jnp.float32)
        vals_ref[b] = vals.astype(jnp.bfloat16)
        total = jnp.sum(vals, axis=0, keepdims=True)
        for p in range(pieces):
            n = b * pieces + p
            small_ref[n : n + 1, :] = total[:, p * width : (p + 1) * width]
        key = slot_x * (width * width) + rows_x * width + cols_x
        same = keyt_ref[:, b : b + 1] == key
        fit_ref[b : b + 1, :] = jnp.sum(jnp.where(same, probt_ref[:, b : b + 1], 0.0), axis=0, keepdims=True)


def ready_call(soft, incidence, keys_t, prob_t, after, width, slots):
    shots, own_width = soft.shape
    blocks = own_width // width
    edges = incidence.shape[2]
    return pl.pallas_call(
        functools.partial(ready_kernel, width, slots),
        out_shape=[
            jax.ShapeDtypeStruct((blocks, edges), jnp.float32),
            jax.ShapeDtypeStruct((blocks, shots, edges), jnp.bfloat16),
            jax.ShapeDtypeStruct((blocks, slots * width, edges), jnp.bfloat16),
            jax.ShapeDtypeStruct((blocks, width, width), jnp.int32),
            jax.ShapeDtypeStruct((blocks * edges // width, width), jnp.float32),
        ],
        in_specs=[VMEM] * 4 + [ANY],
        out_specs=[VMEM] * 5,
        compiler_params=PARAMS,
        cost_estimate=pl.CostEstimate(flops=20_000_000_000, bytes_accessed=12_000_000, transcendentals=0),
    )(soft, incidence, keys_t, prob_t, after)


def pair_kernel(
    upper, width, groups, partners_ref, halo_ref, own_ref, vals_ref, hot_ref, self_ref, early_ref, _,
    first_ref, parts_ref, win,
):
    blocks, slots = partners_ref.shape
    mine = blocks // 2
    low = mine * upper
    reach = HALO * width
    own_width = own_ref.shape[1]
    share = width // groups
    pieces = hot_ref.shape[2] // width
    me = lax.axis_index("shot")
    base = group_index() * blocks
    if upper:
        win[:, 0:own_width] = own_ref[...]
        win[:, own_width:] = halo_ref[...]
        window_first = base + low - HALO
    else:
        win[:, 0:reach] = halo_ref[...]
        win[:, reach:] = own_ref[...]
        window_first = base - HALO
    products, others = [], []
    for b in range(mine):
        block = low + b
        own = win[:, reach + b * width : reach + (b + 1) * width]
        chosen = [own]
        for k in range(1, slots):
            partner = partners_ref[block, k]
            partner = jnp.where(partner >= 0, partner, base + block)
            start = pl.multiple_of((partner - window_first) * width, width)
            chosen.append(win[:, pl.ds(start, width)])
        chosen = jnp.concatenate(chosen, axis=1)
        tiles = lax.dot_general(
            own, chosen[:, width:], (((0,), (0,)), ((), ())), preferred_element_type=jnp.float32
        )
        tiles = fixed(tiles, PAIR_SCALE)
        for d in range(groups):
            rows = slice(d * share, (d + 1) * share)
            values = [self_ref[block, rows, :]]
            values += [tiles[rows, k * width : (k + 1) * width] for k in range(slots - 1)]
            at = lax.rem(d - me + groups, groups)
            for n, word in enumerate(packed(values)):
                parts_ref[at, b * (slots - 1) + n] = word
        other = jnp.dot(chosen, hot_ref[block], preferred_element_type=jnp.float32)
        product = jnp.sum(vals_ref[block].astype(jnp.float32) * other, axis=0, keepdims=True)
        other = jnp.sum(other, axis=0, keepdims=True)
        products += [product[:, p * width : (p + 1) * width] for p in range(pieces)]
        others += [other[:, p * width : (p + 1) * width] for p in range(pieces)]
    ones = jnp.ones((8, win.shape[0]), jnp.bfloat16)
    low_col = reach if upper else 0
    columns = jnp.dot(ones, win[:, low_col : low_col + 4 * width], preferred_element_type=jnp.float32)
    columns = [columns[0:1, p * width : (p + 1) * width] for p in range(4)]
    early = early_ref[upper * mine * pieces : (upper + 1) * mine * pieces, :]
    rest = fixed(jnp.concatenate(products + [early] + others + columns, axis=0), SCALE)
    last = mine * (slots - 1)
    for at in range(groups):
        parts_ref[at, last] = rest
    first_ref[...] = parts_ref[groups // 2]


def pair_call(upper, partners, halo, soft, vals, hot, selfs, early, after, width, groups):
    blocks, slots = partners.shape
    shape = ((blocks // 2) * (slots - 1) + 1, width // groups, width)
    return pl.pallas_call(
        functools.partial(pair_kernel, upper, width, groups),
        out_shape=[
            jax.ShapeDtypeStruct(shape, jnp.int32),
            jax.ShapeDtypeStruct((groups,) + shape, jnp.int32),
        ],
        in_specs=[SMEM] + [VMEM] * 6 + [ANY],
        out_specs=[VMEM] * 2,
        scratch_shapes=[pltpu.VMEM((soft.shape[0], soft.shape[1] + halo.shape[1]), jnp.bfloat16)],
        compiler_params=PARAMS,
        cost_estimate=pl.CostEstimate(flops=3_000_000_000, bytes_accessed=4_000_000, transcendentals=0),
    )(partners, halo, soft, vals, hot, selfs, early, after)


def plus(a, b):
    words = a.shape[0] - 1
    out = []
    for n in range(0, words, 3):
        one, two = unpacked([a[n + i] for i in range(3)]), unpacked([b[n + i] for i in range(3)])
        out += packed([x + y for x, y in zip(one, two)])
    return out + [a[words] + b[words]]


def hop_kernel(at, start, came_ref, lower_ref, upper_ref, _, out_ref):
    half = lower_ref.shape[1]
    if start == 0:
        sources = ((came_ref, 0), (None, 0))
    elif start == 1:
        sources = ((None, 0), (came_ref, 0))
    else:
        sources = ((came_ref, 0), (came_ref, half))
    for (came, low), mine, base in zip(sources, (lower_ref, upper_ref), (0, half)):
        if came is None:
            out_ref[base : base + half] = mine[at]
        else:
            for n, word in enumerate(plus(came[low : low + half], mine[at])):
                out_ref[base + n] = word


def hop_call(at, start, came, lower, upper, after):
    return pl.pallas_call(
        functools.partial(hop_kernel, at, start),
        out_shape=jax.ShapeDtypeStruct((2 * lower.shape[1],) + lower.shape[2:], jnp.int32),
        in_specs=[VMEM] * 3 + [ANY],
        out_specs=VMEM,
        compiler_params=PARAMS,
        cost_estimate=pl.CostEstimate(flops=100_000, bytes_accessed=600_000, transcendentals=0),
    )(came, lower, upper, after)


def final_kernel(
    count, partners_ref, inc_ref, lower_ref, upper_ref, rising_ref, falling_ref, fit_ref,
    pair_ref, grad_ref, means,
):
    blocks, slots = partners_ref.shape
    mine = blocks // 2
    half, share, width = lower_ref.shape[1:]
    pieces = inc_ref.shape[2] // width
    me = lax.axis_index("shot")
    base = group_index() * blocks
    last = half - 1
    grams, smalls = [], []
    for part, low in ((lower_ref, 0), (upper_ref, half)):
        sources = (part[0], rising_ref[low : low + half], falling_ref[low : low + half])
        for b in range(mine):
            parts = [unpacked([source[b * (slots - 1) + n] for n in range(3)]) for source in sources]
            grams.append([
                (x + y + z).astype(jnp.float32) * (1.0 / PAIR_SCALE) for x, y, z in zip(*parts)
            ])
        smalls.append((sources[0][last] + sources[1][last] + sources[2][last]).astype(jnp.float32) * (1.0 / SCALE))
    means[0:4, :] = smalls[0][12:16] / count
    means[4:8, :] = smalls[1][12:16] / count
    spot = lax.broadcasted_iota(jnp.int32, (share, width), 1) == (
        lax.broadcasted_iota(jnp.int32, (share, width), 0) + me * share
    )
    for block in range(blocks):
        small = smalls[block // mine]
        row_mean = jnp.sum(
            jnp.where(spot, means[block + HALO : block + HALO + 1, :], 0.0), axis=1, keepdims=True
        )
        for k in range(slots):
            partner = partners_ref[block, k]
            live = jnp.where(partner >= 0, 1.0, 0.0)
            at = jnp.where(partner >= 0, partner - base, block) + HALO
            quotient = row_mean * means[pl.ds(at, 1), :] * count / grams[block][k]
            pair_ref[block, k] = ((0.5 - 0.5 * jnp.sqrt(quotient)) * live).astype(jnp.bfloat16)
        for p in range(pieces):
            n = (block % mine) * pieces + p
            at = slice(p * width, (p + 1) * width)
            slot_x = inc_ref[1, block : block + 1, at]
            live = jnp.zeros((1, width), jnp.float32)
            for k in range(slots):
                live = live + jnp.where((slot_x == k) & (partners_ref[block, k] >= 0), 1.0, 0.0)
            quotient = (small[4 + n : 5 + n] / count) * (small[8 + n : 9 + n] / count) * count / small[n : n + 1]
            entry = (0.5 - 0.5 * jnp.sqrt(quotient)) * live
            residual = live * (entry - fit_ref[block : block + 1, at]) / NOISE_SPREAD
            grad_ref[block : block + 1, at] = -residual / NOISE_SPREAD


def final_call(partners, incidence, lower, upper, rising, falling, fit, count):
    blocks, slots = partners.shape
    share, width = lower.shape[2:]
    return pl.pallas_call(
        functools.partial(final_kernel, count),
        out_shape=[
            jax.ShapeDtypeStruct((blocks, slots, share, width), jnp.bfloat16),
            jax.ShapeDtypeStruct((blocks, incidence.shape[2]), jnp.float32),
        ],
        in_specs=[SMEM] + [VMEM] * 6,
        out_specs=[VMEM] * 2,
        scratch_shapes=[pltpu.VMEM((blocks + 2 * HALO, width), jnp.float32)],
        compiler_params=PARAMS,
        cost_estimate=pl.CostEstimate(flops=1_000_000, bytes_accessed=2_000_000, transcendentals=100_000),
    )(partners, incidence, lower, upper, rising, falling, fit)


def local(soft, partners, incidence, edge_prob):
    shots, own_width = soft.shape
    blocks, slots = partners.shape
    width = own_width // blocks
    groups = lax.axis_size("shot")
    count = float(shots * groups)
    sides = lax.axis_size(("row", "col"))

    head, tail = cut_call(soft, HALO * width)
    left = lax.ppermute(tail, ("row", "col"), [(i, (i + 1) % sides) for i in range(sides)])
    right = lax.ppermute(head, ("row", "col"), [((i + 1) % sides, i) for i in range(sides)])

    keys = incidence[1] * (width * width) + incidence[0] * width + incidence[2]
    fit, vals, hot, selfs, early = ready_call(soft, incidence, keys.T, edge_prob.T, tail, width, slots)
    args = (soft, vals, hot, selfs, early)
    first_up, lower = pair_call(0, partners, left, *args, early, width, groups)
    first_down, upper = pair_call(1, partners, right, *args, first_up, width, groups)

    half = groups // 2
    rise = [(i, (i + 1) % groups) for i in range(groups)]
    fall = [((i + 1) % groups, i) for i in range(groups)]
    rising = lax.ppermute(first_up, "shot", rise)
    falling = lax.ppermute(first_down, "shot", fall)
    order = first_down
    for step in range(1, half):
        start = 0 if step == 1 else 2
        order = hop_call(half - step, start, rising, lower, upper, order)
        rising = lax.ppermute(order, "shot", rise)
        start = 1 if step == 1 else 2
        order = hop_call(half + step, start, falling, lower, upper, order)
        falling = lax.ppermute(order, "shot", fall)
    return final_call(partners, incidence, lower, upper, rising, falling, fit, count)


def solution(mesh):
    placed = (
        P("shot", ("row", "col")),
        P(("row", "col"), None),
        P(None, ("row", "col"), None),
        P(("row", "col"), None),
    )
    return jax.shard_map(
        local,
        mesh=mesh,
        in_specs=placed,
        out_specs=(P(("row", "col"), None, "shot", None), P(("row", "col"), None)),
        check_vma=False,
    )
```

```python
import functools

import jax
import jax.numpy as jnp
from jax import lax
from jax.experimental import pallas as pl
from jax.experimental.pallas import tpu as pltpu
from jax.sharding import PartitionSpec as P

HALO = 2
NOISE_SPREAD = 0.05
SCALE = 131072.0
PAIR_SCALE = 1638.0
LOW = (1 << 24) - 1
ANY = pl.BlockSpec(memory_space=pl.ANY)
VMEM = pl.BlockSpec(memory_space=pltpu.VMEM)
SMEM = pl.BlockSpec(memory_space=pltpu.SMEM)
PARAMS = pltpu.CompilerParams(vmem_limit_bytes=48 * 1024 * 1024)


def fixed(values, scale):
    return jnp.floor(values * scale + 0.5).astype(jnp.int32)


def packed(parts):
    a, b, c, d = parts
    return (
        a | ((d & 255) << 24),
        b | (((d >> 8) & 255) << 24),
        c | ((d >> 16) << 24),
    )


def unpacked(words):
    tops = [lax.shift_right_logical(word, 24) for word in words]
    return [word & LOW for word in words] + [tops[0] | (tops[1] << 8) | (tops[2] << 16)]


def ring_place(z, count):
    return jnp.where(lax.rem(z, 2) == 0, z // 2, count - 1 - z // 2)


def ring_order(count):
    return list(range(0, count, 2)) + list(range(count - 1, 0, -2))


def group_index():
    return lax.axis_index("row") * lax.axis_size("col") + lax.axis_index("col")


def cut_kernel(soft_ref, head_ref, tail_ref, sems):
    width = soft_ref.shape[1]
    reach = head_ref.shape[1]
    copies = [
        pltpu.make_async_copy(soft_ref.at[:, pl.ds(width - reach, reach)], tail_ref, sems.at[0]),
        pltpu.make_async_copy(soft_ref.at[:, pl.ds(0, reach)], head_ref, sems.at[1]),
    ]
    for copy in copies:
        copy.start()
    for copy in copies:
        copy.wait()


def cut_call(soft, reach):
    shape = jax.ShapeDtypeStruct((soft.shape[0], reach), soft.dtype)
    return pl.pallas_call(
        cut_kernel,
        out_shape=[shape, shape],
        in_specs=[ANY],
        out_specs=[VMEM, VMEM],
        scratch_shapes=[pltpu.SemaphoreType.DMA((2,))],
        compiler_params=PARAMS,
        cost_estimate=pl.CostEstimate(flops=0, bytes_accessed=3_000_000, transcendentals=0),
    )(soft)


def ready_kernel(
    width, slots, own_ref, inc_ref, keyt_ref, probt_ref, _,
    fit_ref, vals_ref, hot_ref, self_ref, small_ref,
):
    blocks = own_ref.shape[1] // width
    edges = inc_ref.shape[2]
    pieces = edges // width
    for b in range(blocks):
        own = own_ref[:, b * width : (b + 1) * width]
        tile = lax.dot_general(own, own, (((0,), (0,)), ((), ())), preferred_element_type=jnp.float32)
        self_ref[b] = fixed(tile, PAIR_SCALE)
        rows_x = inc_ref[0, b : b + 1, :]
        slot_x = inc_ref[1, b : b + 1, :]
        cols_x = inc_ref[2, b : b + 1, :]
        lines = lax.broadcasted_iota(jnp.int32, (width, edges), 0)
        row_hot = (lines == rows_x).astype(jnp.bfloat16)
        for k in range(slots):
            hot_ref[b, k * width : (k + 1) * width, :] = (
                lines == jnp.where(slot_x == k, cols_x, -1)
            ).astype(jnp.bfloat16)
        vals = jnp.dot(own, row_hot, preferred_element_type=jnp.float32)
        vals_ref[b] = vals.astype(jnp.bfloat16)
        total = jnp.sum(vals, axis=0, keepdims=True)
        for p in range(pieces):
            n = b * pieces + p
            small_ref[n : n + 1, :] = total[:, p * width : (p + 1) * width]
        key = slot_x * (width * width) + rows_x * width + cols_x
        same = keyt_ref[:, b : b + 1] == key
        fit_ref[b : b + 1, :] = jnp.sum(jnp.where(same, probt_ref[:, b : b + 1], 0.0), axis=0, keepdims=True)


def ready_call(soft, incidence, keys_t, prob_t, after, width, slots):
    shots, own_width = soft.shape
    blocks = own_width // width
    edges = incidence.shape[2]
    return pl.pallas_call(
        functools.partial(ready_kernel, width, slots),
        out_shape=[
            jax.ShapeDtypeStruct((blocks, edges), jnp.float32),
            jax.ShapeDtypeStruct((blocks, shots, edges), jnp.bfloat16),
            jax.ShapeDtypeStruct((blocks, slots * width, edges), jnp.bfloat16),
            jax.ShapeDtypeStruct((blocks, width, width), jnp.int32),
            jax.ShapeDtypeStruct((blocks * edges // width, width), jnp.float32),
        ],
        in_specs=[VMEM] * 4 + [ANY],
        out_specs=[VMEM] * 5,
        compiler_params=PARAMS,
        cost_estimate=pl.CostEstimate(flops=20_000_000_000, bytes_accessed=12_000_000, transcendentals=0),
    )(soft, incidence, keys_t, prob_t, after)


def pair_kernel(
    upper, width, groups, partners_ref, halo_ref, own_ref, vals_ref, hot_ref, self_ref, early_ref, _,
    first_ref, parts_ref, win,
):
    blocks, slots = partners_ref.shape
    mine = blocks // 2
    low = mine * upper
    reach = HALO * width
    own_width = own_ref.shape[1]
    share = width // groups
    pieces = hot_ref.shape[2] // width
    place = ring_place(lax.axis_index("shot"), groups)
    places = ring_order(groups)
    base = group_index() * blocks
    if upper:
        win[:, 0:own_width] = own_ref[...]
        win[:, own_width:] = halo_ref[...]
        window_first = base + low - HALO
    else:
        win[:, 0:reach] = halo_ref[...]
        win[:, reach:] = own_ref[...]
        window_first = base - HALO
    products, others = [], []
    for b in range(mine):
        block = low + b
        own = win[:, reach + b * width : reach + (b + 1) * width]
        chosen = [own]
        for k in range(1, slots):
            partner = partners_ref[block, k]
            partner = jnp.where(partner >= 0, partner, base + block)
            start = pl.multiple_of((partner - window_first) * width, width)
            chosen.append(win[:, pl.ds(start, width)])
        chosen = jnp.concatenate(chosen, axis=1)
        tiles = lax.dot_general(
            own, chosen[:, width:], (((0,), (0,)), ((), ())), preferred_element_type=jnp.float32
        )
        tiles = fixed(tiles, PAIR_SCALE)
        for d in range(groups):
            rows = slice(d * share, (d + 1) * share)
            values = [self_ref[block, rows, :]]
            values += [tiles[rows, k * width : (k + 1) * width] for k in range(slots - 1)]
            at = lax.rem(places.index(d) - place + groups, groups)
            for n, word in enumerate(packed(values)):
                parts_ref[at, b * (slots - 1) + n] = word
        other = jnp.dot(chosen, hot_ref[block], preferred_element_type=jnp.float32)
        product = jnp.sum(vals_ref[block].astype(jnp.float32) * other, axis=0, keepdims=True)
        other = jnp.sum(other, axis=0, keepdims=True)
        products += [product[:, p * width : (p + 1) * width] for p in range(pieces)]
        others += [other[:, p * width : (p + 1) * width] for p in range(pieces)]
    ones = jnp.ones((8, win.shape[0]), jnp.bfloat16)
    low_col = reach if upper else 0
    columns = jnp.dot(ones, win[:, low_col : low_col + 4 * width], preferred_element_type=jnp.float32)
    columns = [columns[0:1, p * width : (p + 1) * width] for p in range(4)]
    early = early_ref[upper * mine * pieces : (upper + 1) * mine * pieces, :]
    rest = fixed(jnp.concatenate(products + [early] + others + columns, axis=0), SCALE)
    last = mine * (slots - 1)
    for at in range(groups):
        parts_ref[at, last] = rest
    first_ref[...] = parts_ref[groups // 2]


def pair_call(upper, partners, halo, soft, vals, hot, selfs, early, after, width, groups):
    blocks, slots = partners.shape
    shape = ((blocks // 2) * (slots - 1) + 1, width // groups, width)
    return pl.pallas_call(
        functools.partial(pair_kernel, upper, width, groups),
        out_shape=[
            jax.ShapeDtypeStruct(shape, jnp.int32),
            jax.ShapeDtypeStruct((groups,) + shape, jnp.int32),
        ],
        in_specs=[SMEM] + [VMEM] * 6 + [ANY],
        out_specs=[VMEM] * 2,
        scratch_shapes=[pltpu.VMEM((soft.shape[0], soft.shape[1] + halo.shape[1]), jnp.bfloat16)],
        compiler_params=PARAMS,
        cost_estimate=pl.CostEstimate(flops=3_000_000_000, bytes_accessed=4_000_000, transcendentals=0),
    )(partners, halo, soft, vals, hot, selfs, early, after)


def plus(a, b):
    words = a.shape[0] - 1
    out = []
    for n in range(0, words, 3):
        one, two = unpacked([a[n + i] for i in range(3)]), unpacked([b[n + i] for i in range(3)])
        out += packed([x + y for x, y in zip(one, two)])
    return out + [a[words] + b[words]]


def hop_kernel(at, start, came_ref, lower_ref, upper_ref, _, out_ref):
    half = lower_ref.shape[1]
    if start == 0:
        sources = ((came_ref, 0), (None, 0))
    elif start == 1:
        sources = ((None, 0), (came_ref, 0))
    else:
        sources = ((came_ref, 0), (came_ref, half))
    for (came, low), mine, base in zip(sources, (lower_ref, upper_ref), (0, half)):
        if came is None:
            out_ref[base : base + half] = mine[at]
        else:
            for n, word in enumerate(plus(came[low : low + half], mine[at])):
                out_ref[base + n] = word


def hop_call(at, start, came, lower, upper, after):
    return pl.pallas_call(
        functools.partial(hop_kernel, at, start),
        out_shape=jax.ShapeDtypeStruct((2 * lower.shape[1],) + lower.shape[2:], jnp.int32),
        in_specs=[VMEM] * 3 + [ANY],
        out_specs=VMEM,
        compiler_params=PARAMS,
        cost_estimate=pl.CostEstimate(flops=100_000, bytes_accessed=600_000, transcendentals=0),
    )(came, lower, upper, after)


def final_kernel(
    count, partners_ref, inc_ref, lower_ref, upper_ref, rising_ref, falling_ref, fit_ref,
    pair_ref, grad_ref, means,
):
    blocks, slots = partners_ref.shape
    mine = blocks // 2
    half, share, width = lower_ref.shape[1:]
    pieces = inc_ref.shape[2] // width
    me = lax.axis_index("shot")
    base = group_index() * blocks
    last = half - 1
    grams, smalls = [], []
    for part, low in ((lower_ref, 0), (upper_ref, half)):
        sources = (part[0], rising_ref[low : low + half], falling_ref[low : low + half])
        for b in range(mine):
            parts = [unpacked([source[b * (slots - 1) + n] for n in range(3)]) for source in sources]
            grams.append([
                (x + y + z).astype(jnp.float32) * (1.0 / PAIR_SCALE) for x, y, z in zip(*parts)
            ])
        smalls.append((sources[0][last] + sources[1][last] + sources[2][last]).astype(jnp.float32) * (1.0 / SCALE))
    means[0:4, :] = smalls[0][12:16] / count
    means[4:8, :] = smalls[1][12:16] / count
    spot = lax.broadcasted_iota(jnp.int32, (share, width), 1) == (
        lax.broadcasted_iota(jnp.int32, (share, width), 0) + me * share
    )
    for block in range(blocks):
        small = smalls[block // mine]
        row_mean = jnp.sum(
            jnp.where(spot, means[block + HALO : block + HALO + 1, :], 0.0), axis=1, keepdims=True
        )
        for k in range(slots):
            partner = partners_ref[block, k]
            live = jnp.where(partner >= 0, 1.0, 0.0)
            at = jnp.where(partner >= 0, partner - base, block) + HALO
            quotient = row_mean * means[pl.ds(at, 1), :] * count / grams[block][k]
            pair_ref[block, k] = ((0.5 - 0.5 * jnp.sqrt(quotient)) * live).astype(jnp.bfloat16)
        for p in range(pieces):
            n = (block % mine) * pieces + p
            at = slice(p * width, (p + 1) * width)
            slot_x = inc_ref[1, block : block + 1, at]
            live = jnp.zeros((1, width), jnp.float32)
            for k in range(slots):
                live = live + jnp.where((slot_x == k) & (partners_ref[block, k] >= 0), 1.0, 0.0)
            quotient = (small[4 + n : 5 + n] / count) * (small[8 + n : 9 + n] / count) * count / small[n : n + 1]
            entry = (0.5 - 0.5 * jnp.sqrt(quotient)) * live
            residual = live * (entry - fit_ref[block : block + 1, at]) / NOISE_SPREAD
            grad_ref[block : block + 1, at] = -residual / NOISE_SPREAD


def final_call(partners, incidence, lower, upper, rising, falling, fit, count):
    blocks, slots = partners.shape
    share, width = lower.shape[2:]
    return pl.pallas_call(
        functools.partial(final_kernel, count),
        out_shape=[
            jax.ShapeDtypeStruct((blocks, slots, share, width), jnp.bfloat16),
            jax.ShapeDtypeStruct((blocks, incidence.shape[2]), jnp.float32),
        ],
        in_specs=[SMEM] + [VMEM] * 6,
        out_specs=[VMEM] * 2,
        scratch_shapes=[pltpu.VMEM((blocks + 2 * HALO, width), jnp.float32)],
        compiler_params=PARAMS,
        cost_estimate=pl.CostEstimate(flops=1_000_000, bytes_accessed=2_000_000, transcendentals=100_000),
    )(partners, incidence, lower, upper, rising, falling, fit)


def local(soft, partners, incidence, edge_prob):
    shots, own_width = soft.shape
    blocks, slots = partners.shape
    width = own_width // blocks
    groups = lax.axis_size("shot")
    count = float(shots * groups)
    sides = lax.axis_size(("row", "col"))

    head, tail = cut_call(soft, HALO * width)
    left = lax.ppermute(tail, ("row", "col"), [(i, (i + 1) % sides) for i in range(sides)])
    right = lax.ppermute(head, ("row", "col"), [((i + 1) % sides, i) for i in range(sides)])

    keys = incidence[1] * (width * width) + incidence[0] * width + incidence[2]
    fit, vals, hot, selfs, early = ready_call(soft, incidence, keys.T, edge_prob.T, tail, width, slots)
    args = (soft, vals, hot, selfs, early)
    first_up, lower = pair_call(0, partners, left, *args, early, width, groups)
    first_down, upper = pair_call(1, partners, right, *args, first_up, width, groups)

    half = groups // 2
    places = ring_order(groups)
    rise = [(places[i], places[(i + 1) % groups]) for i in range(groups)]
    fall = [(b, a) for a, b in rise]
    rising = lax.ppermute(first_up, "shot", rise)
    falling = lax.ppermute(first_down, "shot", fall)
    order = first_down
    for step in range(1, half):
        start = 0 if step == 1 else 2
        order = hop_call(half - step, start, rising, lower, upper, order)
        rising = lax.ppermute(order, "shot", rise)
        start = 1 if step == 1 else 2
        order = hop_call(half + step, start, falling, lower, upper, order)
        falling = lax.ppermute(order, "shot", fall)
    return final_call(partners, incidence, lower, upper, rising, falling, fit, count)


def solution(mesh):
    placed = (
        P("shot", ("row", "col")),
        P(("row", "col"), None),
        P(None, ("row", "col"), None),
        P(("row", "col"), None),
    )
    return jax.shard_map(
        local,
        mesh=mesh,
        in_specs=placed,
        out_specs=(P(("row", "col"), None, "shot", None), P(("row", "col"), None)),
        check_vma=False,
    )
```

```python
import functools

import jax
import jax.numpy as jnp
from jax import lax
from jax.experimental import pallas as pl
from jax.experimental.pallas import tpu as pltpu
from jax.sharding import PartitionSpec as P

HALO = 2
NOISE_SPREAD = 0.05
SCALE = 131072.0
UNIT = 1600.0 / 65535.0
SHOTS = 768
TAIL = 40
ANY = pl.BlockSpec(memory_space=pl.ANY)
VMEM = pl.BlockSpec(memory_space=pltpu.VMEM)
SMEM = pl.BlockSpec(memory_space=pltpu.SMEM)
PARAMS = pltpu.CompilerParams(vmem_limit_bytes=48 * 1024 * 1024)


def fixed(values):
    return jnp.floor(values * SCALE + 0.5).astype(jnp.int32)


def coded(values):
    top = jnp.max(jnp.abs(values), axis=0, keepdims=True)
    scale = jnp.floor(top * (1.0 / UNIT)).astype(jnp.int32) + 1
    steps = jnp.floor(values * (32767.0 / (scale.astype(jnp.float32) * UNIT)) + 0.5)
    return steps.astype(jnp.int32), scale


def decoded(steps, scale):
    return steps.astype(jnp.float32) * (scale.astype(jnp.float32) * (UNIT / 32767.0))


def column_of(row, first, count):
    spot = lax.broadcasted_iota(jnp.int32, (count, row.shape[1]), 1) == (
        lax.broadcasted_iota(jnp.int32, (count, row.shape[1]), 0) + first
    )
    return jnp.sum(jnp.where(spot, row, 0.0), axis=1, keepdims=True)


def group_index():
    return lax.axis_index("row") * lax.axis_size("col") + lax.axis_index("col")


def row_sums(values):
    ones = jnp.ones((8, values.shape[0]), jnp.bfloat16)
    return jnp.dot(ones, values, preferred_element_type=jnp.float32)[0:1, :]


def sums_of(values):
    ones = jnp.ones((values.shape[0], 128), jnp.bfloat16)
    return lax.dot_general(values, ones, (((0,), (0,)), ((), ())), preferred_element_type=jnp.float32)[:, 0:1]


def cut_kernel(soft_ref, head_ref, tail_ref, sems):
    width = soft_ref.shape[1]
    reach = head_ref.shape[1]
    copies = [
        pltpu.make_async_copy(soft_ref.at[:, pl.ds(width - reach, reach)], tail_ref, sems.at[0]),
        pltpu.make_async_copy(soft_ref.at[:, pl.ds(0, reach)], head_ref, sems.at[1]),
    ]
    for copy in copies:
        copy.start()
    for copy in copies:
        copy.wait()


def cut_call(soft, reach):
    shape = jax.ShapeDtypeStruct((soft.shape[0], reach), soft.dtype)
    return pl.pallas_call(
        cut_kernel,
        out_shape=[shape, shape],
        in_specs=[ANY],
        out_specs=[VMEM, VMEM],
        scratch_shapes=[pltpu.SemaphoreType.DMA((2,))],
        compiler_params=PARAMS,
        cost_estimate=pl.CostEstimate(flops=0, bytes_accessed=3_000_000, transcendentals=0),
    )(soft)


def ready_kernel(
    width, slots, own_ref, inc_ref, keyt_ref, probt_ref, _,
    fit_ref, vals_ref, hot_ref, self_ref, small_ref,
):
    blocks = own_ref.shape[1] // width
    edges = inc_ref.shape[2]
    pieces = edges // width
    for b in range(blocks):
        own = own_ref[:, b * width : (b + 1) * width]
        tile = lax.dot_general(own, own, (((0,), (0,)), ((), ())), preferred_element_type=jnp.float32)
        self_ref[b] = tile - sums_of(own) * row_sums(own) * (1.0 / own.shape[0])
        rows_x = inc_ref[0, b : b + 1, :]
        slot_x = inc_ref[1, b : b + 1, :]
        cols_x = inc_ref[2, b : b + 1, :]
        lines = lax.broadcasted_iota(jnp.int32, (width, edges), 0)
        row_hot = (lines == rows_x).astype(jnp.bfloat16)
        for k in range(slots):
            hot_ref[b, k * width : (k + 1) * width, :] = (
                lines == jnp.where(slot_x == k, cols_x, -1)
            ).astype(jnp.bfloat16)
        vals = jnp.dot(own, row_hot, preferred_element_type=jnp.float32)
        vals_ref[b] = vals.astype(jnp.bfloat16)
        total = jnp.sum(vals, axis=0, keepdims=True)
        for p in range(pieces):
            n = b * pieces + p
            small_ref[n : n + 1, :] = total[:, p * width : (p + 1) * width]
        key = slot_x * (width * width) + rows_x * width + cols_x
        same = keyt_ref[:, b : b + 1] == key
        fit_ref[b : b + 1, :] = jnp.sum(jnp.where(same, probt_ref[:, b : b + 1], 0.0), axis=0, keepdims=True)


def ready_call(soft, incidence, keys_t, prob_t, after, width, slots):
    shots, own_width = soft.shape
    blocks = own_width // width
    edges = incidence.shape[2]
    return pl.pallas_call(
        functools.partial(ready_kernel, width, slots),
        out_shape=[
            jax.ShapeDtypeStruct((blocks, edges), jnp.float32),
            jax.ShapeDtypeStruct((blocks, shots, edges), jnp.bfloat16),
            jax.ShapeDtypeStruct((blocks, slots * width, edges), jnp.bfloat16),
            jax.ShapeDtypeStruct((blocks, width, width), jnp.float32),
            jax.ShapeDtypeStruct((blocks * edges // width, width), jnp.float32),
        ],
        in_specs=[VMEM] * 4 + [ANY],
        out_specs=[VMEM] * 5,
        compiler_params=PARAMS,
        cost_estimate=pl.CostEstimate(flops=20_000_000_000, bytes_accessed=12_000_000, transcendentals=0),
    )(soft, incidence, keys_t, prob_t, after)


def pair_kernel(
    upper, width, groups, partners_ref, halo_ref, own_ref, vals_ref, hot_ref, self_ref, early_ref, _,
    cov_ref, edge_ref, sums_ref, win,
):
    blocks, slots = partners_ref.shape
    mine = blocks // 2
    low = mine * upper
    reach = HALO * width
    own_width = own_ref.shape[1]
    shots = own_ref.shape[0]
    share = width // groups
    pieces = hot_ref.shape[2] // width
    me = lax.axis_index("shot")
    base = group_index() * blocks
    if upper:
        win[:, 0:own_width] = own_ref[...]
        win[:, own_width:] = halo_ref[...]
        window_first = base + low - HALO
    else:
        win[:, 0:reach] = halo_ref[...]
        win[:, reach:] = own_ref[...]
        window_first = base - HALO
    products, others = [], []
    for b in range(mine):
        block = low + b
        own = win[:, reach + b * width : reach + (b + 1) * width]
        chosen = [own]
        for k in range(1, slots):
            partner = partners_ref[block, k]
            partner = jnp.where(partner >= 0, partner, base + block)
            start = pl.multiple_of((partner - window_first) * width, width)
            chosen.append(win[:, pl.ds(start, width)])
        chosen = jnp.concatenate(chosen, axis=1)
        tiles = lax.dot_general(
            own, chosen[:, width:], (((0,), (0,)), ((), ())), preferred_element_type=jnp.float32
        )
        tiles = tiles - sums_of(own) * (row_sums(chosen[:, width:]) * (1.0 / shots))
        for d in range(groups):
            rows = slice(d * share, (d + 1) * share)
            at = lax.rem(d - me + groups, groups)
            cov_ref[at, b * slots] = self_ref[block, rows, :]
            for k in range(1, slots):
                cov_ref[at, b * slots + k] = tiles[rows, (k - 1) * width : k * width]
        other = jnp.dot(chosen, hot_ref[block], preferred_element_type=jnp.float32)
        product = jnp.sum(vals_ref[block].astype(jnp.float32) * other, axis=0, keepdims=True)
        other = jnp.sum(other, axis=0, keepdims=True)
        products += [product[:, p * width : (p + 1) * width] for p in range(pieces)]
        others += [other[:, p * width : (p + 1) * width] for p in range(pieces)]
    low_col = reach if upper else 0
    columns = row_sums(win[:, low_col : low_col + 4 * width])
    sums_ref[...] = fixed(jnp.concatenate([columns[:, p * width : (p + 1) * width] for p in range(4)], axis=0))
    early = early_ref[upper * mine * pieces : (upper + 1) * mine * pieces, :]
    edge_ref[...] = fixed(jnp.concatenate(products + [early] + others, axis=0))


def pair_call(upper, partners, halo, soft, vals, hot, selfs, early, after, width, groups):
    blocks, slots = partners.shape
    mine = blocks // 2
    return pl.pallas_call(
        functools.partial(pair_kernel, upper, width, groups),
        out_shape=[
            jax.ShapeDtypeStruct((groups, mine * slots, width // groups, width), jnp.float32),
            jax.ShapeDtypeStruct((3 * mine * hot.shape[2] // width, width), jnp.int32),
            jax.ShapeDtypeStruct((mine + HALO, width), jnp.int32),
        ],
        in_specs=[SMEM] + [VMEM] * 6 + [ANY],
        out_specs=[VMEM] * 3,
        scratch_shapes=[pltpu.VMEM((soft.shape[0], soft.shape[1] + halo.shape[1]), jnp.bfloat16)],
        compiler_params=PARAMS,
        cost_estimate=pl.CostEstimate(flops=3_000_000_000, bytes_accessed=4_000_000, transcendentals=0),
    )(partners, halo, soft, vals, hot, selfs, early, after)


def partner_row(partners_ref, block, k, base):
    partner = partners_ref[block, k]
    return jnp.where(partner >= 0, partner - base, block) + HALO


def words_of(came_ref, word, share):
    words = came_ref[word * share : (word + 1) * share, :]
    at = came_ref.shape[0] - TAIL + word
    scales = came_ref[at : at + 1, :]
    low = decoded(lax.shift_right_arithmetic(words << 16, 16), scales & 65535)
    high = decoded(lax.shift_right_arithmetic(words, 16), lax.shift_right_logical(scales, 16))
    return low, high


def hop_kernel(at, seen, partners_ref, *refs):
    came_ref = refs[0] if seen else None
    cov_l, cov_u, edge_l, edge_u, sums_l, sums_u, _, out_ref, own_means, shift = refs[-10:]
    blocks, slots = partners_ref.shape
    share, width = cov_l.shape[2:]
    mine = blocks // 2
    groups = cov_l.shape[0]
    base = group_index() * blocks
    words = blocks * slots // 2
    body = words * share
    quarter = edge_l.shape[0] // 3
    shots = SHOTS
    sums = jnp.concatenate([sums_l[...], sums_u[...]], axis=0)
    edges = jnp.concatenate(
        [part[n * quarter : (n + 1) * quarter, :] for n in range(3) for part in (edge_l, edge_u)], axis=0
    )
    if seen:
        old = came_ref[body + words : body + words + 8, :]
        shift[...] = old.astype(jnp.float32) * (1.0 / (SCALE * shots * seen)) - sums.astype(jnp.float32) * (
            1.0 / (SCALE * shots)
        )
        sums = sums + old
        edges = edges + came_ref[body + words + 8 :, :]
        weight = float(shots) * seen / (seen + 1)
    dest = lax.rem(lax.axis_index("shot") + at, groups)
    for block in range(blocks):
        cov_ref, b = (cov_l, block) if block < mine else (cov_u, block - mine)
        if seen:
            column = column_of(shift[block + HALO : block + HALO + 1, :], dest * share, share) * weight
        for pair in range(slots // 2):
            word = block * (slots // 2) + pair
            values = [cov_ref[at, b * slots + 2 * pair + i] for i in range(2)]
            if seen:
                came = words_of(came_ref, word, share)
                for i in range(2):
                    row = shift[pl.ds(partner_row(partners_ref, block, 2 * pair + i, base), 1), :]
                    values[i] = values[i] + came[i] + column * row
            (low, low_scale), (high, high_scale) = coded(values[0]), coded(values[1])
            out_ref[word * share : (word + 1) * share, :] = (high << 16) | (low & 65535)
            out_ref[body + word : body + word + 1, :] = (high_scale << 16) | low_scale
    out_ref[body + words : body + words + 8, :] = sums
    out_ref[body + words + 8 :, :] = edges


def hop_call(at, seen, partners, came, parts, after):
    (cov_l, edge_l, sums_l), (cov_u, edge_u, sums_u) = parts
    share, width = cov_l.shape[2:]
    body = 2 * cov_l.shape[1] * share // 2
    came = (came,) if seen else ()
    return pl.pallas_call(
        functools.partial(hop_kernel, at, seen),
        out_shape=jax.ShapeDtypeStruct((body + TAIL, width), jnp.int32),
        in_specs=[SMEM] + [VMEM] * (6 + len(came)) + [ANY],
        out_specs=VMEM,
        scratch_shapes=[pltpu.VMEM((8, width), jnp.float32), pltpu.VMEM((8, width), jnp.float32)],
        compiler_params=PARAMS,
        cost_estimate=pl.CostEstimate(flops=1_000_000, bytes_accessed=600_000, transcendentals=0),
    )(partners, *came, cov_l, cov_u, edge_l, edge_u, sums_l, sums_u, after)


def final_kernel(
    rises, falls, partners_ref, inc_ref, rising_ref, falling_ref,
    cov_l, cov_u, edge_l, edge_u, sums_l, sums_u, fit_ref,
    pair_ref, grad_ref, first_shift, second_shift, totals,
):
    blocks, slots = partners_ref.shape
    mine = blocks // 2
    groups = cov_l.shape[0]
    share, width = cov_l.shape[2:]
    pieces = inc_ref.shape[2] // width
    quarter = edge_l.shape[0] // 3
    words = blocks * slots // 2
    body = words * share
    shots = SHOTS
    count = float(shots * groups)
    base = group_index() * blocks
    start = lax.axis_index("shot") * share
    sums = jnp.concatenate([sums_l[...], sums_u[...]], axis=0)
    rise_sums = rising_ref[body + words : body + words + 8, :]
    fall_sums = falling_ref[body + words : body + words + 8, :]

    def mean(values, sources):
        return values.astype(jnp.float32) * (1.0 / (SCALE * shots * sources))

    first_shift[...] = mean(rise_sums, rises) - mean(sums, 1)
    second_shift[...] = mean(fall_sums, falls) - mean(sums + rise_sums, rises + 1)
    totals[...] = (sums + rise_sums + fall_sums).astype(jnp.float32) * (1.0 / SCALE)
    first_weight = float(shots) * rises / (rises + 1)
    second_weight = float(shots) * falls * (rises + 1) / (rises + 1 + falls)
    edges = jnp.concatenate(
        [part[n * quarter : (n + 1) * quarter, :] for n in range(3) for part in (edge_l, edge_u)], axis=0
    )
    edges = edges + rising_ref[body + words + 8 :, :] + falling_ref[body + words + 8 :, :]
    edges = edges.astype(jnp.float32) * (1.0 / SCALE)
    for block in range(blocks):
        cov_ref, b = (cov_l, block) if block < mine else (cov_u, block - mine)
        own = slice(block + HALO, block + HALO + 1)
        first_column = column_of(first_shift[own, :], start, share) * first_weight
        second_column = column_of(second_shift[own, :], start, share) * second_weight
        total_column = column_of(totals[own, :], start, share) * (1.0 / count)
        for pair in range(slots // 2):
            word = block * (slots // 2) + pair
            risen, fallen = words_of(rising_ref, word, share), words_of(falling_ref, word, share)
            for i in range(2):
                k = 2 * pair + i
                at = pl.ds(partner_row(partners_ref, block, k, base), 1)
                live = jnp.where(partners_ref[block, k] >= 0, 1.0, 0.0)
                cov = cov_ref[0, b * slots + k] + risen[i] + first_column * first_shift[at, :]
                cov = cov + fallen[i] + second_column * second_shift[at, :]
                alone = total_column * totals[at, :]
                entry = 0.5 - 0.5 * jnp.sqrt(alone / (alone + cov))
                pair_ref[block, k] = (entry * live).astype(jnp.bfloat16)
        for p in range(pieces):
            n = block * pieces + p
            at = slice(p * width, (p + 1) * width)
            slot_x = inc_ref[1, block : block + 1, at]
            live = jnp.zeros((1, width), jnp.float32)
            for k in range(slots):
                live = live + jnp.where((slot_x == k) & (partners_ref[block, k] >= 0), 1.0, 0.0)
            rows = 2 * quarter
            quotient = (edges[rows + n : rows + n + 1] / count) * (
                edges[2 * rows + n : 2 * rows + n + 1] / count
            ) * count / edges[n : n + 1]
            entry = (0.5 - 0.5 * jnp.sqrt(quotient)) * live
            residual = live * (entry - fit_ref[block : block + 1, at]) / NOISE_SPREAD
            grad_ref[block : block + 1, at] = -residual / NOISE_SPREAD


def final_call(partners, incidence, rising, falling, parts, fit):
    (cov_l, edge_l, sums_l), (cov_u, edge_u, sums_u) = parts
    blocks, slots = partners.shape
    groups, _, share, width = cov_l.shape
    half = groups // 2
    return pl.pallas_call(
        functools.partial(final_kernel, half, groups - 1 - half),
        out_shape=[
            jax.ShapeDtypeStruct((blocks, slots, share, width), jnp.bfloat16),
            jax.ShapeDtypeStruct((blocks, incidence.shape[2]), jnp.float32),
        ],
        in_specs=[SMEM] + [VMEM] * 10,
        out_specs=[VMEM] * 2,
        scratch_shapes=[pltpu.VMEM((8, width), jnp.float32)] * 3,
        compiler_params=PARAMS,
        cost_estimate=pl.CostEstimate(flops=1_000_000, bytes_accessed=2_000_000, transcendentals=100_000),
    )(partners, incidence, rising, falling, cov_l, cov_u, edge_l, edge_u, sums_l, sums_u, fit)


def local(soft, partners, incidence, edge_prob):
    shots, own_width = soft.shape
    blocks, slots = partners.shape
    width = own_width // blocks
    groups = lax.axis_size("shot")
    sides = lax.axis_size(("row", "col"))

    head, tail = cut_call(soft, HALO * width)
    left = lax.ppermute(tail, ("row", "col"), [(i, (i + 1) % sides) for i in range(sides)])
    right = lax.ppermute(head, ("row", "col"), [((i + 1) % sides, i) for i in range(sides)])

    keys = incidence[1] * (width * width) + incidence[0] * width + incidence[2]
    fit, vals, hot, selfs, early = ready_call(soft, incidence, keys.T, edge_prob.T, tail, width, slots)
    args = (soft, vals, hot, selfs, early)
    lower = pair_call(0, partners, left, *args, early, width, groups)
    upper = pair_call(1, partners, right, *args, lower[1], width, groups)
    parts = (lower, upper)

    half = groups // 2
    rise = [(i, (i + 1) % groups) for i in range(groups)]
    fall = [(b, a) for a, b in rise]
    rising = falling = None
    order = early
    for step in range(half):
        order = hop_call(half - step, step, partners, rising, parts, order)
        rising = lax.ppermute(order, "shot", rise)
        if step < half - 1:
            order = hop_call(half + 1 + step, step, partners, falling, parts, order)
            falling = lax.ppermute(order, "shot", fall)
    return final_call(partners, incidence, rising, falling, parts, fit)


def solution(mesh):
    placed = (
        P("shot", ("row", "col")),
        P(("row", "col"), None),
        P(None, ("row", "col"), None),
        P(("row", "col"), None),
    )
    return jax.shard_map(
        local,
        mesh=mesh,
        in_specs=placed,
        out_specs=(P(("row", "col"), None, "shot", None), P(("row", "col"), None)),
        check_vma=False,
    )
```

```python
import functools

import jax
import jax.numpy as jnp
from jax import lax
from jax.experimental import pallas as pl
from jax.experimental.pallas import tpu as pltpu
from jax.sharding import PartitionSpec as P

HALO = 2
NOISE_SPREAD = 0.05
SCALE = 131072.0
UNIT = 1600.0 / 65535.0
SHOTS = 768
TAIL = 40
ANY = pl.BlockSpec(memory_space=pl.ANY)
VMEM = pl.BlockSpec(memory_space=pltpu.VMEM)
SMEM = pl.BlockSpec(memory_space=pltpu.SMEM)
HBM = pl.BlockSpec(memory_space=pltpu.HBM)
PARAMS = pltpu.CompilerParams(vmem_limit_bytes=20 * 1024 * 1024)


def fixed(values):
    return jnp.floor(values * SCALE + 0.5).astype(jnp.int32)


def column_of(row, first, count):
    spot = lax.broadcasted_iota(jnp.int32, (count, row.shape[1]), 1) == (
        lax.broadcasted_iota(jnp.int32, (count, row.shape[1]), 0) + first
    )
    return jnp.sum(jnp.where(spot, row, 0.0), axis=1, keepdims=True)


def group_index():
    return lax.axis_index("row") * lax.axis_size("col") + lax.axis_index("col")


def row_sums(values):
    ones = jnp.ones((8, values.shape[0]), jnp.bfloat16)
    return jnp.dot(ones, values, preferred_element_type=jnp.float32)[0:1, :]


def sums_of(values):
    ones = jnp.ones((values.shape[0], 128), jnp.bfloat16)
    return lax.dot_general(values, ones, (((0,), (0,)), ((), ())), preferred_element_type=jnp.float32)[:, 0:1]


def cut_kernel(soft_ref, head_ref, tail_ref, done_ref, sems):
    width = soft_ref.shape[1]
    reach = head_ref.shape[1]
    copies = [
        pltpu.make_async_copy(soft_ref.at[:, pl.ds(width - reach, reach)], tail_ref, sems.at[0]),
        pltpu.make_async_copy(soft_ref.at[:, pl.ds(0, reach)], head_ref, sems.at[1]),
    ]
    for copy in copies:
        copy.start()
    done_ref[...] = jnp.zeros_like(done_ref)
    for copy in copies:
        copy.wait()


def cut_call(soft, reach):
    shape = jax.ShapeDtypeStruct((soft.shape[0], reach), soft.dtype)
    return pl.pallas_call(
        cut_kernel,
        out_shape=[shape, shape, jax.ShapeDtypeStruct((8, 128), jnp.float32)],
        in_specs=[HBM],
        out_specs=[VMEM, VMEM, VMEM],
        scratch_shapes=[pltpu.SemaphoreType.DMA((2,))],
        compiler_params=pltpu.CompilerParams(vmem_limit_bytes=58 * 1024 * 1024),
        cost_estimate=pl.CostEstimate(flops=0, bytes_accessed=3_000_000, transcendentals=0),
    )(soft)


def spread(cov_ref, slot, tile, me):
    groups, _, share, _ = cov_ref.shape
    for d in range(groups):
        at = lax.rem(d - me + groups, groups)
        cov_ref[at, slot] = tile[d * share : (d + 1) * share, :]


def rows_of(row, pieces):
    width = row.shape[1] // pieces
    return [row[:, p * width : (p + 1) * width] for p in range(pieces)]


def ready_kernel(
    width, partners_ref, own_ref, inc_ref, keyt_ref, probt_ref, _,
    fit_ref, vals_ref, hot_ref, lower_ref, upper_ref, early_ref, sums_ref,
):
    blocks, slots = partners_ref.shape
    mine = blocks // 2
    shots = own_ref.shape[0]
    edges = inc_ref.shape[2]
    pieces = edges // width
    me = lax.axis_index("shot")
    base = group_index() * blocks
    lines = lax.broadcasted_iota(jnp.int32, (width, edges), 0)
    products, firsts, others = [], [], []
    for b in range(blocks):
        own = own_ref[:, b * width : (b + 1) * width]
        rows_x = inc_ref[0, b : b + 1, :]
        slot_x = inc_ref[1, b : b + 1, :]
        cols_x = inc_ref[2, b : b + 1, :]
        halo_first = base - HALO if b < mine else base + blocks
        chosen, hot = [], []
        far = [jnp.full((1, edges), -1, jnp.int32) for _ in range(HALO)]
        for k in range(slots):
            partner = partners_ref[b, k]
            partner = jnp.where(partner >= 0, partner, base + b)
            inside = (partner >= base) & (partner < base + blocks)
            start = pl.multiple_of(jnp.where(inside, partner - base, b) * width, width)
            chosen.append(own_ref[:, pl.ds(start, width)])
            here = slot_x == k
            hot.append((lines == jnp.where(here & inside, cols_x, -1)).astype(jnp.bfloat16))
            for w in range(HALO):
                there = here & (partner == halo_first + w) & jnp.logical_not(inside)
                far[w] = jnp.where(there, cols_x, far[w])
        for w in range(HALO):
            hot_ref[b, w * width : (w + 1) * width, :] = (lines == far[w]).astype(jnp.bfloat16)
        chosen = jnp.concatenate(chosen, axis=1)
        tiles = lax.dot_general(own, chosen, (((0,), (0,)), ((), ())), preferred_element_type=jnp.float32)
        tiles = tiles - sums_of(own) * (row_sums(chosen) * (1.0 / shots))
        for k in range(slots):
            spread(
                lower_ref if b < mine else upper_ref, (b % mine) * slots + k,
                tiles[:, k * width : (k + 1) * width], me,
            )
        vals = jnp.dot(own, (lines == rows_x).astype(jnp.bfloat16), preferred_element_type=jnp.float32)
        vals_ref[b] = vals.astype(jnp.bfloat16)
        other = jnp.dot(chosen, jnp.concatenate(hot, axis=0), preferred_element_type=jnp.float32)
        products += rows_of(jnp.sum(vals * other, axis=0, keepdims=True), pieces)
        firsts += rows_of(jnp.sum(vals, axis=0, keepdims=True), pieces)
        others += rows_of(jnp.sum(other, axis=0, keepdims=True), pieces)
        key = slot_x * (width * width) + rows_x * width + cols_x
        same = keyt_ref[:, b : b + 1] == key
        fit_ref[b : b + 1, :] = jnp.sum(jnp.where(same, probt_ref[:, b : b + 1], 0.0), axis=0, keepdims=True)
    early_ref[...] = jnp.concatenate(products + firsts + others, axis=0)
    sums_ref[...] = jnp.concatenate(rows_of(row_sums(own_ref[...]), blocks), axis=0)


def ready_call(partners, soft, incidence, keys_t, prob_t, after, width, groups):
    shots = soft.shape[0]
    blocks, slots = partners.shape
    edges = incidence.shape[2]
    cov = jax.ShapeDtypeStruct((groups, blocks // 2 * slots, width // groups, width), jnp.float32)
    return pl.pallas_call(
        functools.partial(ready_kernel, width),
        out_shape=[
            jax.ShapeDtypeStruct((blocks, edges), jnp.float32),
            jax.ShapeDtypeStruct((blocks, shots, edges), jnp.bfloat16),
            jax.ShapeDtypeStruct((blocks, HALO * width, edges), jnp.bfloat16),
            cov,
            cov,
            jax.ShapeDtypeStruct((3 * blocks * edges // width, width), jnp.float32),
            jax.ShapeDtypeStruct((blocks, width), jnp.float32),
        ],
        in_specs=[SMEM] + [VMEM] * 4 + [ANY],
        out_specs=[VMEM] * 7,
        compiler_params=PARAMS,
        cost_estimate=pl.CostEstimate(flops=20_000_000_000, bytes_accessed=12_000_000, transcendentals=0),
    )(partners, soft, incidence, keys_t, prob_t, after)


def pair_kernel(
    upper, partners_ref, halo_ref, own_ref, vals_ref, hot_ref, early_ref, own_sums_ref, _, _after,
    cov_ref, edge_ref, sums_ref,
):
    blocks, slots = partners_ref.shape
    mine = blocks // 2
    low = mine * upper
    shots = own_ref.shape[0]
    width = cov_ref.shape[3]
    pieces = hot_ref.shape[2] // width
    me = lax.axis_index("shot")
    base = group_index() * blocks
    halo_first = base + blocks if upper else base - HALO
    halo = halo_ref[...]
    halo_sums = row_sums(halo)
    products, others = [], []
    for b in range(mine):
        block = low + b
        own = own_ref[:, block * width : (block + 1) * width]
        reached = [w for w in range(HALO) if abs(block - (blocks + w if upper else w - HALO)) <= HALO]
        first, last = reached[0] * width, (reached[-1] + 1) * width
        tiles = lax.dot_general(
            own, halo[:, first:last], (((0,), (0,)), ((), ())), preferred_element_type=jnp.float32
        )
        tiles = tiles - sums_of(own) * (halo_sums[:, first:last] * (1.0 / shots))
        for n, w in enumerate(reached):
            for k in range(1, slots):
                partner = partners_ref[block, k]

                @pl.when((partner >= 0) & (partner == halo_first + w))
                def _():
                    spread(cov_ref, b * slots + k, tiles[:, n * width : (n + 1) * width], me)

        other = jnp.dot(halo, hot_ref[block], preferred_element_type=jnp.float32)
        product = jnp.sum(vals_ref[block].astype(jnp.float32) * other, axis=0, keepdims=True)
        products += rows_of(product, pieces)
        others += rows_of(jnp.sum(other, axis=0, keepdims=True), pieces)
    count = mine * pieces
    early = [early_ref[n * 2 * count + upper * count : n * 2 * count + (upper + 1) * count, :] for n in range(3)]
    own_sums = [own_sums_ref[low : low + mine, :]]
    side = rows_of(halo_sums, HALO)
    sums_ref[...] = fixed(jnp.concatenate(own_sums + side if upper else side + own_sums, axis=0))
    edge_ref[...] = fixed(
        jnp.concatenate(
            [early[0] + jnp.concatenate(products, axis=0), early[1], early[2] + jnp.concatenate(others, axis=0)],
            axis=0,
        )
    )


def pair_call(upper, partners, halo, soft, vals, hot, early, own_sums, cov, after):
    blocks = partners.shape[0]
    mine = blocks // 2
    width = cov.shape[3]
    return pl.pallas_call(
        functools.partial(pair_kernel, upper),
        out_shape=[
            jax.ShapeDtypeStruct(cov.shape, jnp.float32),
            jax.ShapeDtypeStruct((3 * mine * hot.shape[2] // width, width), jnp.int32),
            jax.ShapeDtypeStruct((mine + HALO, width), jnp.int32),
        ],
        in_specs=[SMEM] + [VMEM] * 7 + [ANY],
        out_specs=[VMEM] * 3,
        input_output_aliases={7: 0},
        compiler_params=PARAMS,
        cost_estimate=pl.CostEstimate(flops=1_000_000_000, bytes_accessed=4_000_000, transcendentals=0),
    )(partners, halo, soft, vals, hot, early, own_sums, cov, after)


def partner_row(partners_ref, block, k, base):
    partner = partners_ref[block, k]
    return jnp.where(partner >= 0, partner - base, block) + HALO


def factors_of(came_ref, words):
    scales = came_ref[came_ref.shape[0] - TAIL : came_ref.shape[0] - TAIL + words, :]
    step = UNIT / 32767.0
    low = (scales & 65535).astype(jnp.float32) * step
    return low, lax.shift_right_logical(scales, 16).astype(jnp.float32) * step


def words_of(came_ref, word, share, factors):
    words = came_ref[word * share : (word + 1) * share, :]
    low = lax.shift_right_arithmetic(words << 16, 16).astype(jnp.float32)
    high = lax.shift_right_arithmetic(words, 16).astype(jnp.float32)
    return low * factors[0][word : word + 1, :], high * factors[1][word : word + 1, :]


def hop_kernel(at, seen, partners_ref, *refs):
    came_ref = refs[0] if seen else None
    cov_l, cov_u, edge_l, edge_u, sums_l, sums_u, _, out_ref, shift, exact = refs[-10:]
    blocks, slots = partners_ref.shape
    share, width = cov_l.shape[2:]
    mine = blocks // 2
    groups = cov_l.shape[0]
    base = group_index() * blocks
    words = blocks * slots // 2
    body = words * share
    quarter = edge_l.shape[0] // 3
    shots = SHOTS
    sums = jnp.concatenate([sums_l[...], sums_u[...]], axis=0)
    edges = jnp.concatenate(
        [part[n * quarter : (n + 1) * quarter, :] for n in range(3) for part in (edge_l, edge_u)], axis=0
    )
    if seen:
        old = came_ref[body + words : body + words + 8, :]
        shift[...] = old.astype(jnp.float32) * (1.0 / (SCALE * shots * seen)) - sums.astype(jnp.float32) * (
            1.0 / (SCALE * shots)
        )
        sums = sums + old
        edges = edges + came_ref[body + words + 8 :, :]
        weight = float(shots) * seen / (seen + 1)
        factors = factors_of(came_ref, words)
    out_ref[body + words : body + words + 8, :] = sums
    out_ref[body + words + 8 :, :] = edges
    dest = lax.rem(lax.axis_index("shot") + at, groups)
    tops = [[], []]
    for block in range(blocks):
        cov_ref, b = (cov_l, block) if block < mine else (cov_u, block - mine)
        if seen:
            column = column_of(shift[block + HALO : block + HALO + 1, :], dest * share, share) * weight
        for pair in range(slots // 2):
            word = block * (slots // 2) + pair
            if seen:
                came = words_of(came_ref, word, share, factors)
            for i in range(2):
                value = cov_ref[at, b * slots + 2 * pair + i]
                if seen:
                    row = shift[pl.ds(partner_row(partners_ref, block, 2 * pair + i, base), 1), :]
                    value = value + came[i] + column * row
                exact[i, word] = value
                tops[i].append(jnp.max(jnp.abs(value), axis=0, keepdims=True))
    scales, steps = [], []
    for i in range(2):
        scale = jnp.floor(jnp.concatenate(tops[i], axis=0) * (1.0 / UNIT)).astype(jnp.int32) + 1
        scales.append(scale)
        steps.append(32767.0 / (scale.astype(jnp.float32) * UNIT))
    out_ref[body : body + words, :] = (scales[1] << 16) | scales[0]
    for word in range(words):
        low, high = [
            jnp.floor(exact[i, word] * steps[i][word : word + 1, :] + 0.5).astype(jnp.int32) for i in range(2)
        ]
        out_ref[word * share : (word + 1) * share, :] = (high << 16) | (low & 65535)


def hop_call(at, seen, partners, came, parts, after):
    (cov_l, edge_l, sums_l), (cov_u, edge_u, sums_u) = parts
    share, width = cov_l.shape[2:]
    body = 2 * cov_l.shape[1] * share // 2
    came = (came,) if seen else ()
    return pl.pallas_call(
        functools.partial(hop_kernel, at, seen),
        out_shape=jax.ShapeDtypeStruct((body + TAIL, width), jnp.int32),
        in_specs=[SMEM] + [VMEM] * (6 + len(came)) + [ANY],
        out_specs=VMEM,
        scratch_shapes=[
            pltpu.VMEM((8, width), jnp.float32),
            pltpu.VMEM((2, body // share, share, width), jnp.float32),
        ],
        compiler_params=PARAMS,
        cost_estimate=pl.CostEstimate(flops=1_000_000, bytes_accessed=600_000, transcendentals=0),
    )(partners, *came, cov_l, cov_u, edge_l, edge_u, sums_l, sums_u, after)


def final_kernel(
    rises, falls, partners_ref, inc_ref, rising_ref, falling_ref,
    cov_l, cov_u, edge_l, edge_u, sums_l, sums_u, fit_ref,
    pair_ref, grad_ref, first_shift, second_shift, totals,
):
    blocks, slots = partners_ref.shape
    mine = blocks // 2
    groups = cov_l.shape[0]
    share, width = cov_l.shape[2:]
    pieces = inc_ref.shape[2] // width
    quarter = edge_l.shape[0] // 3
    words = blocks * slots // 2
    body = words * share
    shots = SHOTS
    count = float(shots * groups)
    base = group_index() * blocks
    start = lax.axis_index("shot") * share
    sums = jnp.concatenate([sums_l[...], sums_u[...]], axis=0)
    rise_sums = rising_ref[body + words : body + words + 8, :]
    fall_sums = falling_ref[body + words : body + words + 8, :]

    def mean(values, sources):
        return values.astype(jnp.float32) * (1.0 / (SCALE * shots * sources))

    first_shift[...] = mean(rise_sums, rises) - mean(sums, 1)
    second_shift[...] = mean(fall_sums, falls) - mean(sums + rise_sums, rises + 1)
    totals[...] = (sums + rise_sums + fall_sums).astype(jnp.float32) * (1.0 / SCALE)
    first_weight = float(shots) * rises / (rises + 1)
    second_weight = float(shots) * falls * (rises + 1) / (rises + 1 + falls)
    edges = jnp.concatenate(
        [part[n * quarter : (n + 1) * quarter, :] for n in range(3) for part in (edge_l, edge_u)], axis=0
    )
    edges = edges + rising_ref[body + words + 8 :, :] + falling_ref[body + words + 8 :, :]
    edges = edges.astype(jnp.float32) * (1.0 / SCALE)
    risen_factors, fallen_factors = factors_of(rising_ref, words), factors_of(falling_ref, words)
    for block in range(blocks):
        cov_ref, b = (cov_l, block) if block < mine else (cov_u, block - mine)
        own = slice(block + HALO, block + HALO + 1)
        first_column = column_of(first_shift[own, :], start, share) * first_weight
        second_column = column_of(second_shift[own, :], start, share) * second_weight
        total_column = column_of(totals[own, :], start, share) * (1.0 / count)
        for pair in range(slots // 2):
            word = block * (slots // 2) + pair
            risen = words_of(rising_ref, word, share, risen_factors)
            fallen = words_of(falling_ref, word, share, fallen_factors)
            for i in range(2):
                k = 2 * pair + i
                at = pl.ds(partner_row(partners_ref, block, k, base), 1)
                live = jnp.where(partners_ref[block, k] >= 0, 1.0, 0.0)
                cov = cov_ref[0, b * slots + k] + risen[i] + first_column * first_shift[at, :]
                cov = cov + fallen[i] + second_column * second_shift[at, :]
                alone = total_column * totals[at, :]
                entry = 0.5 - 0.5 * jnp.sqrt(alone / (alone + cov))
                pair_ref[block, k] = (entry * live).astype(jnp.bfloat16)
        for p in range(pieces):
            n = block * pieces + p
            at = slice(p * width, (p + 1) * width)
            slot_x = inc_ref[1, block : block + 1, at]
            live = jnp.zeros((1, width), jnp.float32)
            for k in range(slots):
                live = live + jnp.where((slot_x == k) & (partners_ref[block, k] >= 0), 1.0, 0.0)
            rows = 2 * quarter
            quotient = (edges[rows + n : rows + n + 1] / count) * (
                edges[2 * rows + n : 2 * rows + n + 1] / count
            ) * count / edges[n : n + 1]
            entry = (0.5 - 0.5 * jnp.sqrt(quotient)) * live
            residual = live * (entry - fit_ref[block : block + 1, at]) / NOISE_SPREAD
            grad_ref[block : block + 1, at] = -residual / NOISE_SPREAD


def final_call(partners, incidence, rising, falling, parts, fit):
    (cov_l, edge_l, sums_l), (cov_u, edge_u, sums_u) = parts
    blocks, slots = partners.shape
    groups, _, share, width = cov_l.shape
    half = groups // 2
    return pl.pallas_call(
        functools.partial(final_kernel, half, groups - 1 - half),
        out_shape=[
            jax.ShapeDtypeStruct((blocks, slots, share, width), jnp.bfloat16),
            jax.ShapeDtypeStruct((blocks, incidence.shape[2]), jnp.float32),
        ],
        in_specs=[SMEM] + [VMEM] * 10,
        out_specs=[VMEM] * 2,
        scratch_shapes=[pltpu.VMEM((8, width), jnp.float32)] * 3,
        compiler_params=PARAMS,
        cost_estimate=pl.CostEstimate(flops=1_000_000, bytes_accessed=2_000_000, transcendentals=100_000),
    )(partners, incidence, rising, falling, cov_l, cov_u, edge_l, edge_u, sums_l, sums_u, fit)


def local(soft, partners, incidence, edge_prob):
    shots, own_width = soft.shape
    blocks, slots = partners.shape
    width = own_width // blocks
    groups = lax.axis_size("shot")
    sides = lax.axis_size(("row", "col"))

    head, tail, cut = cut_call(soft, HALO * width)
    left = lax.ppermute(tail, ("row", "col"), [(i, (i + 1) % sides) for i in range(sides)])
    right = lax.ppermute(head, ("row", "col"), [((i + 1) % sides, i) for i in range(sides)])

    keys = incidence[1] * (width * width) + incidence[0] * width + incidence[2]
    fit, vals, hot, cov_l, cov_u, early, own_sums = ready_call(
        partners, soft, incidence, keys.T, edge_prob.T, cut, width, groups
    )
    args = (soft, vals, hot, early, own_sums)
    lower = pair_call(0, partners, left, *args, cov_l, early)
    upper = pair_call(1, partners, right, *args, cov_u, lower[1])
    parts = (lower, upper)

    half = groups // 2
    rise = [(i, (i + 1) % groups) for i in range(groups)]
    fall = [(b, a) for a, b in rise]
    rising = falling = None
    order = early
    for step in range(half):
        order = hop_call(half - step, step, partners, rising, parts, order)
        rising = lax.ppermute(order, "shot", rise)
        if step < half - 1:
            order = hop_call(half + 1 + step, step, partners, falling, parts, order)
            falling = lax.ppermute(order, "shot", fall)
    return final_call(partners, incidence, rising, falling, parts, fit)


def solution(mesh):
    placed = (
        P("shot", ("row", "col")),
        P(("row", "col"), None),
        P(None, ("row", "col"), None),
        P(("row", "col"), None),
    )
    return jax.shard_map(
        local,
        mesh=mesh,
        in_specs=placed,
        out_specs=(P(("row", "col"), None, "shot", None), P(("row", "col"), None)),
        check_vma=False,
    )
```

```python
import functools

import jax
import jax.numpy as jnp
from jax import lax
from jax.experimental import pallas as pl
from jax.experimental.pallas import tpu as pltpu
from jax.sharding import PartitionSpec as P

HALO = 2
REACH = 8
NOISE_SPREAD = 0.05
SCALE = 131072.0
UNIT = 1600.0 / 65535.0
SHOTS = 768
TAIL = 40
ANY = pl.BlockSpec(memory_space=pl.ANY)
VMEM = pl.BlockSpec(memory_space=pltpu.VMEM)
SMEM = pl.BlockSpec(memory_space=pltpu.SMEM)
HBM = pl.BlockSpec(memory_space=pltpu.HBM)
PARAMS = pltpu.CompilerParams(vmem_limit_bytes=20 * 1024 * 1024)


def fixed(values):
    return jnp.floor(values * SCALE + 0.5).astype(jnp.int32)


def column_of(row, first, count):
    spot = lax.broadcasted_iota(jnp.int32, (count, row.shape[1]), 1) == (
        lax.broadcasted_iota(jnp.int32, (count, row.shape[1]), 0) + first
    )
    return jnp.sum(jnp.where(spot, row, 0.0), axis=1, keepdims=True)


def group_index():
    return lax.axis_index("row") * lax.axis_size("col") + lax.axis_index("col")


def row_sums(values):
    ones = jnp.ones((8, values.shape[0]), jnp.bfloat16)
    return jnp.dot(ones, values, preferred_element_type=jnp.float32)[0:1, :]


def sums_of(values):
    ones = jnp.ones((values.shape[0], 128), jnp.bfloat16)
    return lax.dot_general(values, ones, (((0,), (0,)), ((), ())), preferred_element_type=jnp.float32)[:, 0:1]


def cut_kernel(soft_ref, head_ref, tail_ref, done_ref, sems):
    width = soft_ref.shape[1]
    reach = head_ref.shape[1]
    copies = [
        pltpu.make_async_copy(soft_ref.at[:, pl.ds(width - reach, reach)], tail_ref, sems.at[0]),
        pltpu.make_async_copy(soft_ref.at[:, pl.ds(0, reach)], head_ref, sems.at[1]),
    ]
    for copy in copies:
        copy.start()
    done_ref[...] = jnp.zeros_like(done_ref)
    for copy in copies:
        copy.wait()


def cut_call(soft, reach):
    shape = jax.ShapeDtypeStruct((soft.shape[0], reach), soft.dtype)
    return pl.pallas_call(
        cut_kernel,
        out_shape=[shape, shape, jax.ShapeDtypeStruct((8, 128), jnp.float32)],
        in_specs=[HBM],
        out_specs=[VMEM, VMEM, VMEM],
        scratch_shapes=[pltpu.SemaphoreType.DMA((2,))],
        compiler_params=pltpu.CompilerParams(vmem_limit_bytes=58 * 1024 * 1024),
        cost_estimate=pl.CostEstimate(flops=0, bytes_accessed=3_000_000, transcendentals=0),
    )(soft)


def spread(cov_ref, slot, tile, me):
    groups, _, share, _ = cov_ref.shape
    for d in range(groups):
        at = lax.rem(d - me + groups, groups)
        cov_ref[at, slot] = tile[d * share : (d + 1) * share, :]


def rows_of(row, pieces):
    width = row.shape[1] // pieces
    return [row[:, p * width : (p + 1) * width] for p in range(pieces)]


def ready_kernel(
    width, partners_ref, own_ref, inc_ref, keyt_ref, probt_ref, _,
    fit_ref, vals_ref, hot_ref, cov_ref, early_ref, sums_ref, pick_ref,
):
    blocks, slots = partners_ref.shape
    mine = blocks // 2
    shots = own_ref.shape[0]
    edges = inc_ref.shape[2]
    pieces = edges // width
    me = lax.axis_index("shot")
    base = group_index() * blocks
    lines = lax.broadcasted_iota(jnp.int32, (width, edges), 0)
    products, firsts, others = [], [], []
    for b in range(blocks):
        own = own_ref[:, b * width : (b + 1) * width]
        rows_x = inc_ref[0, b : b + 1, :]
        slot_x = inc_ref[1, b : b + 1, :]
        cols_x = inc_ref[2, b : b + 1, :]
        halo_first = base - HALO if b < mine else base + blocks
        chosen, hot = [], []
        far = [jnp.full((1, edges), -1, jnp.int32) for _ in range(HALO)]
        for k in range(slots):
            partner = partners_ref[b, k]
            tile = b * slots + k
            pick_ref[REACH, tile : tile + 1, :] = jnp.where(
                jnp.full((1, width), partner, jnp.int32) >= 0, 1.0, 0.0
            )
            partner = jnp.where(partner >= 0, partner, base + b)
            for w in range(REACH):
                pick_ref[w, tile : tile + 1, :] = jnp.where(
                    jnp.full((1, width), partner - base + HALO, jnp.int32) == w, 1.0, 0.0
                )
            inside = (partner >= base) & (partner < base + blocks)
            start = pl.multiple_of(jnp.where(inside, partner - base, b) * width, width)
            chosen.append(own_ref[:, pl.ds(start, width)])
            here = slot_x == k
            hot.append((lines == jnp.where(here & inside, cols_x, -1)).astype(jnp.bfloat16))
            for w in range(HALO):
                there = here & (partner == halo_first + w) & jnp.logical_not(inside)
                far[w] = jnp.where(there, cols_x, far[w])
        for w in range(HALO):
            hot_ref[b, w * width : (w + 1) * width, :] = (lines == far[w]).astype(jnp.bfloat16)
        chosen = jnp.concatenate(chosen, axis=1)
        tiles = lax.dot_general(own, chosen, (((0,), (0,)), ((), ())), preferred_element_type=jnp.float32)
        tiles = tiles - sums_of(own) * (row_sums(chosen) * (1.0 / shots))
        for k in range(slots):
            spread(cov_ref, b * slots + k, tiles[:, k * width : (k + 1) * width], me)
        vals = jnp.dot(own, (lines == rows_x).astype(jnp.bfloat16), preferred_element_type=jnp.float32)
        vals_ref[b] = vals.astype(jnp.bfloat16)
        other = jnp.dot(chosen, jnp.concatenate(hot, axis=0), preferred_element_type=jnp.float32)
        products += rows_of(jnp.sum(vals * other, axis=0, keepdims=True), pieces)
        firsts += rows_of(jnp.sum(vals, axis=0, keepdims=True), pieces)
        others += rows_of(jnp.sum(other, axis=0, keepdims=True), pieces)
        key = slot_x * (width * width) + rows_x * width + cols_x
        same = keyt_ref[:, b : b + 1] == key
        fit_ref[b : b + 1, :] = jnp.sum(jnp.where(same, probt_ref[:, b : b + 1], 0.0), axis=0, keepdims=True)
    early_ref[...] = jnp.concatenate(products + firsts + others, axis=0)
    sums_ref[...] = jnp.concatenate(rows_of(row_sums(own_ref[...]), blocks), axis=0)


def ready_call(partners, soft, incidence, keys_t, prob_t, after, width, groups):
    shots = soft.shape[0]
    blocks, slots = partners.shape
    edges = incidence.shape[2]
    return pl.pallas_call(
        functools.partial(ready_kernel, width),
        out_shape=[
            jax.ShapeDtypeStruct((blocks, edges), jnp.float32),
            jax.ShapeDtypeStruct((blocks, shots, edges), jnp.bfloat16),
            jax.ShapeDtypeStruct((blocks, HALO * width, edges), jnp.bfloat16),
            jax.ShapeDtypeStruct((groups, blocks * slots, width // groups, width), jnp.float32),
            jax.ShapeDtypeStruct((3 * blocks * edges // width, width), jnp.float32),
            jax.ShapeDtypeStruct((blocks, width), jnp.float32),
            jax.ShapeDtypeStruct((REACH + 1, blocks * slots, width), jnp.float32),
        ],
        in_specs=[SMEM] + [VMEM] * 4 + [ANY],
        out_specs=[VMEM] * 7,
        compiler_params=PARAMS,
        cost_estimate=pl.CostEstimate(flops=20_000_000_000, bytes_accessed=12_000_000, transcendentals=0),
    )(partners, soft, incidence, keys_t, prob_t, after)


def factors_of(came_ref, words):
    scales = came_ref[came_ref.shape[0] - TAIL : came_ref.shape[0] - TAIL + words, :]
    step = UNIT / 32767.0
    low = (scales & 65535).astype(jnp.float32) * step
    return low, lax.shift_right_logical(scales, 16).astype(jnp.float32) * step


def words_of(came_ref, word, share, factors):
    words = came_ref[word * share : (word + 1) * share, :]
    low = lax.shift_right_arithmetic(words << 16, 16).astype(jnp.float32)
    high = lax.shift_right_arithmetic(words, 16).astype(jnp.float32)
    return low * factors[0][word : word + 1, :], high * factors[1][word : word + 1, :]


def encode(exact, sums, edges, out_ref):
    tiles, share, _ = exact.shape
    words = tiles // 2
    body = words * share
    out_ref[body + words : body + words + REACH, :] = sums
    out_ref[body + words + REACH :, :] = edges
    scales, steps = [], []
    for i in range(2):
        tops = [jnp.max(jnp.abs(exact[2 * word + i]), axis=0, keepdims=True) for word in range(words)]
        scale = jnp.floor(jnp.concatenate(tops, axis=0) * (1.0 / UNIT)).astype(jnp.int32) + 1
        scales.append(scale)
        steps.append(32767.0 / (scale.astype(jnp.float32) * UNIT))
    out_ref[body : body + words, :] = (scales[1] << 16) | scales[0]
    for word in range(words):
        low, high = [
            jnp.floor(exact[2 * word + i] * steps[i][word : word + 1, :] + 0.5).astype(jnp.int32) for i in range(2)
        ]
        out_ref[word * share : (word + 1) * share, :] = (high << 16) | (low & 65535)


def pair_kernel(
    partners_ref, left_ref, right_ref, own_ref, vals_ref, hot_ref, early_ref, own_sums_ref, _,
    cov_ref, edge_ref, sums_ref, up_ref, down_ref,
):
    blocks, slots = partners_ref.shape
    mine = blocks // 2
    shots = own_ref.shape[0]
    groups = cov_ref.shape[0]
    width = cov_ref.shape[3]
    pieces = hot_ref.shape[2] // width
    me = lax.axis_index("shot")
    base = group_index() * blocks
    halves = [ref[...] for ref in (left_ref, right_ref)]
    halo_sums = [row_sums(halo) for halo in halves]
    products, others = [], []
    for block in range(blocks):
        side = block // mine
        halo = halves[side]
        offsets = [w + (blocks if side else -HALO) for w in range(HALO)]
        own = own_ref[:, block * width : (block + 1) * width]
        reached = [w for w in range(HALO) if abs(block - offsets[w]) <= HALO]
        first, last = reached[0] * width, (reached[-1] + 1) * width
        tiles = lax.dot_general(
            own, halo[:, first:last], (((0,), (0,)), ((), ())), preferred_element_type=jnp.float32
        )
        tiles = tiles - sums_of(own) * (halo_sums[side][:, first:last] * (1.0 / shots))
        for n, w in enumerate(reached):
            for k in range(1, slots):
                partner = partners_ref[block, k]

                @pl.when((partner >= 0) & (partner == base + offsets[w]))
                def _():
                    spread(cov_ref, block * slots + k, tiles[:, n * width : (n + 1) * width], me)

        other = jnp.dot(halo, hot_ref[block], preferred_element_type=jnp.float32)
        product = jnp.sum(vals_ref[block].astype(jnp.float32) * other, axis=0, keepdims=True)
        products += rows_of(product, pieces)
        others += rows_of(jnp.sum(other, axis=0, keepdims=True), pieces)
    count = blocks * pieces
    sums = fixed(
        jnp.concatenate(rows_of(halo_sums[0], HALO) + [own_sums_ref[...]] + rows_of(halo_sums[1], HALO), axis=0)
    )
    edges = early_ref[...] + jnp.concatenate(
        products + [jnp.zeros((count, width), jnp.float32)] + others, axis=0
    )
    edges = fixed(edges)
    sums_ref[...] = sums
    edge_ref[...] = edges
    encode(cov_ref.at[groups // 2], sums, edges, up_ref)
    encode(cov_ref.at[groups // 2 + 1], sums, edges, down_ref)


def pair_call(partners, left, right, soft, vals, hot, early, own_sums, cov):
    _, tiles, share, width = cov.shape
    message = jax.ShapeDtypeStruct((tiles // 2 * share + TAIL, width), jnp.int32)
    return pl.pallas_call(
        pair_kernel,
        out_shape=[
            jax.ShapeDtypeStruct(cov.shape, jnp.float32),
            jax.ShapeDtypeStruct(early.shape, jnp.int32),
            jax.ShapeDtypeStruct((REACH, width), jnp.int32),
            message,
            message,
        ],
        in_specs=[SMEM] + [VMEM] * 8,
        out_specs=[VMEM] * 5,
        input_output_aliases={8: 0},
        compiler_params=PARAMS,
        cost_estimate=pl.CostEstimate(flops=2_000_000_000, bytes_accessed=4_000_000, transcendentals=0),
    )(partners, left, right, soft, vals, hot, early, own_sums, cov)


def picked(pick_ref, rows):
    total = pick_ref[0] * rows[0:1, :]
    for w in range(1, REACH):
        total = total + pick_ref[w] * rows[w : w + 1, :]
    return total


def hop_kernel(at, seen, came_ref, cov_ref, edge_ref, sums_ref, pick_ref, _, out_ref, exact):
    groups, tiles, share, width = cov_ref.shape
    words = tiles // 2
    body = words * share
    blocks = REACH - 2 * HALO
    slots = tiles // blocks
    old = came_ref[body + words : body + words + REACH, :]
    sums = sums_ref[...]
    shift = old.astype(jnp.float32) * (1.0 / (SCALE * SHOTS * seen)) - sums.astype(jnp.float32) * (
        1.0 / (SCALE * SHOTS)
    )
    others = picked(pick_ref, shift)
    factors = factors_of(came_ref, words)
    dest = lax.rem(lax.axis_index("shot") + at, groups)
    for block in range(blocks):
        column = column_of(shift[block + HALO : block + HALO + 1, :], dest * share, share)
        column = column * (float(SHOTS) * seen / (seen + 1))
        for pair in range(slots // 2):
            word = block * (slots // 2) + pair
            came = words_of(came_ref, word, share, factors)
            for i in range(2):
                tile = 2 * word + i
                exact[tile] = cov_ref[at, tile] + came[i] + column * others[tile : tile + 1, :]
    encode(exact, sums + old, edge_ref[...] + came_ref[body + words + REACH :, :], out_ref)


def hop_call(at, seen, came, parts, after):
    tiles, share, width = parts[0].shape[1:]
    return pl.pallas_call(
        functools.partial(hop_kernel, at, seen),
        out_shape=jax.ShapeDtypeStruct(came.shape, jnp.int32),
        in_specs=[VMEM] * 5 + [ANY],
        out_specs=VMEM,
        scratch_shapes=[pltpu.VMEM((tiles, share, width), jnp.float32)],
        compiler_params=PARAMS,
        cost_estimate=pl.CostEstimate(flops=1_000_000, bytes_accessed=600_000, transcendentals=0),
    )(came, *parts, after)


def final_kernel(
    rises, falls, inc_ref, rising_ref, falling_ref, cov_ref, edge_ref, sums_ref, pick_ref, fit_ref,
    pair_ref, grad_ref,
):
    groups, tiles, share, width = cov_ref.shape
    words = tiles // 2
    body = words * share
    blocks, slots = pair_ref.shape[:2]
    pieces = inc_ref.shape[2] // width
    count = float(SHOTS * groups)
    start = lax.axis_index("shot") * share
    sums = sums_ref[...]
    rise_sums = rising_ref[body + words : body + words + REACH, :]
    fall_sums = falling_ref[body + words : body + words + REACH, :]

    def mean(values, sources):
        return values.astype(jnp.float32) * (1.0 / (SCALE * SHOTS * sources))

    first_shift = mean(rise_sums, rises) - mean(sums, 1)
    second_shift = mean(fall_sums, falls) - mean(sums + rise_sums, rises + 1)
    totals = (sums + rise_sums + fall_sums).astype(jnp.float32) * (1.0 / SCALE)
    firsts, seconds, alls = picked(pick_ref, first_shift), picked(pick_ref, second_shift), picked(pick_ref, totals)
    first_weight = float(SHOTS) * rises / (rises + 1)
    second_weight = float(SHOTS) * falls * (rises + 1) / (rises + 1 + falls)
    edges = edge_ref[...] + rising_ref[body + words + REACH :, :] + falling_ref[body + words + REACH :, :]
    edges = edges.astype(jnp.float32) * (1.0 / SCALE)
    risen_factors, fallen_factors = factors_of(rising_ref, words), factors_of(falling_ref, words)
    for block in range(blocks):
        own = slice(block + HALO, block + HALO + 1)
        first_column = column_of(first_shift[own, :], start, share) * first_weight
        second_column = column_of(second_shift[own, :], start, share) * second_weight
        total_column = column_of(totals[own, :], start, share) * (1.0 / count)
        for pair in range(slots // 2):
            word = block * (slots // 2) + pair
            risen = words_of(rising_ref, word, share, risen_factors)
            fallen = words_of(falling_ref, word, share, fallen_factors)
            for i in range(2):
                row = slice(2 * word + i, 2 * word + i + 1)
                cov = cov_ref[0, 2 * word + i] + risen[i] + first_column * firsts[row, :]
                cov = cov + fallen[i] + second_column * seconds[row, :]
                alone = total_column * alls[row, :]
                entry = 0.5 - 0.5 * jnp.sqrt(alone / (alone + cov))
                pair_ref[block, 2 * pair + i] = (entry * pick_ref[REACH, row, :]).astype(jnp.bfloat16)
        for p in range(pieces):
            n = block * pieces + p
            at = slice(p * width, (p + 1) * width)
            slot_x = inc_ref[1, block : block + 1, at]
            live = jnp.zeros((1, width), jnp.float32)
            for k in range(slots):
                tile = block * slots + k
                live = live + jnp.where(slot_x == k, pick_ref[REACH, tile : tile + 1, :], 0.0)
            rows = blocks * pieces
            quotient = (edges[rows + n : rows + n + 1] / count) * (
                edges[2 * rows + n : 2 * rows + n + 1] / count
            ) * count / edges[n : n + 1]
            entry = (0.5 - 0.5 * jnp.sqrt(quotient)) * live
            residual = live * (entry - fit_ref[block : block + 1, at]) / NOISE_SPREAD
            grad_ref[block : block + 1, at] = -residual / NOISE_SPREAD


def final_call(slots, incidence, rising, falling, parts, fit):
    groups, tiles, share, width = parts[0].shape
    half = groups // 2
    return pl.pallas_call(
        functools.partial(final_kernel, half, groups - 1 - half),
        out_shape=[
            jax.ShapeDtypeStruct((tiles // slots, slots, share, width), jnp.bfloat16),
            jax.ShapeDtypeStruct((tiles // slots, incidence.shape[2]), jnp.float32),
        ],
        in_specs=[VMEM] * 8,
        out_specs=[VMEM] * 2,
        compiler_params=PARAMS,
        cost_estimate=pl.CostEstimate(flops=1_000_000, bytes_accessed=2_000_000, transcendentals=100_000),
    )(incidence, rising, falling, *parts, fit)


def local(soft, partners, incidence, edge_prob):
    shots, own_width = soft.shape
    blocks, slots = partners.shape
    width = own_width // blocks
    groups = lax.axis_size("shot")
    sides = lax.axis_size(("row", "col"))

    head, tail, cut = cut_call(soft, HALO * width)
    left = lax.ppermute(tail, ("row", "col"), [(i, (i + 1) % sides) for i in range(sides)])
    right = lax.ppermute(head, ("row", "col"), [((i + 1) % sides, i) for i in range(sides)])

    keys = incidence[1] * (width * width) + incidence[0] * width + incidence[2]
    fit, vals, hot, cov, early, own_sums, pick = ready_call(
        partners, soft, incidence, keys.T, edge_prob.T, cut, width, groups
    )
    cov, edges, sums, up, down = pair_call(partners, left, right, soft, vals, hot, early, own_sums, cov)
    parts = (cov, edges, sums, pick)

    half = groups // 2
    rise = [(i, (i + 1) % groups) for i in range(groups)]
    fall = [(b, a) for a, b in rise]
    rising = lax.ppermute(up, "shot", rise)
    falling = lax.ppermute(down, "shot", fall)
    order = down
    for step in range(1, half):
        order = hop_call(half - step, step, rising, parts, order)
        rising = lax.ppermute(order, "shot", rise)
        if step < half - 1:
            order = hop_call(half + 1 + step, step, falling, parts, order)
            falling = lax.ppermute(order, "shot", fall)
    return final_call(slots, incidence, rising, falling, parts, fit)


def solution(mesh):
    placed = (
        P("shot", ("row", "col")),
        P(("row", "col"), None),
        P(None, ("row", "col"), None),
        P(("row", "col"), None),
    )
    return jax.shard_map(
        local,
        mesh=mesh,
        in_specs=placed,
        out_specs=(P(("row", "col"), None, "shot", None), P(("row", "col"), None)),
        check_vma=False,
    )
```

```python
import functools

import jax
import jax.numpy as jnp
from jax import lax
from jax.experimental import pallas as pl
from jax.experimental.pallas import tpu as pltpu
from jax.sharding import PartitionSpec as P

HALO = 2
REACH = 8
NOISE_SPREAD = 0.05
SCALE = 131072.0
UNIT = 1600.0 / 65535.0
SHOTS = 768
TAIL = 40
ANY = pl.BlockSpec(memory_space=pl.ANY)
VMEM = pl.BlockSpec(memory_space=pltpu.VMEM)
SMEM = pl.BlockSpec(memory_space=pltpu.SMEM)
PARAMS = pltpu.CompilerParams(vmem_limit_bytes=20 * 1024 * 1024)


def fixed(values):
    return jnp.floor(values * SCALE + 0.5).astype(jnp.int32)


def column_of(row, first, count):
    spot = lax.broadcasted_iota(jnp.int32, (count, row.shape[1]), 1) == (
        lax.broadcasted_iota(jnp.int32, (count, row.shape[1]), 0) + first
    )
    return jnp.sum(jnp.where(spot, row, 0.0), axis=1, keepdims=True)


def group_index():
    return lax.axis_index("row") * lax.axis_size("col") + lax.axis_index("col")


def row_sums(values):
    ones = jnp.ones((8, values.shape[0]), jnp.bfloat16)
    return jnp.dot(ones, values, preferred_element_type=jnp.float32)[0:1, :]


def sums_of(values):
    ones = jnp.ones((values.shape[0], 128), jnp.bfloat16)
    return lax.dot_general(values, ones, (((0,), (0,)), ((), ())), preferred_element_type=jnp.float32)[:, 0:1]


def cut_kernel(soft_ref, head_ref, tail_ref, done_ref, sems):
    width = soft_ref.shape[1]
    reach = head_ref.shape[1]
    copies = [
        pltpu.make_async_copy(soft_ref.at[:, pl.ds(width - reach, reach)], tail_ref, sems.at[0]),
        pltpu.make_async_copy(soft_ref.at[:, pl.ds(0, reach)], head_ref, sems.at[1]),
    ]
    for copy in copies:
        copy.start()
    done_ref[...] = jnp.zeros_like(done_ref)
    for copy in copies:
        copy.wait()


def cut_call(soft, reach):
    shape = jax.ShapeDtypeStruct((soft.shape[0], reach), soft.dtype)
    return pl.pallas_call(
        cut_kernel,
        out_shape=[shape, shape, jax.ShapeDtypeStruct((8, 128), jnp.float32)],
        in_specs=[ANY],
        out_specs=[VMEM, VMEM, VMEM],
        scratch_shapes=[pltpu.SemaphoreType.DMA((2,))],
        compiler_params=PARAMS,
        cost_estimate=pl.CostEstimate(flops=0, bytes_accessed=3_000_000, transcendentals=0),
    )(soft)


def spread(cov_ref, slot, tile, me):
    groups, _, share, _ = cov_ref.shape
    for d in range(groups):
        at = lax.rem(d - me + groups, groups)
        cov_ref[at, slot] = tile[d * share : (d + 1) * share, :]


def rows_of(row, pieces):
    width = row.shape[1] // pieces
    return [row[:, p * width : (p + 1) * width] for p in range(pieces)]


def ready_kernel(
    width, partners_ref, own_ref, inc_ref, keyt_ref, probt_ref, _,
    fit_ref, vals_ref, hot_ref, cov_ref, early_ref, sums_ref, pick_ref,
):
    blocks, slots = partners_ref.shape
    mine = blocks // 2
    shots = own_ref.shape[0]
    edges = inc_ref.shape[2]
    pieces = edges // width
    me = lax.axis_index("shot")
    base = group_index() * blocks
    lines = lax.broadcasted_iota(jnp.int32, (width, edges), 0)
    products, firsts, others = [], [], []
    for b in range(blocks):
        own = own_ref[:, b * width : (b + 1) * width]
        rows_x = inc_ref[0, b : b + 1, :]
        slot_x = inc_ref[1, b : b + 1, :]
        cols_x = inc_ref[2, b : b + 1, :]
        halo_first = base - HALO if b < mine else base + blocks
        chosen, hot = [], []
        far = [jnp.full((1, edges), -1, jnp.int32) for _ in range(HALO)]
        for k in range(slots):
            partner = partners_ref[b, k]
            tile = b * slots + k
            pick_ref[REACH, tile : tile + 1, :] = jnp.where(
                jnp.full((1, width), partner, jnp.int32) >= 0, 1.0, 0.0
            )
            partner = jnp.where(partner >= 0, partner, base + b)
            for w in range(REACH):
                pick_ref[w, tile : tile + 1, :] = jnp.where(
                    jnp.full((1, width), partner - base + HALO, jnp.int32) == w, 1.0, 0.0
                )
            inside = (partner >= base) & (partner < base + blocks)
            start = pl.multiple_of(jnp.where(inside, partner - base, b) * width, width)
            chosen.append(own_ref[:, pl.ds(start, width)])
            here = slot_x == k
            hot.append((lines == jnp.where(here & inside, cols_x, -1)).astype(jnp.bfloat16))
            for w in range(HALO):
                there = here & (partner == halo_first + w) & jnp.logical_not(inside)
                far[w] = jnp.where(there, cols_x, far[w])
        for w in range(HALO):
            hot_ref[b, w * width : (w + 1) * width, :] = (lines == far[w]).astype(jnp.bfloat16)
        chosen = jnp.concatenate(chosen, axis=1)
        tiles = lax.dot_general(own, chosen, (((0,), (0,)), ((), ())), preferred_element_type=jnp.float32)
        tiles = tiles - sums_of(own) * (row_sums(chosen) * (1.0 / shots))
        for k in range(slots):
            spread(cov_ref, b * slots + k, tiles[:, k * width : (k + 1) * width], me)
        vals = jnp.dot(own, (lines == rows_x).astype(jnp.bfloat16), preferred_element_type=jnp.float32)
        vals_ref[b] = vals.astype(jnp.bfloat16)
        other = jnp.dot(chosen, jnp.concatenate(hot, axis=0), preferred_element_type=jnp.float32)
        products += rows_of(jnp.sum(vals * other, axis=0, keepdims=True), pieces)
        firsts += rows_of(jnp.sum(vals, axis=0, keepdims=True), pieces)
        others += rows_of(jnp.sum(other, axis=0, keepdims=True), pieces)
        key = slot_x * (width * width) + rows_x * width + cols_x
        same = keyt_ref[:, b : b + 1] == key
        fit_ref[b : b + 1, :] = jnp.sum(jnp.where(same, probt_ref[:, b : b + 1], 0.0), axis=0, keepdims=True)
    early_ref[...] = jnp.concatenate(products + firsts + others, axis=0)
    sums_ref[...] = jnp.concatenate(rows_of(row_sums(own_ref[...]), blocks), axis=0)


def ready_call(partners, soft, incidence, keys_t, prob_t, after, width, groups):
    shots = soft.shape[0]
    blocks, slots = partners.shape
    edges = incidence.shape[2]
    return pl.pallas_call(
        functools.partial(ready_kernel, width),
        out_shape=[
            jax.ShapeDtypeStruct((blocks, edges), jnp.float32),
            jax.ShapeDtypeStruct((blocks, shots, edges), jnp.bfloat16),
            jax.ShapeDtypeStruct((blocks, HALO * width, edges), jnp.bfloat16),
            jax.ShapeDtypeStruct((groups, blocks * slots, width // groups, width), jnp.float32),
            jax.ShapeDtypeStruct((3 * blocks * edges // width, width), jnp.float32),
            jax.ShapeDtypeStruct((blocks, width), jnp.float32),
            jax.ShapeDtypeStruct((REACH + 1, blocks * slots, width), jnp.float32),
        ],
        in_specs=[SMEM] + [VMEM] * 4 + [ANY],
        out_specs=[VMEM] * 7,
        compiler_params=PARAMS,
        cost_estimate=pl.CostEstimate(flops=20_000_000_000, bytes_accessed=12_000_000, transcendentals=0),
    )(partners, soft, incidence, keys_t, prob_t, after)


def factors_of(came_ref, words):
    scales = came_ref[came_ref.shape[0] - TAIL : came_ref.shape[0] - TAIL + words, :]
    step = UNIT / 32767.0
    low = (scales & 65535).astype(jnp.float32) * step
    return low, lax.shift_right_logical(scales, 16).astype(jnp.float32) * step


def words_of(came_ref, word, share, factors):
    words = came_ref[word * share : (word + 1) * share, :]
    low = lax.shift_right_arithmetic(words << 16, 16).astype(jnp.float32)
    high = lax.shift_right_arithmetic(words, 16).astype(jnp.float32)
    return low * factors[0][word : word + 1, :], high * factors[1][word : word + 1, :]


def encode(exact, sums, edges, out_ref):
    tiles, share, _ = exact.shape
    words = tiles // 2
    body = words * share
    out_ref[body + words : body + words + REACH, :] = sums
    out_ref[body + words + REACH :, :] = edges
    scales, steps = [], []
    for i in range(2):
        tops = [jnp.max(jnp.abs(exact[2 * word + i]), axis=0, keepdims=True) for word in range(words)]
        scale = jnp.floor(jnp.concatenate(tops, axis=0) * (1.0 / UNIT)).astype(jnp.int32) + 1
        scales.append(scale)
        steps.append(32767.0 / (scale.astype(jnp.float32) * UNIT))
    out_ref[body : body + words, :] = (scales[1] << 16) | scales[0]
    for word in range(words):
        low, high = [
            jnp.floor(exact[2 * word + i] * steps[i][word : word + 1, :] + 0.5).astype(jnp.int32) for i in range(2)
        ]
        out_ref[word * share : (word + 1) * share, :] = (high << 16) | (low & 65535)


def pair_kernel(
    partners_ref, left_ref, right_ref, own_ref, vals_ref, hot_ref, early_ref, own_sums_ref, _,
    cov_ref, edge_ref, sums_ref, up_ref, down_ref, turn_ref,
):
    blocks, slots = partners_ref.shape
    mine = blocks // 2
    shots = own_ref.shape[0]
    groups = cov_ref.shape[0]
    width = cov_ref.shape[3]
    pieces = hot_ref.shape[2] // width
    me = lax.axis_index("shot")
    base = group_index() * blocks
    halves = [ref[...] for ref in (left_ref, right_ref)]
    halo_sums = [row_sums(halo) for halo in halves]
    products, others = [], []
    for block in range(blocks):
        side = block // mine
        halo = halves[side]
        offsets = [w + (blocks if side else -HALO) for w in range(HALO)]
        own = own_ref[:, block * width : (block + 1) * width]
        reached = [w for w in range(HALO) if abs(block - offsets[w]) <= HALO]
        first, last = reached[0] * width, (reached[-1] + 1) * width
        tiles = lax.dot_general(
            own, halo[:, first:last], (((0,), (0,)), ((), ())), preferred_element_type=jnp.float32
        )
        tiles = tiles - sums_of(own) * (halo_sums[side][:, first:last] * (1.0 / shots))
        for n, w in enumerate(reached):
            for k in range(1, slots):
                partner = partners_ref[block, k]

                @pl.when((partner >= 0) & (partner == base + offsets[w]))
                def _():
                    spread(cov_ref, block * slots + k, tiles[:, n * width : (n + 1) * width], me)

        other = jnp.dot(halo, hot_ref[block], preferred_element_type=jnp.float32)
        product = jnp.sum(vals_ref[block].astype(jnp.float32) * other, axis=0, keepdims=True)
        products += rows_of(product, pieces)
        others += rows_of(jnp.sum(other, axis=0, keepdims=True), pieces)
    count = blocks * pieces
    sums = fixed(
        jnp.concatenate(rows_of(halo_sums[0], HALO) + [own_sums_ref[...]] + rows_of(halo_sums[1], HALO), axis=0)
    )
    edges = early_ref[...] + jnp.concatenate(
        products + [jnp.zeros((count, width), jnp.float32)] + others, axis=0
    )
    edges = fixed(edges)
    sums_ref[...] = sums
    edge_ref[...] = edges
    encode(cov_ref.at[groups // 2], sums, edges, up_ref)
    encode(cov_ref.at[groups // 2 + 1], sums, edges, down_ref)
    turn_ref[...] = jnp.where(me == groups - 1, up_ref[...], down_ref[...])


def pair_call(partners, left, right, soft, vals, hot, early, own_sums, cov):
    _, tiles, share, width = cov.shape
    message = jax.ShapeDtypeStruct((tiles // 2 * share + TAIL, width), jnp.int32)
    return pl.pallas_call(
        pair_kernel,
        out_shape=[
            jax.ShapeDtypeStruct(cov.shape, jnp.float32),
            jax.ShapeDtypeStruct(early.shape, jnp.int32),
            jax.ShapeDtypeStruct((REACH, width), jnp.int32),
            message,
            message,
            message,
        ],
        in_specs=[SMEM] + [VMEM] * 8,
        out_specs=[VMEM] * 6,
        input_output_aliases={8: 0},
        compiler_params=PARAMS,
        cost_estimate=pl.CostEstimate(flops=2_000_000_000, bytes_accessed=4_000_000, transcendentals=0),
    )(partners, left, right, soft, vals, hot, early, own_sums, cov)


def picked(pick_ref, rows):
    total = pick_ref[0] * rows[0:1, :]
    for w in range(1, REACH):
        total = total + pick_ref[w] * rows[w : w + 1, :]
    return total


def hop_kernel(step, up, came_ref, turned_ref, cov_ref, edge_ref, sums_ref, pick_ref, *refs):
    out_ref = refs[1]
    came, exact = refs[-2:]
    groups, tiles, share, width = cov_ref.shape
    words = tiles // 2
    body = words * share
    blocks = REACH - 2 * HALO
    slots = tiles // blocks
    me = lax.axis_index("shot")
    reach = groups // 2 if up else groups // 2 - 1
    place = me if up else groups - 1 - me
    late = jnp.where((place < reach) & (step > 1 + place), 1, 0)
    hop = reach + 1 - step + late
    seen = jnp.full((1, width), reach - hop, jnp.int32).astype(jnp.float32)
    at = hop if up else lax.rem(groups - hop, groups)
    came[...] = jnp.where(place == 0, turned_ref[...], came_ref[...])
    old = came[body + words : body + words + REACH, :]
    sums = sums_ref[...]
    shift = (
        old.astype(jnp.float32) * (1.0 / jnp.maximum(seen, 1.0)) - sums.astype(jnp.float32)
    ) * (1.0 / (SCALE * SHOTS))
    others = picked(pick_ref, shift * (seen * float(SHOTS) / (seen + 1.0)))
    factors = factors_of(came, words)
    dest = lax.rem(me + at, groups)
    for block in range(blocks):
        column = column_of(shift[block + HALO : block + HALO + 1, :], dest * share, share)
        for pair in range(slots // 2):
            word = block * (slots // 2) + pair
            values = words_of(came, word, share, factors)
            for i in range(2):
                tile = 2 * word + i
                exact[tile] = cov_ref[at, tile] + values[i] + column * others[tile : tile + 1, :]
    encode(exact, sums + old, edge_ref[...] + came[body + words + REACH :, :], out_ref)
    if not up:
        refs[2][...] = jnp.where(me == groups - 1, refs[0][...], out_ref[...])


def hop_call(step, up, came, turned, parts, risen):
    tiles, share, width = parts[0].shape[1:]
    shape = jax.ShapeDtypeStruct(came.shape, jnp.int32)
    return pl.pallas_call(
        functools.partial(hop_kernel, step, up),
        out_shape=shape if up else [shape, shape],
        in_specs=[VMEM] * 6 + [ANY if up else VMEM],
        out_specs=VMEM if up else [VMEM, VMEM],
        scratch_shapes=[pltpu.VMEM(came.shape, jnp.int32), pltpu.VMEM((tiles, share, width), jnp.float32)],
        compiler_params=PARAMS,
        cost_estimate=pl.CostEstimate(flops=1_000_000, bytes_accessed=600_000, transcendentals=0),
    )(came, turned, *parts, risen)


def final_kernel(
    rises, falls, inc_ref, rising_refs, falling_refs, cov_ref, edge_ref, sums_ref, pick_ref, fit_ref,
    pair_ref, grad_ref, rising_ref, falling_ref,
):
    groups, tiles, share, width = cov_ref.shape
    words = tiles // 2
    body = words * share
    blocks, slots = pair_ref.shape[:2]
    pieces = inc_ref.shape[2] // width
    count = float(SHOTS * groups)
    me = lax.axis_index("shot")
    start = me * share
    for out, refs, place, arc in (
        (rising_ref, rising_refs, me, rises), (falling_ref, falling_refs, groups - 1 - me, falls),
    ):
        late = jnp.where(place < arc, refs[1][...], refs[0][...])
        out[...] = jnp.where(place == 0, refs[2][...], late)
    sums = sums_ref[...]
    rise_sums = rising_ref[body + words : body + words + REACH, :]
    fall_sums = falling_ref[body + words : body + words + REACH, :]

    def mean(values, sources):
        return values.astype(jnp.float32) * (1.0 / (SCALE * SHOTS * sources))

    first_shift = mean(rise_sums, rises) - mean(sums, 1)
    second_shift = mean(fall_sums, falls) - mean(sums + rise_sums, rises + 1)
    totals = (sums + rise_sums + fall_sums).astype(jnp.float32) * (1.0 / SCALE)
    firsts, seconds, alls = picked(pick_ref, first_shift), picked(pick_ref, second_shift), picked(pick_ref, totals)
    first_weight = float(SHOTS) * rises / (rises + 1)
    second_weight = float(SHOTS) * falls * (rises + 1) / (rises + 1 + falls)
    edges = edge_ref[...] + rising_ref[body + words + REACH :, :] + falling_ref[body + words + REACH :, :]
    edges = edges.astype(jnp.float32) * (1.0 / SCALE)
    risen_factors, fallen_factors = factors_of(rising_ref, words), factors_of(falling_ref, words)
    for block in range(blocks):
        own = slice(block + HALO, block + HALO + 1)
        first_column = column_of(first_shift[own, :], start, share) * first_weight
        second_column = column_of(second_shift[own, :], start, share) * second_weight
        total_column = column_of(totals[own, :], start, share) * (1.0 / count)
        for pair in range(slots // 2):
            word = block * (slots // 2) + pair
            risen = words_of(rising_ref, word, share, risen_factors)
            fallen = words_of(falling_ref, word, share, fallen_factors)
            for i in range(2):
                row = slice(2 * word + i, 2 * word + i + 1)
                cov = cov_ref[0, 2 * word + i] + risen[i] + first_column * firsts[row, :]
                cov = cov + fallen[i] + second_column * seconds[row, :]
                alone = total_column * alls[row, :]
                entry = 0.5 - 0.5 * jnp.sqrt(alone / (alone + cov))
                pair_ref[block, 2 * pair + i] = (entry * pick_ref[REACH, row, :]).astype(jnp.bfloat16)
        for p in range(pieces):
            n = block * pieces + p
            at = slice(p * width, (p + 1) * width)
            slot_x = inc_ref[1, block : block + 1, at]
            live = jnp.zeros((1, width), jnp.float32)
            for k in range(slots):
                tile = block * slots + k
                live = live + jnp.where(slot_x == k, pick_ref[REACH, tile : tile + 1, :], 0.0)
            rows = blocks * pieces
            quotient = (edges[rows + n : rows + n + 1] / count) * (
                edges[2 * rows + n : 2 * rows + n + 1] / count
            ) * count / edges[n : n + 1]
            entry = (0.5 - 0.5 * jnp.sqrt(quotient)) * live
            residual = live * (entry - fit_ref[block : block + 1, at]) / NOISE_SPREAD
            grad_ref[block : block + 1, at] = -residual / NOISE_SPREAD


def final_call(slots, incidence, rising, falling, parts, fit):
    groups, tiles, share, width = parts[0].shape
    half = groups // 2
    message = pltpu.VMEM(rising[0].shape, jnp.int32)

    def kernel(inc_ref, *refs):
        final_kernel(half, groups - 1 - half, inc_ref, refs[:3], refs[3:6], *refs[6:])

    return pl.pallas_call(
        kernel,
        out_shape=[
            jax.ShapeDtypeStruct((tiles // slots, slots, share, width), jnp.bfloat16),
            jax.ShapeDtypeStruct((tiles // slots, incidence.shape[2]), jnp.float32),
        ],
        in_specs=[VMEM] * 12,
        out_specs=[VMEM] * 2,
        scratch_shapes=[message, message],
        compiler_params=PARAMS,
        cost_estimate=pl.CostEstimate(flops=1_000_000, bytes_accessed=2_000_000, transcendentals=100_000),
    )(incidence, *rising, *falling, *parts, fit)


def local(soft, partners, incidence, edge_prob):
    shots, own_width = soft.shape
    blocks, slots = partners.shape
    width = own_width // blocks
    groups = lax.axis_size("shot")
    sides = lax.axis_size(("row", "col"))

    head, tail, cut = cut_call(soft, HALO * width)
    left = lax.ppermute(tail, ("row", "col"), [(i, (i + 1) % sides) for i in range(sides)])
    right = lax.ppermute(head, ("row", "col"), [((i + 1) % sides, i) for i in range(sides)])

    keys = incidence[1] * (width * width) + incidence[0] * width + incidence[2]
    fit, vals, hot, cov, early, own_sums, pick = ready_call(
        partners, soft, incidence, keys.T, edge_prob.T, cut, width, groups
    )
    cov, edges, sums, up, down, turn = pair_call(
        partners, left, right, soft, vals, hot, early, own_sums, cov
    )
    parts = (cov, edges, sums, pick)

    half = groups // 2
    rise = [(i, i + 1) for i in range(groups - 1)]
    fall = [(b, a) for a, b in rise]
    ends = [(groups - 1, 0), (0, groups - 1)]
    rising = [lax.ppermute(up, "shot", rise)]
    falling = [lax.ppermute(down, "shot", fall)]
    turned = [lax.ppermute(turn, "shot", ends)]
    for step in range(2, half + 2):
        crossed = turned[step - 3] if step > 2 else turn
        up = hop_call(step, True, rising[-1], crossed, parts, down)
        rising.append(lax.ppermute(up, "shot", rise))
        if step <= half:
            down, turn = hop_call(step, False, falling[-1], crossed, parts, up)
            falling.append(lax.ppermute(down, "shot", fall))
            turned.append(lax.ppermute(turn, "shot", ends))
    rising = (rising[half - 1], rising[half], turned[half - 1])
    falling = (falling[half - 2], falling[half - 1], turned[half - 2])
    return final_call(slots, incidence, rising, falling, parts, fit)


def solution(mesh):
    placed = (
        P("shot", ("row", "col")),
        P(("row", "col"), None),
        P(None, ("row", "col"), None),
        P(("row", "col"), None),
    )
    return jax.shard_map(
        local,
        mesh=mesh,
        in_specs=placed,
        out_specs=(P(("row", "col"), None, "shot", None), P(("row", "col"), None)),
        check_vma=False,
    )
```

```python
import functools

import jax
import jax.numpy as jnp
from jax import lax
from jax.experimental import pallas as pl
from jax.experimental.pallas import tpu as pltpu
from jax.sharding import PartitionSpec as P

HALO = 2
REACH = 8
NOISE_SPREAD = 0.05
SCALE = 131072.0
UNIT = 1600.0 / 65535.0
SHOTS = 768
TAIL = 40
ANY = pl.BlockSpec(memory_space=pl.ANY)
VMEM = pl.BlockSpec(memory_space=pltpu.VMEM)
SMEM = pl.BlockSpec(memory_space=pltpu.SMEM)
HBM = pl.BlockSpec(memory_space=pltpu.HBM)
PARAMS = pltpu.CompilerParams(vmem_limit_bytes=20 * 1024 * 1024)


def fixed(values):
    return jnp.floor(values * SCALE + 0.5).astype(jnp.int32)


def column_of(row, first, count):
    spot = lax.broadcasted_iota(jnp.int32, (count, row.shape[1]), 1) == (
        lax.broadcasted_iota(jnp.int32, (count, row.shape[1]), 0) + first
    )
    return jnp.sum(jnp.where(spot, row, 0.0), axis=1, keepdims=True)


def group_index():
    return lax.axis_index("row") * lax.axis_size("col") + lax.axis_index("col")


def row_sums(values):
    ones = jnp.ones((8, values.shape[0]), jnp.bfloat16)
    return jnp.dot(ones, values, preferred_element_type=jnp.float32)[0:1, :]


def sums_of(values):
    ones = jnp.ones((values.shape[0], 128), jnp.bfloat16)
    return lax.dot_general(values, ones, (((0,), (0,)), ((), ())), preferred_element_type=jnp.float32)[:, 0:1]


def cut_kernel(soft_ref, head_ref, tail_ref, done_ref, sems):
    width = soft_ref.shape[1]
    reach = head_ref.shape[1]
    copies = [
        pltpu.make_async_copy(soft_ref.at[:, pl.ds(width - reach, reach)], tail_ref, sems.at[0]),
        pltpu.make_async_copy(soft_ref.at[:, pl.ds(0, reach)], head_ref, sems.at[1]),
    ]
    for copy in copies:
        copy.start()
    done_ref[...] = jnp.zeros_like(done_ref)
    for copy in copies:
        copy.wait()


def cut_call(soft, reach):
    shape = jax.ShapeDtypeStruct((soft.shape[0], reach), soft.dtype)
    return pl.pallas_call(
        cut_kernel,
        out_shape=[shape, shape, jax.ShapeDtypeStruct((8, 128), jnp.float32)],
        in_specs=[HBM],
        out_specs=[VMEM, VMEM, VMEM],
        scratch_shapes=[pltpu.SemaphoreType.DMA((2,))],
        compiler_params=pltpu.CompilerParams(vmem_limit_bytes=58 * 1024 * 1024),
        cost_estimate=pl.CostEstimate(flops=0, bytes_accessed=3_000_000, transcendentals=0),
    )(soft)


def way():
    return 1 - 2 * lax.rem(lax.axis_index("row"), 2)


def spread(cov_ref, slot, tile, me):
    groups, _, share, _ = cov_ref.shape
    for d in range(groups):
        at = lax.rem((d - me) * way() + groups, groups)
        cov_ref[at, slot] = tile[d * share : (d + 1) * share, :]


def rows_of(row, pieces):
    width = row.shape[1] // pieces
    return [row[:, p * width : (p + 1) * width] for p in range(pieces)]


def ready_kernel(
    width, partners_ref, own_ref, inc_ref, keyt_ref, probt_ref, _,
    fit_ref, vals_ref, hot_ref, cov_ref, early_ref, sums_ref, pick_ref,
):
    blocks, slots = partners_ref.shape
    mine = blocks // 2
    shots = own_ref.shape[0]
    edges = inc_ref.shape[2]
    pieces = edges // width
    me = lax.axis_index("shot")
    base = group_index() * blocks
    lines = lax.broadcasted_iota(jnp.int32, (width, edges), 0)
    products, firsts, others = [], [], []
    for b in range(blocks):
        own = own_ref[:, b * width : (b + 1) * width]
        rows_x = inc_ref[0, b : b + 1, :]
        slot_x = inc_ref[1, b : b + 1, :]
        cols_x = inc_ref[2, b : b + 1, :]
        halo_first = base - HALO if b < mine else base + blocks
        chosen, hot = [], []
        far = [jnp.full((1, edges), -1, jnp.int32) for _ in range(HALO)]
        for k in range(slots):
            partner = partners_ref[b, k]
            tile = b * slots + k
            pick_ref[REACH, tile : tile + 1, :] = jnp.where(
                jnp.full((1, width), partner, jnp.int32) >= 0, 1.0, 0.0
            )
            partner = jnp.where(partner >= 0, partner, base + b)
            for w in range(REACH):
                pick_ref[w, tile : tile + 1, :] = jnp.where(
                    jnp.full((1, width), partner - base + HALO, jnp.int32) == w, 1.0, 0.0
                )
            inside = (partner >= base) & (partner < base + blocks)
            start = pl.multiple_of(jnp.where(inside, partner - base, b) * width, width)
            chosen.append(own_ref[:, pl.ds(start, width)])
            here = slot_x == k
            hot.append((lines == jnp.where(here & inside, cols_x, -1)).astype(jnp.bfloat16))
            for w in range(HALO):
                there = here & (partner == halo_first + w) & jnp.logical_not(inside)
                far[w] = jnp.where(there, cols_x, far[w])
        for w in range(HALO):
            hot_ref[b, w * width : (w + 1) * width, :] = (lines == far[w]).astype(jnp.bfloat16)
        chosen = jnp.concatenate(chosen, axis=1)
        tiles = lax.dot_general(own, chosen, (((0,), (0,)), ((), ())), preferred_element_type=jnp.float32)
        tiles = tiles - sums_of(own) * (row_sums(chosen) * (1.0 / shots))
        for k in range(slots):
            spread(cov_ref, b * slots + k, tiles[:, k * width : (k + 1) * width], me)
        vals = jnp.dot(own, (lines == rows_x).astype(jnp.bfloat16), preferred_element_type=jnp.float32)
        vals_ref[b] = vals.astype(jnp.bfloat16)
        other = jnp.dot(chosen, jnp.concatenate(hot, axis=0), preferred_element_type=jnp.float32)
        products += rows_of(jnp.sum(vals * other, axis=0, keepdims=True), pieces)
        firsts += rows_of(jnp.sum(vals, axis=0, keepdims=True), pieces)
        others += rows_of(jnp.sum(other, axis=0, keepdims=True), pieces)
        key = slot_x * (width * width) + rows_x * width + cols_x
        same = keyt_ref[:, b : b + 1] == key
        fit_ref[b : b + 1, :] = jnp.sum(jnp.where(same, probt_ref[:, b : b + 1], 0.0), axis=0, keepdims=True)
    early_ref[...] = jnp.concatenate(products + firsts + others, axis=0)
    sums_ref[...] = jnp.concatenate(rows_of(row_sums(own_ref[...]), blocks), axis=0)


def ready_call(partners, soft, incidence, keys_t, prob_t, after, width, groups):
    shots = soft.shape[0]
    blocks, slots = partners.shape
    edges = incidence.shape[2]
    return pl.pallas_call(
        functools.partial(ready_kernel, width),
        out_shape=[
            jax.ShapeDtypeStruct((blocks, edges), jnp.float32),
            jax.ShapeDtypeStruct((blocks, shots, edges), jnp.bfloat16),
            jax.ShapeDtypeStruct((blocks, HALO * width, edges), jnp.bfloat16),
            jax.ShapeDtypeStruct((groups, blocks * slots, width // groups, width), jnp.float32),
            jax.ShapeDtypeStruct((3 * blocks * edges // width, width), jnp.float32),
            jax.ShapeDtypeStruct((blocks, width), jnp.float32),
            jax.ShapeDtypeStruct((REACH + 1, blocks * slots, width), jnp.float32),
        ],
        in_specs=[SMEM] + [VMEM] * 4 + [ANY],
        out_specs=[VMEM] * 7,
        compiler_params=PARAMS,
        cost_estimate=pl.CostEstimate(flops=20_000_000_000, bytes_accessed=12_000_000, transcendentals=0),
    )(partners, soft, incidence, keys_t, prob_t, after)


def factors_of(came_ref, words):
    scales = came_ref[came_ref.shape[0] - TAIL : came_ref.shape[0] - TAIL + words, :]
    step = UNIT / 32767.0
    low = (scales & 65535).astype(jnp.float32) * step
    return low, lax.shift_right_logical(scales, 16).astype(jnp.float32) * step


def words_of(came_ref, word, share, factors):
    words = came_ref[word * share : (word + 1) * share, :]
    low = lax.shift_right_arithmetic(words << 16, 16).astype(jnp.float32)
    high = lax.shift_right_arithmetic(words, 16).astype(jnp.float32)
    return low * factors[0][word : word + 1, :], high * factors[1][word : word + 1, :]


def encode(exact, sums, edges, out_ref):
    tiles, share, _ = exact.shape
    words = tiles // 2
    body = words * share
    out_ref[body + words : body + words + REACH, :] = sums
    out_ref[body + words + REACH :, :] = edges
    scales, steps = [], []
    for i in range(2):
        tops = [jnp.max(jnp.abs(exact[2 * word + i]), axis=0, keepdims=True) for word in range(words)]
        scale = jnp.floor(jnp.concatenate(tops, axis=0) * (1.0 / UNIT)).astype(jnp.int32) + 1
        scales.append(scale)
        steps.append(32767.0 / (scale.astype(jnp.float32) * UNIT))
    out_ref[body : body + words, :] = (scales[1] << 16) | scales[0]
    for word in range(words):
        low, high = [
            jnp.floor(exact[2 * word + i] * steps[i][word : word + 1, :] + 0.5).astype(jnp.int32) for i in range(2)
        ]
        out_ref[word * share : (word + 1) * share, :] = (high << 16) | (low & 65535)


def pair_kernel(
    partners_ref, left_ref, right_ref, own_ref, vals_ref, hot_ref, early_ref, own_sums_ref, _,
    cov_ref, edge_ref, sums_ref, up_ref, down_ref,
):
    blocks, slots = partners_ref.shape
    mine = blocks // 2
    shots = own_ref.shape[0]
    groups = cov_ref.shape[0]
    width = cov_ref.shape[3]
    pieces = hot_ref.shape[2] // width
    me = lax.axis_index("shot")
    base = group_index() * blocks
    halves = [ref[...] for ref in (left_ref, right_ref)]
    halo_sums = [row_sums(halo) for halo in halves]
    products, others = [], []
    for block in range(blocks):
        side = block // mine
        halo = halves[side]
        offsets = [w + (blocks if side else -HALO) for w in range(HALO)]
        own = own_ref[:, block * width : (block + 1) * width]
        reached = [w for w in range(HALO) if abs(block - offsets[w]) <= HALO]
        first, last = reached[0] * width, (reached[-1] + 1) * width
        tiles = lax.dot_general(
            own, halo[:, first:last], (((0,), (0,)), ((), ())), preferred_element_type=jnp.float32
        )
        tiles = tiles - sums_of(own) * (halo_sums[side][:, first:last] * (1.0 / shots))
        for n, w in enumerate(reached):
            for k in range(1, slots):
                partner = partners_ref[block, k]

                @pl.when((partner >= 0) & (partner == base + offsets[w]))
                def _():
                    spread(cov_ref, block * slots + k, tiles[:, n * width : (n + 1) * width], me)

        other = jnp.dot(halo, hot_ref[block], preferred_element_type=jnp.float32)
        product = jnp.sum(vals_ref[block].astype(jnp.float32) * other, axis=0, keepdims=True)
        products += rows_of(product, pieces)
        others += rows_of(jnp.sum(other, axis=0, keepdims=True), pieces)
    count = blocks * pieces
    sums = fixed(
        jnp.concatenate(rows_of(halo_sums[0], HALO) + [own_sums_ref[...]] + rows_of(halo_sums[1], HALO), axis=0)
    )
    edges = early_ref[...] + jnp.concatenate(
        products + [jnp.zeros((count, width), jnp.float32)] + others, axis=0
    )
    edges = fixed(edges)
    sums_ref[...] = sums
    edge_ref[...] = edges
    encode(cov_ref.at[groups // 2], sums, edges, up_ref)
    encode(cov_ref.at[groups // 2 + 1], sums, edges, down_ref)


def pair_call(partners, left, right, soft, vals, hot, early, own_sums, cov):
    _, tiles, share, width = cov.shape
    message = jax.ShapeDtypeStruct((tiles // 2 * share + TAIL, width), jnp.int32)
    return pl.pallas_call(
        pair_kernel,
        out_shape=[
            jax.ShapeDtypeStruct(cov.shape, jnp.float32),
            jax.ShapeDtypeStruct(early.shape, jnp.int32),
            jax.ShapeDtypeStruct((REACH, width), jnp.int32),
            message,
            message,
        ],
        in_specs=[SMEM] + [VMEM] * 8,
        out_specs=[VMEM] * 5,
        input_output_aliases={8: 0},
        compiler_params=PARAMS,
        cost_estimate=pl.CostEstimate(flops=2_000_000_000, bytes_accessed=4_000_000, transcendentals=0),
    )(partners, left, right, soft, vals, hot, early, own_sums, cov)


def picked(pick_ref, rows):
    total = pick_ref[0] * rows[0:1, :]
    for w in range(1, REACH):
        total = total + pick_ref[w] * rows[w : w + 1, :]
    return total


def hop_kernel(at, seen, came_ref, cov_ref, edge_ref, sums_ref, pick_ref, _, out_ref, exact):
    groups, tiles, share, width = cov_ref.shape
    words = tiles // 2
    body = words * share
    blocks = REACH - 2 * HALO
    slots = tiles // blocks
    old = came_ref[body + words : body + words + REACH, :]
    sums = sums_ref[...]
    shift = old.astype(jnp.float32) * (1.0 / (SCALE * SHOTS * seen)) - sums.astype(jnp.float32) * (
        1.0 / (SCALE * SHOTS)
    )
    others = picked(pick_ref, shift)
    factors = factors_of(came_ref, words)
    dest = lax.rem(lax.axis_index("shot") + way() * at + groups, groups)
    for block in range(blocks):
        column = column_of(shift[block + HALO : block + HALO + 1, :], dest * share, share)
        column = column * (float(SHOTS) * seen / (seen + 1))
        for pair in range(slots // 2):
            word = block * (slots // 2) + pair
            came = words_of(came_ref, word, share, factors)
            for i in range(2):
                tile = 2 * word + i
                exact[tile] = cov_ref[at, tile] + came[i] + column * others[tile : tile + 1, :]
    encode(exact, sums + old, edge_ref[...] + came_ref[body + words + REACH :, :], out_ref)


def hop_call(at, seen, came, parts, after):
    tiles, share, width = parts[0].shape[1:]
    return pl.pallas_call(
        functools.partial(hop_kernel, at, seen),
        out_shape=jax.ShapeDtypeStruct(came.shape, jnp.int32),
        in_specs=[VMEM] * 5 + [ANY],
        out_specs=VMEM,
        scratch_shapes=[pltpu.VMEM((tiles, share, width), jnp.float32)],
        compiler_params=PARAMS,
        cost_estimate=pl.CostEstimate(flops=1_000_000, bytes_accessed=600_000, transcendentals=0),
    )(came, *parts, after)


def final_kernel(
    rises, falls, inc_ref, rising_ref, falling_ref, cov_ref, edge_ref, sums_ref, pick_ref, fit_ref,
    pair_ref, grad_ref,
):
    groups, tiles, share, width = cov_ref.shape
    words = tiles // 2
    body = words * share
    blocks, slots = pair_ref.shape[:2]
    pieces = inc_ref.shape[2] // width
    count = float(SHOTS * groups)
    start = lax.axis_index("shot") * share
    sums = sums_ref[...]
    rise_sums = rising_ref[body + words : body + words + REACH, :]
    fall_sums = falling_ref[body + words : body + words + REACH, :]

    def mean(values, sources):
        return values.astype(jnp.float32) * (1.0 / (SCALE * SHOTS * sources))

    first_shift = mean(rise_sums, rises) - mean(sums, 1)
    second_shift = mean(fall_sums, falls) - mean(sums + rise_sums, rises + 1)
    totals = (sums + rise_sums + fall_sums).astype(jnp.float32) * (1.0 / SCALE)
    firsts, seconds, alls = picked(pick_ref, first_shift), picked(pick_ref, second_shift), picked(pick_ref, totals)
    first_weight = float(SHOTS) * rises / (rises + 1)
    second_weight = float(SHOTS) * falls * (rises + 1) / (rises + 1 + falls)
    edges = edge_ref[...] + rising_ref[body + words + REACH :, :] + falling_ref[body + words + REACH :, :]
    edges = edges.astype(jnp.float32) * (1.0 / SCALE)
    risen_factors, fallen_factors = factors_of(rising_ref, words), factors_of(falling_ref, words)
    for block in range(blocks):
        own = slice(block + HALO, block + HALO + 1)
        first_column = column_of(first_shift[own, :], start, share) * first_weight
        second_column = column_of(second_shift[own, :], start, share) * second_weight
        total_column = column_of(totals[own, :], start, share) * (1.0 / count)
        for pair in range(slots // 2):
            word = block * (slots // 2) + pair
            risen = words_of(rising_ref, word, share, risen_factors)
            fallen = words_of(falling_ref, word, share, fallen_factors)
            for i in range(2):
                row = slice(2 * word + i, 2 * word + i + 1)
                cov = cov_ref[0, 2 * word + i] + risen[i] + first_column * firsts[row, :]
                cov = cov + fallen[i] + second_column * seconds[row, :]
                alone = total_column * alls[row, :]
                entry = 0.5 - 0.5 * jnp.sqrt(alone / (alone + cov))
                pair_ref[block, 2 * pair + i] = (entry * pick_ref[REACH, row, :]).astype(jnp.bfloat16)
        for p in range(pieces):
            n = block * pieces + p
            at = slice(p * width, (p + 1) * width)
            slot_x = inc_ref[1, block : block + 1, at]
            live = jnp.zeros((1, width), jnp.float32)
            for k in range(slots):
                tile = block * slots + k
                live = live + jnp.where(slot_x == k, pick_ref[REACH, tile : tile + 1, :], 0.0)
            rows = blocks * pieces
            quotient = (edges[rows + n : rows + n + 1] / count) * (
                edges[2 * rows + n : 2 * rows + n + 1] / count
            ) * count / edges[n : n + 1]
            entry = (0.5 - 0.5 * jnp.sqrt(quotient)) * live
            residual = live * (entry - fit_ref[block : block + 1, at]) / NOISE_SPREAD
            grad_ref[block : block + 1, at] = -residual / NOISE_SPREAD


def final_call(slots, incidence, rising, falling, parts, fit):
    groups, tiles, share, width = parts[0].shape
    half = groups // 2
    return pl.pallas_call(
        functools.partial(final_kernel, half, groups - 1 - half),
        out_shape=[
            jax.ShapeDtypeStruct((tiles // slots, slots, share, width), jnp.bfloat16),
            jax.ShapeDtypeStruct((tiles // slots, incidence.shape[2]), jnp.float32),
        ],
        in_specs=[VMEM] * 8,
        out_specs=[VMEM] * 2,
        compiler_params=PARAMS,
        cost_estimate=pl.CostEstimate(flops=1_000_000, bytes_accessed=2_000_000, transcendentals=100_000),
    )(incidence, rising, falling, *parts, fit)


def local(soft, partners, incidence, edge_prob):
    shots, own_width = soft.shape
    blocks, slots = partners.shape
    width = own_width // blocks
    groups = lax.axis_size("shot")
    sides = lax.axis_size(("row", "col"))

    head, tail, cut = cut_call(soft, HALO * width)
    left = lax.ppermute(tail, ("row", "col"), [(i, (i + 1) % sides) for i in range(sides)])
    right = lax.ppermute(head, ("row", "col"), [((i + 1) % sides, i) for i in range(sides)])

    keys = incidence[1] * (width * width) + incidence[0] * width + incidence[2]
    fit, vals, hot, cov, early, own_sums, pick = ready_call(
        partners, soft, incidence, keys.T, edge_prob.T, cut, width, groups
    )
    cov, edges, sums, up, down = pair_call(partners, left, right, soft, vals, hot, early, own_sums, cov)
    parts = (cov, edges, sums, pick)

    half = groups // 2
    rows = lax.axis_size("row")
    rise = [
        (z * rows + row, (z + 1 - 2 * (row % 2)) % groups * rows + row) for z in range(groups) for row in range(rows)
    ]
    fall = [(b, a) for a, b in rise]
    axes = ("shot", "row")
    rising = lax.ppermute(up, axes, rise)
    falling = lax.ppermute(down, axes, fall)
    order = down
    for step in range(1, half):
        order = hop_call(half - step, step, rising, parts, order)
        rising = lax.ppermute(order, axes, rise)
        if step < half - 1:
            order = hop_call(half + 1 + step, step, falling, parts, order)
            falling = lax.ppermute(order, axes, fall)
    return final_call(slots, incidence, rising, falling, parts, fit)


def solution(mesh):
    placed = (
        P("shot", ("row", "col")),
        P(("row", "col"), None),
        P(None, ("row", "col"), None),
        P(("row", "col"), None),
    )
    return jax.shard_map(
        local,
        mesh=mesh,
        in_specs=placed,
        out_specs=(P(("row", "col"), None, "shot", None), P(("row", "col"), None)),
        check_vma=False,
    )
```

```python
import functools

import jax
import jax.numpy as jnp
from jax import lax
from jax.experimental import pallas as pl
from jax.experimental.pallas import tpu as pltpu
from jax.sharding import PartitionSpec as P

HALO = 2
REACH = 8
NOISE_SPREAD = 0.05
SCALE = 131072.0
UNIT = 1600.0 / 65535.0
SHOTS = 768
TAIL = 40
ANY = pl.BlockSpec(memory_space=pl.ANY)
VMEM = pl.BlockSpec(memory_space=pltpu.VMEM)
SMEM = pl.BlockSpec(memory_space=pltpu.SMEM)
HBM = pl.BlockSpec(memory_space=pltpu.HBM)
PARAMS = pltpu.CompilerParams(vmem_limit_bytes=20 * 1024 * 1024)


def fixed(values):
    return jnp.floor(values * SCALE + 0.5).astype(jnp.int32)


def column_of(row, first, count):
    spot = lax.broadcasted_iota(jnp.int32, (count, row.shape[1]), 1) == (
        lax.broadcasted_iota(jnp.int32, (count, row.shape[1]), 0) + first
    )
    return jnp.sum(jnp.where(spot, row, 0.0), axis=1, keepdims=True)


def group_index():
    return lax.axis_index("row") * lax.axis_size("col") + lax.axis_index("col")


def row_sums(values):
    ones = jnp.ones((8, values.shape[0]), jnp.bfloat16)
    return jnp.dot(ones, values, preferred_element_type=jnp.float32)[0:1, :]


def sums_of(values):
    ones = jnp.ones((values.shape[0], 128), jnp.bfloat16)
    return lax.dot_general(values, ones, (((0,), (0,)), ((), ())), preferred_element_type=jnp.float32)[:, 0:1]


def cut_kernel(soft_ref, head_ref, tail_ref, done_ref, sems):
    width = soft_ref.shape[1]
    reach = head_ref.shape[1]
    copies = [
        pltpu.make_async_copy(soft_ref.at[:, pl.ds(width - reach, reach)], tail_ref, sems.at[0]),
        pltpu.make_async_copy(soft_ref.at[:, pl.ds(0, reach)], head_ref, sems.at[1]),
    ]
    for copy in copies:
        copy.start()
    done_ref[...] = jnp.zeros_like(done_ref)
    for copy in copies:
        copy.wait()


def cut_call(soft, reach):
    shape = jax.ShapeDtypeStruct((soft.shape[0], reach), soft.dtype)
    return pl.pallas_call(
        cut_kernel,
        out_shape=[shape, shape, jax.ShapeDtypeStruct((8, 128), jnp.float32)],
        in_specs=[HBM],
        out_specs=[ANY, ANY, VMEM],
        scratch_shapes=[pltpu.SemaphoreType.DMA((2,))],
        compiler_params=pltpu.CompilerParams(vmem_limit_bytes=51 * 1024 * 1024),
        cost_estimate=pl.CostEstimate(flops=0, bytes_accessed=3_000_000, transcendentals=0),
    )(soft)


def spread(cov_ref, slot, tile, me):
    groups, _, share, _ = cov_ref.shape
    for d in range(groups):
        at = lax.rem(d - me + groups, groups)
        cov_ref[at, slot] = tile[d * share : (d + 1) * share, :]


def rows_of(row, pieces):
    width = row.shape[1] // pieces
    return [row[:, p * width : (p + 1) * width] for p in range(pieces)]


def ready_kernel(
    width, partners_ref, soft_ref, inc_ref, keyt_ref, probt_ref, _,
    fit_ref, vals_ref, hot_ref, cov_ref, early_ref, sums_ref, pick_ref, own_ref, sem,
):
    blocks, slots = partners_ref.shape
    mine = blocks // 2
    shots = own_ref.shape[0]
    edges = inc_ref.shape[2]
    pieces = edges // width
    me = lax.axis_index("shot")
    base = group_index() * blocks
    fetch = pltpu.make_async_copy(soft_ref, own_ref, sem)
    fetch.start()
    for b in range(blocks):
        key = inc_ref[1, b : b + 1, :] * (width * width) + inc_ref[0, b : b + 1, :] * width + inc_ref[2, b : b + 1, :]
        same = keyt_ref[:, b : b + 1] == key
        fit_ref[b : b + 1, :] = jnp.sum(jnp.where(same, probt_ref[:, b : b + 1], 0.0), axis=0, keepdims=True)
    fetch.wait()
    lines = lax.broadcasted_iota(jnp.int32, (width, edges), 0)
    products, firsts, others = [], [], []
    for b in range(blocks):
        own = own_ref[:, b * width : (b + 1) * width]
        rows_x = inc_ref[0, b : b + 1, :]
        slot_x = inc_ref[1, b : b + 1, :]
        cols_x = inc_ref[2, b : b + 1, :]
        halo_first = base - HALO if b < mine else base + blocks
        chosen, hot = [], []
        far = [jnp.full((1, edges), -1, jnp.int32) for _ in range(HALO)]
        for k in range(slots):
            partner = partners_ref[b, k]
            tile = b * slots + k
            pick_ref[REACH, tile : tile + 1, :] = jnp.where(
                jnp.full((1, width), partner, jnp.int32) >= 0, 1.0, 0.0
            )
            partner = jnp.where(partner >= 0, partner, base + b)
            for w in range(REACH):
                pick_ref[w, tile : tile + 1, :] = jnp.where(
                    jnp.full((1, width), partner - base + HALO, jnp.int32) == w, 1.0, 0.0
                )
            inside = (partner >= base) & (partner < base + blocks)
            start = pl.multiple_of(jnp.where(inside, partner - base, b) * width, width)
            chosen.append(own_ref[:, pl.ds(start, width)])
            here = slot_x == k
            hot.append((lines == jnp.where(here & inside, cols_x, -1)).astype(jnp.bfloat16))
            for w in range(HALO):
                there = here & (partner == halo_first + w) & jnp.logical_not(inside)
                far[w] = jnp.where(there, cols_x, far[w])
        for w in range(HALO):
            hot_ref[b, w * width : (w + 1) * width, :] = (lines == far[w]).astype(jnp.bfloat16)
        chosen = jnp.concatenate(chosen, axis=1)
        tiles = lax.dot_general(own, chosen, (((0,), (0,)), ((), ())), preferred_element_type=jnp.float32)
        tiles = tiles - sums_of(own) * (row_sums(chosen) * (1.0 / shots))
        for k in range(slots):
            spread(cov_ref, b * slots + k, tiles[:, k * width : (k + 1) * width], me)
        vals = jnp.dot(own, (lines == rows_x).astype(jnp.bfloat16), preferred_element_type=jnp.float32)
        vals_ref[b] = vals.astype(jnp.bfloat16)
        other = jnp.dot(chosen, jnp.concatenate(hot, axis=0), preferred_element_type=jnp.float32)
        products += rows_of(jnp.sum(vals * other, axis=0, keepdims=True), pieces)
        firsts += rows_of(jnp.sum(vals, axis=0, keepdims=True), pieces)
        others += rows_of(jnp.sum(other, axis=0, keepdims=True), pieces)
    early_ref[...] = jnp.concatenate(products + firsts + others, axis=0)
    sums_ref[...] = jnp.concatenate(rows_of(row_sums(own_ref[...]), blocks), axis=0)


def ready_call(partners, soft, incidence, keys_t, prob_t, after, width, groups):
    shots = soft.shape[0]
    blocks, slots = partners.shape
    edges = incidence.shape[2]
    return pl.pallas_call(
        functools.partial(ready_kernel, width),
        out_shape=[
            jax.ShapeDtypeStruct((blocks, edges), jnp.float32),
            jax.ShapeDtypeStruct((blocks, shots, edges), jnp.bfloat16),
            jax.ShapeDtypeStruct((blocks, HALO * width, edges), jnp.bfloat16),
            jax.ShapeDtypeStruct((groups, blocks * slots, width // groups, width), jnp.float32),
            jax.ShapeDtypeStruct((3 * blocks * edges // width, width), jnp.float32),
            jax.ShapeDtypeStruct((blocks, width), jnp.float32),
            jax.ShapeDtypeStruct((REACH + 1, blocks * slots, width), jnp.float32),
        ],
        in_specs=[SMEM, ANY] + [VMEM] * 3 + [ANY],
        out_specs=[VMEM] * 7,
        scratch_shapes=[pltpu.VMEM(soft.shape, soft.dtype), pltpu.SemaphoreType.DMA],
        compiler_params=PARAMS,
        cost_estimate=pl.CostEstimate(flops=20_000_000_000, bytes_accessed=12_000_000, transcendentals=0),
    )(partners, soft, incidence, keys_t, prob_t, after)


def factors_of(came_ref, words):
    scales = came_ref[came_ref.shape[0] - TAIL : came_ref.shape[0] - TAIL + words, :]
    step = UNIT / 32767.0
    low = (scales & 65535).astype(jnp.float32) * step
    return low, lax.shift_right_logical(scales, 16).astype(jnp.float32) * step


def words_of(came_ref, word, share, factors):
    words = came_ref[word * share : (word + 1) * share, :]
    low = lax.shift_right_arithmetic(words << 16, 16).astype(jnp.float32)
    high = lax.shift_right_arithmetic(words, 16).astype(jnp.float32)
    return low * factors[0][word : word + 1, :], high * factors[1][word : word + 1, :]


def encode(exact, sums, edges, out_ref):
    tiles, share, _ = exact.shape
    words = tiles // 2
    body = words * share
    out_ref[body + words : body + words + REACH, :] = sums
    out_ref[body + words + REACH :, :] = edges
    scales, steps = [], []
    for i in range(2):
        tops = [jnp.max(jnp.abs(exact[2 * word + i]), axis=0, keepdims=True) for word in range(words)]
        scale = jnp.floor(jnp.concatenate(tops, axis=0) * (1.0 / UNIT)).astype(jnp.int32) + 1
        scales.append(scale)
        steps.append(32767.0 / (scale.astype(jnp.float32) * UNIT))
    out_ref[body : body + words, :] = (scales[1] << 16) | scales[0]
    for word in range(words):
        low, high = [
            jnp.floor(exact[2 * word + i] * steps[i][word : word + 1, :] + 0.5).astype(jnp.int32) for i in range(2)
        ]
        out_ref[word * share : (word + 1) * share, :] = (high << 16) | (low & 65535)


def pair_kernel(
    partners_ref, left_ref, right_ref, own_ref, vals_ref, hot_ref, early_ref, own_sums_ref, _,
    cov_ref, edge_ref, sums_ref, up_ref, down_ref,
):
    blocks, slots = partners_ref.shape
    mine = blocks // 2
    shots = own_ref.shape[0]
    groups = cov_ref.shape[0]
    width = cov_ref.shape[3]
    pieces = hot_ref.shape[2] // width
    me = lax.axis_index("shot")
    base = group_index() * blocks
    halves = [ref[...] for ref in (left_ref, right_ref)]
    halo_sums = [row_sums(halo) for halo in halves]
    products, others = [], []
    for block in range(blocks):
        side = block // mine
        halo = halves[side]
        offsets = [w + (blocks if side else -HALO) for w in range(HALO)]
        own = own_ref[:, block * width : (block + 1) * width]
        reached = [w for w in range(HALO) if abs(block - offsets[w]) <= HALO]
        first, last = reached[0] * width, (reached[-1] + 1) * width
        tiles = lax.dot_general(
            own, halo[:, first:last], (((0,), (0,)), ((), ())), preferred_element_type=jnp.float32
        )
        tiles = tiles - sums_of(own) * (halo_sums[side][:, first:last] * (1.0 / shots))
        for n, w in enumerate(reached):
            for k in range(1, slots):
                partner = partners_ref[block, k]

                @pl.when((partner >= 0) & (partner == base + offsets[w]))
                def _():
                    spread(cov_ref, block * slots + k, tiles[:, n * width : (n + 1) * width], me)

        other = jnp.dot(halo[:, first:last], hot_ref[block, first:last, :], preferred_element_type=jnp.float32)
        product = jnp.sum(vals_ref[block].astype(jnp.float32) * other, axis=0, keepdims=True)
        products += rows_of(product, pieces)
        others += rows_of(jnp.sum(other, axis=0, keepdims=True), pieces)
    count = blocks * pieces
    sums = fixed(
        jnp.concatenate(rows_of(halo_sums[0], HALO) + [own_sums_ref[...]] + rows_of(halo_sums[1], HALO), axis=0)
    )
    edges = early_ref[...] + jnp.concatenate(
        products + [jnp.zeros((count, width), jnp.float32)] + others, axis=0
    )
    edges = fixed(edges)
    sums_ref[...] = sums
    edge_ref[...] = edges
    encode(cov_ref.at[groups // 2], sums, edges, up_ref)
    encode(cov_ref.at[groups // 2 + 1], sums, edges, down_ref)


def pair_call(partners, left, right, soft, vals, hot, early, own_sums, cov):
    _, tiles, share, width = cov.shape
    message = jax.ShapeDtypeStruct((tiles // 2 * share + TAIL, width), jnp.int32)
    return pl.pallas_call(
        pair_kernel,
        out_shape=[
            jax.ShapeDtypeStruct(cov.shape, jnp.float32),
            jax.ShapeDtypeStruct(early.shape, jnp.int32),
            jax.ShapeDtypeStruct((REACH, width), jnp.int32),
            message,
            message,
        ],
        in_specs=[SMEM] + [VMEM] * 8,
        out_specs=[VMEM] * 5,
        input_output_aliases={8: 0},
        compiler_params=PARAMS,
        cost_estimate=pl.CostEstimate(flops=2_000_000_000, bytes_accessed=4_000_000, transcendentals=0),
    )(partners, left, right, soft, vals, hot, early, own_sums, cov)


def picked(pick_ref, rows):
    total = pick_ref[0] * rows[0:1, :]
    for w in range(1, REACH):
        total = total + pick_ref[w] * rows[w : w + 1, :]
    return total


def hop_kernel(at, seen, came_ref, cov_ref, edge_ref, sums_ref, pick_ref, _, out_ref, exact):
    groups, tiles, share, width = cov_ref.shape
    words = tiles // 2
    body = words * share
    blocks = REACH - 2 * HALO
    slots = tiles // blocks
    old = came_ref[body + words : body + words + REACH, :]
    sums = sums_ref[...]
    shift = old.astype(jnp.float32) * (1.0 / (SCALE * SHOTS * seen)) - sums.astype(jnp.float32) * (
        1.0 / (SCALE * SHOTS)
    )
    others = picked(pick_ref, shift)
    factors = factors_of(came_ref, words)
    dest = lax.rem(lax.axis_index("shot") + at, groups)
    for block in range(blocks):
        column = column_of(shift[block + HALO : block + HALO + 1, :], dest * share, share)
        column = column * (float(SHOTS) * seen / (seen + 1))
        for pair in range(slots // 2):
            word = block * (slots // 2) + pair
            came = words_of(came_ref, word, share, factors)
            for i in range(2):
                tile = 2 * word + i
                exact[tile] = cov_ref[at, tile] + came[i] + column * others[tile : tile + 1, :]
    encode(exact, sums + old, edge_ref[...] + came_ref[body + words + REACH :, :], out_ref)


def hop_call(at, seen, came, parts, after):
    tiles, share, width = parts[0].shape[1:]
    return pl.pallas_call(
        functools.partial(hop_kernel, at, seen),
        out_shape=jax.ShapeDtypeStruct(came.shape, jnp.int32),
        in_specs=[VMEM] * 5 + [ANY],
        out_specs=VMEM,
        scratch_shapes=[pltpu.VMEM((tiles, share, width), jnp.float32)],
        compiler_params=PARAMS,
        cost_estimate=pl.CostEstimate(flops=1_000_000, bytes_accessed=600_000, transcendentals=0),
    )(came, *parts, after)


def final_kernel(
    rises, falls, inc_ref, rising_ref, falling_ref, cov_ref, edge_ref, sums_ref, pick_ref, fit_ref,
    pair_ref, grad_ref,
):
    groups, tiles, share, width = cov_ref.shape
    words = tiles // 2
    body = words * share
    blocks, slots = pair_ref.shape[:2]
    pieces = inc_ref.shape[2] // width
    count = float(SHOTS * groups)
    start = lax.axis_index("shot") * share
    sums = sums_ref[...]
    rise_sums = rising_ref[body + words : body + words + REACH, :]
    fall_sums = falling_ref[body + words : body + words + REACH, :]

    def mean(values, sources):
        return values.astype(jnp.float32) * (1.0 / (SCALE * SHOTS * sources))

    first_shift = mean(rise_sums, rises) - mean(sums, 1)
    second_shift = mean(fall_sums, falls) - mean(sums + rise_sums, rises + 1)
    totals = (sums + rise_sums + fall_sums).astype(jnp.float32) * (1.0 / SCALE)
    firsts, seconds, alls = picked(pick_ref, first_shift), picked(pick_ref, second_shift), picked(pick_ref, totals)
    first_weight = float(SHOTS) * rises / (rises + 1)
    second_weight = float(SHOTS) * falls * (rises + 1) / (rises + 1 + falls)
    edges = edge_ref[...] + rising_ref[body + words + REACH :, :] + falling_ref[body + words + REACH :, :]
    edges = edges.astype(jnp.float32) * (1.0 / SCALE)
    risen_factors, fallen_factors = factors_of(rising_ref, words), factors_of(falling_ref, words)
    for block in range(blocks):
        own = slice(block + HALO, block + HALO + 1)
        first_column = column_of(first_shift[own, :], start, share) * first_weight
        second_column = column_of(second_shift[own, :], start, share) * second_weight
        total_column = column_of(totals[own, :], start, share) * (1.0 / count)
        for pair in range(slots // 2):
            word = block * (slots // 2) + pair
            risen = words_of(rising_ref, word, share, risen_factors)
            fallen = words_of(falling_ref, word, share, fallen_factors)
            for i in range(2):
                row = slice(2 * word + i, 2 * word + i + 1)
                cov = cov_ref[0, 2 * word + i] + risen[i] + first_column * firsts[row, :]
                cov = cov + fallen[i] + second_column * seconds[row, :]
                alone = total_column * alls[row, :]
                entry = 0.5 - 0.5 * jnp.sqrt(alone / (alone + cov))
                pair_ref[block, 2 * pair + i] = (entry * pick_ref[REACH, row, :]).astype(jnp.bfloat16)
        for p in range(pieces):
            n = block * pieces + p
            at = slice(p * width, (p + 1) * width)
            slot_x = inc_ref[1, block : block + 1, at]
            live = jnp.zeros((1, width), jnp.float32)
            for k in range(slots):
                tile = block * slots + k
                live = live + jnp.where(slot_x == k, pick_ref[REACH, tile : tile + 1, :], 0.0)
            rows = blocks * pieces
            quotient = (edges[rows + n : rows + n + 1] / count) * (
                edges[2 * rows + n : 2 * rows + n + 1] / count
            ) * count / edges[n : n + 1]
            entry = (0.5 - 0.5 * jnp.sqrt(quotient)) * live
            residual = live * (entry - fit_ref[block : block + 1, at]) / NOISE_SPREAD
            grad_ref[block : block + 1, at] = -residual / NOISE_SPREAD


def final_call(slots, incidence, rising, falling, parts, fit):
    groups, tiles, share, width = parts[0].shape
    half = groups // 2
    return pl.pallas_call(
        functools.partial(final_kernel, half, groups - 1 - half),
        out_shape=[
            jax.ShapeDtypeStruct((tiles // slots, slots, share, width), jnp.bfloat16),
            jax.ShapeDtypeStruct((tiles // slots, incidence.shape[2]), jnp.float32),
        ],
        in_specs=[VMEM] * 8,
        out_specs=[VMEM] * 2,
        compiler_params=PARAMS,
        cost_estimate=pl.CostEstimate(flops=1_000_000, bytes_accessed=2_000_000, transcendentals=100_000),
    )(incidence, rising, falling, *parts, fit)


def local(soft, partners, incidence, edge_prob):
    shots, own_width = soft.shape
    blocks, slots = partners.shape
    width = own_width // blocks
    groups = lax.axis_size("shot")
    sides = lax.axis_size(("row", "col"))

    head, tail, cut = cut_call(soft, HALO * width)
    left = lax.ppermute(tail, ("row", "col"), [(i, (i + 1) % sides) for i in range(sides)])
    right = lax.ppermute(head, ("row", "col"), [((i + 1) % sides, i) for i in range(sides)])

    keys = incidence[1] * (width * width) + incidence[0] * width + incidence[2]
    fit, vals, hot, cov, early, own_sums, pick = ready_call(
        partners, soft, incidence, keys.T, edge_prob.T, cut, width, groups
    )
    cov, edges, sums, up, down = pair_call(partners, left, right, soft, vals, hot, early, own_sums, cov)
    parts = (cov, edges, sums, pick)

    half = groups // 2
    rise = [(i, (i + 1) % groups) for i in range(groups)]
    fall = [(b, a) for a, b in rise]
    rising = lax.ppermute(up, "shot", rise)
    falling = lax.ppermute(down, "shot", fall)
    order = down
    for step in range(1, half):
        order = hop_call(half - step, step, rising, parts, order)
        rising = lax.ppermute(order, "shot", rise)
        if step < half - 1:
            order = hop_call(half + 1 + step, step, falling, parts, order)
            falling = lax.ppermute(order, "shot", fall)
    return final_call(slots, incidence, rising, falling, parts, fit)


def solution(mesh):
    placed = (
        P("shot", ("row", "col")),
        P(("row", "col"), None),
        P(None, ("row", "col"), None),
        P(("row", "col"), None),
    )
    return jax.shard_map(
        local,
        mesh=mesh,
        in_specs=placed,
        out_specs=(P(("row", "col"), None, "shot", None), P(("row", "col"), None)),
        check_vma=False,
    )
```

```python
import functools

import jax
import jax.numpy as jnp
from jax import lax
from jax.experimental import pallas as pl
from jax.experimental.pallas import tpu as pltpu
from jax.sharding import PartitionSpec as P

HALO = 2
REACH = 8
NOISE_SPREAD = 0.05
SCALE = 131072.0
UNIT = 1600.0 / 65535.0
SHOTS = 768
TAIL = 40
ANY = pl.BlockSpec(memory_space=pl.ANY)
VMEM = pl.BlockSpec(memory_space=pltpu.VMEM)
SMEM = pl.BlockSpec(memory_space=pltpu.SMEM)
HBM = pl.BlockSpec(memory_space=pltpu.HBM)
PARAMS = pltpu.CompilerParams(vmem_limit_bytes=20 * 1024 * 1024)


def fixed(values):
    return jnp.floor(values * SCALE + 0.5).astype(jnp.int32)


def column_of(row, first, count):
    spot = lax.broadcasted_iota(jnp.int32, (count, row.shape[1]), 1) == (
        lax.broadcasted_iota(jnp.int32, (count, row.shape[1]), 0) + first
    )
    return jnp.sum(jnp.where(spot, row, 0.0), axis=1, keepdims=True)


def group_index():
    return lax.axis_index("row") * lax.axis_size("col") + lax.axis_index("col")


def row_sums(values):
    ones = jnp.ones((8, values.shape[0]), jnp.bfloat16)
    return jnp.dot(ones, values, preferred_element_type=jnp.float32)[0:1, :]


def sums_of(values):
    ones = jnp.ones((values.shape[0], 128), jnp.bfloat16)
    return lax.dot_general(values, ones, (((0,), (0,)), ((), ())), preferred_element_type=jnp.float32)[:, 0:1]


def cut_kernel(soft_ref, head_ref, tail_ref, done_ref, sems):
    width = soft_ref.shape[1]
    reach = head_ref.shape[1]
    copies = [
        pltpu.make_async_copy(soft_ref.at[:, pl.ds(width - reach, reach)], tail_ref, sems.at[0]),
        pltpu.make_async_copy(soft_ref.at[:, pl.ds(0, reach)], head_ref, sems.at[1]),
    ]
    for copy in copies:
        copy.start()
    done_ref[...] = jnp.zeros_like(done_ref)
    for copy in copies:
        copy.wait()


def cut_call(soft, reach):
    shape = jax.ShapeDtypeStruct((soft.shape[0], reach), soft.dtype)
    return pl.pallas_call(
        cut_kernel,
        out_shape=[shape, shape, jax.ShapeDtypeStruct((8, 128), jnp.float32)],
        in_specs=[HBM],
        out_specs=[VMEM, VMEM, VMEM],
        scratch_shapes=[pltpu.SemaphoreType.DMA((2,))],
        compiler_params=pltpu.CompilerParams(vmem_limit_bytes=50 * 1024 * 1024),
        cost_estimate=pl.CostEstimate(flops=0, bytes_accessed=3_000_000, transcendentals=0),
    )(soft)


def spread(cov_ref, slot, tile, me):
    groups, _, share, _ = cov_ref.shape
    for d in range(groups):
        at = lax.rem(d - me + groups, groups)
        cov_ref[at, slot] = tile[d * share : (d + 1) * share, :]


def rows_of(row, pieces):
    width = row.shape[1] // pieces
    return [row[:, p * width : (p + 1) * width] for p in range(pieces)]


def ready_kernel(
    width, partners_ref, soft_ref, inc_ref, keyt_ref, probt_ref, _,
    fit_ref, vals_ref, hot_ref, cov_ref, early_ref, sums_ref, pick_ref, own_ref, sem,
):
    blocks, slots = partners_ref.shape
    mine = blocks // 2
    shots = own_ref.shape[0]
    edges = inc_ref.shape[2]
    pieces = edges // width
    me = lax.axis_index("shot")
    base = group_index() * blocks
    fetch = pltpu.make_async_copy(soft_ref, own_ref, sem)
    fetch.start()
    for b in range(blocks):
        key = inc_ref[1, b : b + 1, :] * (width * width) + inc_ref[0, b : b + 1, :] * width + inc_ref[2, b : b + 1, :]
        same = keyt_ref[:, b : b + 1] == key
        fit_ref[b : b + 1, :] = jnp.sum(jnp.where(same, probt_ref[:, b : b + 1], 0.0), axis=0, keepdims=True)
    fetch.wait()
    lines = lax.broadcasted_iota(jnp.int32, (width, edges), 0)
    products, firsts, others = [], [], []
    for b in range(blocks):
        own = own_ref[:, b * width : (b + 1) * width]
        rows_x = inc_ref[0, b : b + 1, :]
        slot_x = inc_ref[1, b : b + 1, :]
        cols_x = inc_ref[2, b : b + 1, :]
        halo_first = base - HALO if b < mine else base + blocks
        chosen, hot = [], []
        far = [jnp.full((1, edges), -1, jnp.int32) for _ in range(HALO)]
        for k in range(slots):
            partner = partners_ref[b, k]
            tile = b * slots + k
            pick_ref[REACH, tile : tile + 1, :] = jnp.where(
                jnp.full((1, width), partner, jnp.int32) >= 0, 1.0, 0.0
            )
            partner = jnp.where(partner >= 0, partner, base + b)
            for w in range(REACH):
                pick_ref[w, tile : tile + 1, :] = jnp.where(
                    jnp.full((1, width), partner - base + HALO, jnp.int32) == w, 1.0, 0.0
                )
            inside = (partner >= base) & (partner < base + blocks)
            start = pl.multiple_of(jnp.where(inside, partner - base, b) * width, width)
            chosen.append(own_ref[:, pl.ds(start, width)])
            here = slot_x == k
            hot.append((lines == jnp.where(here & inside, cols_x, -1)).astype(jnp.bfloat16))
            for w in range(HALO):
                there = here & (partner == halo_first + w) & jnp.logical_not(inside)
                far[w] = jnp.where(there, cols_x, far[w])
        for w in range(HALO):
            hot_ref[b, w * width : (w + 1) * width, :] = (lines == far[w]).astype(jnp.bfloat16)
        chosen = jnp.concatenate(chosen, axis=1)
        tiles = lax.dot_general(own, chosen, (((0,), (0,)), ((), ())), preferred_element_type=jnp.float32)
        tiles = tiles - sums_of(own) * (row_sums(chosen) * (1.0 / shots))
        for k in range(slots):
            spread(cov_ref, b * slots + k, tiles[:, k * width : (k + 1) * width], me)
        vals = jnp.dot(own, (lines == rows_x).astype(jnp.bfloat16), preferred_element_type=jnp.float32)
        vals_ref[b] = vals.astype(jnp.bfloat16)
        other = jnp.dot(chosen, jnp.concatenate(hot, axis=0), preferred_element_type=jnp.float32)
        products += rows_of(jnp.sum(vals * other, axis=0, keepdims=True), pieces)
        firsts += rows_of(jnp.sum(vals, axis=0, keepdims=True), pieces)
        others += rows_of(jnp.sum(other, axis=0, keepdims=True), pieces)
    early_ref[...] = jnp.concatenate(products + firsts + others, axis=0)
    sums_ref[...] = jnp.concatenate(rows_of(row_sums(own_ref[...]), blocks), axis=0)


def ready_call(partners, soft, incidence, keys_t, prob_t, after, width, groups):
    shots = soft.shape[0]
    blocks, slots = partners.shape
    edges = incidence.shape[2]
    return pl.pallas_call(
        functools.partial(ready_kernel, width),
        out_shape=[
            jax.ShapeDtypeStruct((blocks, edges), jnp.float32),
            jax.ShapeDtypeStruct((blocks, shots, edges), jnp.bfloat16),
            jax.ShapeDtypeStruct((blocks, HALO * width, edges), jnp.bfloat16),
            jax.ShapeDtypeStruct((groups, blocks * slots, width // groups, width), jnp.float32),
            jax.ShapeDtypeStruct((3 * blocks * edges // width, width), jnp.float32),
            jax.ShapeDtypeStruct((blocks, width), jnp.float32),
            jax.ShapeDtypeStruct((REACH + 1, blocks * slots, width), jnp.float32),
        ],
        in_specs=[SMEM, ANY] + [VMEM] * 3 + [ANY],
        out_specs=[VMEM] * 7,
        scratch_shapes=[pltpu.VMEM(soft.shape, soft.dtype), pltpu.SemaphoreType.DMA],
        compiler_params=PARAMS,
        cost_estimate=pl.CostEstimate(flops=20_000_000_000, bytes_accessed=12_000_000, transcendentals=0),
    )(partners, soft, incidence, keys_t, prob_t, after)


def factors_of(came_ref, words):
    scales = came_ref[came_ref.shape[0] - TAIL : came_ref.shape[0] - TAIL + words, :]
    step = UNIT / 32767.0
    low = (scales & 65535).astype(jnp.float32) * step
    return low, lax.shift_right_logical(scales, 16).astype(jnp.float32) * step


def words_of(came_ref, word, share, factors):
    words = came_ref[word * share : (word + 1) * share, :]
    low = lax.shift_right_arithmetic(words << 16, 16).astype(jnp.float32)
    high = lax.shift_right_arithmetic(words, 16).astype(jnp.float32)
    return low * factors[0][word : word + 1, :], high * factors[1][word : word + 1, :]


def encode(exact, sums, edges, out_ref):
    tiles, share, _ = exact.shape
    words = tiles // 2
    body = words * share
    out_ref[body + words : body + words + REACH, :] = sums
    out_ref[body + words + REACH :, :] = edges
    scales, steps = [], []
    for i in range(2):
        tops = [jnp.max(jnp.abs(exact[2 * word + i]), axis=0, keepdims=True) for word in range(words)]
        scale = jnp.floor(jnp.concatenate(tops, axis=0) * (1.0 / UNIT)).astype(jnp.int32) + 1
        scales.append(scale)
        steps.append(32767.0 / (scale.astype(jnp.float32) * UNIT))
    out_ref[body : body + words, :] = (scales[1] << 16) | scales[0]
    for word in range(words):
        low, high = [
            jnp.floor(exact[2 * word + i] * steps[i][word : word + 1, :] + 0.5).astype(jnp.int32) for i in range(2)
        ]
        out_ref[word * share : (word + 1) * share, :] = (high << 16) | (low & 65535)


def pair_kernel(
    partners_ref, left_ref, right_ref, own_ref, vals_ref, hot_ref, early_ref, own_sums_ref, _,
    cov_ref, edge_ref, sums_ref, up_ref, down_ref,
):
    blocks, slots = partners_ref.shape
    mine = blocks // 2
    shots = own_ref.shape[0]
    groups = cov_ref.shape[0]
    width = cov_ref.shape[3]
    pieces = hot_ref.shape[2] // width
    me = lax.axis_index("shot")
    base = group_index() * blocks
    halves = [ref[...] for ref in (left_ref, right_ref)]
    halo_sums = [row_sums(halo) for halo in halves]
    products, others = [], []
    for block in range(blocks):
        side = block // mine
        halo = halves[side]
        offsets = [w + (blocks if side else -HALO) for w in range(HALO)]
        own = own_ref[:, block * width : (block + 1) * width]
        reached = [w for w in range(HALO) if abs(block - offsets[w]) <= HALO]
        first, last = reached[0] * width, (reached[-1] + 1) * width
        tiles = lax.dot_general(
            own, halo[:, first:last], (((0,), (0,)), ((), ())), preferred_element_type=jnp.float32
        )
        tiles = tiles - sums_of(own) * (halo_sums[side][:, first:last] * (1.0 / shots))
        for n, w in enumerate(reached):
            for k in range(1, slots):
                partner = partners_ref[block, k]

                @pl.when((partner >= 0) & (partner == base + offsets[w]))
                def _():
                    spread(cov_ref, block * slots + k, tiles[:, n * width : (n + 1) * width], me)

        other = jnp.dot(halo[:, first:last], hot_ref[block, first:last, :], preferred_element_type=jnp.float32)
        product = jnp.sum(vals_ref[block].astype(jnp.float32) * other, axis=0, keepdims=True)
        products += rows_of(product, pieces)
        others += rows_of(jnp.sum(other, axis=0, keepdims=True), pieces)
    count = blocks * pieces
    sums = fixed(
        jnp.concatenate(rows_of(halo_sums[0], HALO) + [own_sums_ref[...]] + rows_of(halo_sums[1], HALO), axis=0)
    )
    edges = early_ref[...] + jnp.concatenate(
        products + [jnp.zeros((count, width), jnp.float32)] + others, axis=0
    )
    edges = fixed(edges)
    sums_ref[...] = sums
    edge_ref[...] = edges
    encode(cov_ref.at[groups // 2], sums, edges, up_ref)
    encode(cov_ref.at[groups // 2 + 1], sums, edges, down_ref)


def pair_call(partners, left, right, soft, vals, hot, early, own_sums, cov):
    _, tiles, share, width = cov.shape
    message = jax.ShapeDtypeStruct((tiles // 2 * share + TAIL, width), jnp.int32)
    return pl.pallas_call(
        pair_kernel,
        out_shape=[
            jax.ShapeDtypeStruct(cov.shape, jnp.float32),
            jax.ShapeDtypeStruct(early.shape, jnp.int32),
            jax.ShapeDtypeStruct((REACH, width), jnp.int32),
            message,
            message,
        ],
        in_specs=[SMEM] + [VMEM] * 8,
        out_specs=[VMEM] * 5,
        input_output_aliases={8: 0},
        compiler_params=PARAMS,
        cost_estimate=pl.CostEstimate(flops=2_000_000_000, bytes_accessed=4_000_000, transcendentals=0),
    )(partners, left, right, soft, vals, hot, early, own_sums, cov)


def picked(pick_ref, rows):
    total = pick_ref[0] * rows[0:1, :]
    for w in range(1, REACH):
        total = total + pick_ref[w] * rows[w : w + 1, :]
    return total


def hop_kernel(at, seen, came_ref, cov_ref, edge_ref, sums_ref, pick_ref, _, out_ref, exact):
    groups, tiles, share, width = cov_ref.shape
    words = tiles // 2
    body = words * share
    blocks = REACH - 2 * HALO
    slots = tiles // blocks
    old = came_ref[body + words : body + words + REACH, :]
    sums = sums_ref[...]
    shift = old.astype(jnp.float32) * (1.0 / (SCALE * SHOTS * seen)) - sums.astype(jnp.float32) * (
        1.0 / (SCALE * SHOTS)
    )
    others = picked(pick_ref, shift)
    factors = factors_of(came_ref, words)
    dest = lax.rem(lax.axis_index("shot") + at, groups)
    for block in range(blocks):
        column = column_of(shift[block + HALO : block + HALO + 1, :], dest * share, share)
        column = column * (float(SHOTS) * seen / (seen + 1))
        for pair in range(slots // 2):
            word = block * (slots // 2) + pair
            came = words_of(came_ref, word, share, factors)
            for i in range(2):
                tile = 2 * word + i
                exact[tile] = cov_ref[at, tile] + came[i] + column * others[tile : tile + 1, :]
    encode(exact, sums + old, edge_ref[...] + came_ref[body + words + REACH :, :], out_ref)


def hop_call(at, seen, came, parts, after):
    tiles, share, width = parts[0].shape[1:]
    return pl.pallas_call(
        functools.partial(hop_kernel, at, seen),
        out_shape=jax.ShapeDtypeStruct(came.shape, jnp.int32),
        in_specs=[VMEM] * 5 + [ANY],
        out_specs=VMEM,
        scratch_shapes=[pltpu.VMEM((tiles, share, width), jnp.float32)],
        compiler_params=PARAMS,
        cost_estimate=pl.CostEstimate(flops=1_000_000, bytes_accessed=600_000, transcendentals=0),
    )(came, *parts, after)


def final_kernel(
    rises, falls, inc_ref, rising_ref, falling_ref, cov_ref, edge_ref, sums_ref, pick_ref, fit_ref,
    pair_ref, grad_ref,
):
    groups, tiles, share, width = cov_ref.shape
    words = tiles // 2
    body = words * share
    blocks, slots = pair_ref.shape[:2]
    pieces = inc_ref.shape[2] // width
    count = float(SHOTS * groups)
    start = lax.axis_index("shot") * share
    sums = sums_ref[...]
    rise_sums = rising_ref[body + words : body + words + REACH, :]
    fall_sums = falling_ref[body + words : body + words + REACH, :]

    def mean(values, sources):
        return values.astype(jnp.float32) * (1.0 / (SCALE * SHOTS * sources))

    first_shift = mean(rise_sums, rises) - mean(sums, 1)
    second_shift = mean(fall_sums, falls) - mean(sums + rise_sums, rises + 1)
    totals = (sums + rise_sums + fall_sums).astype(jnp.float32) * (1.0 / SCALE)
    firsts, seconds, alls = picked(pick_ref, first_shift), picked(pick_ref, second_shift), picked(pick_ref, totals)
    first_weight = float(SHOTS) * rises / (rises + 1)
    second_weight = float(SHOTS) * falls * (rises + 1) / (rises + 1 + falls)
    edges = edge_ref[...] + rising_ref[body + words + REACH :, :] + falling_ref[body + words + REACH :, :]
    edges = edges.astype(jnp.float32) * (1.0 / SCALE)
    risen_factors, fallen_factors = factors_of(rising_ref, words), factors_of(falling_ref, words)
    for block in range(blocks):
        own = slice(block + HALO, block + HALO + 1)
        first_column = column_of(first_shift[own, :], start, share) * first_weight
        second_column = column_of(second_shift[own, :], start, share) * second_weight
        total_column = column_of(totals[own, :], start, share) * (1.0 / count)
        for pair in range(slots // 2):
            word = block * (slots // 2) + pair
            risen = words_of(rising_ref, word, share, risen_factors)
            fallen = words_of(falling_ref, word, share, fallen_factors)
            for i in range(2):
                row = slice(2 * word + i, 2 * word + i + 1)
                cov = cov_ref[0, 2 * word + i] + risen[i] + first_column * firsts[row, :]
                cov = cov + fallen[i] + second_column * seconds[row, :]
                alone = total_column * alls[row, :]
                entry = 0.5 - 0.5 * jnp.sqrt(alone / (alone + cov))
                pair_ref[block, 2 * pair + i] = (entry * pick_ref[REACH, row, :]).astype(jnp.bfloat16)
        for p in range(pieces):
            n = block * pieces + p
            at = slice(p * width, (p + 1) * width)
            slot_x = inc_ref[1, block : block + 1, at]
            live = jnp.zeros((1, width), jnp.float32)
            for k in range(slots):
                tile = block * slots + k
                live = live + jnp.where(slot_x == k, pick_ref[REACH, tile : tile + 1, :], 0.0)
            rows = blocks * pieces
            quotient = (edges[rows + n : rows + n + 1] / count) * (
                edges[2 * rows + n : 2 * rows + n + 1] / count
            ) * count / edges[n : n + 1]
            entry = (0.5 - 0.5 * jnp.sqrt(quotient)) * live
            residual = live * (entry - fit_ref[block : block + 1, at]) / NOISE_SPREAD
            grad_ref[block : block + 1, at] = -residual / NOISE_SPREAD


def final_call(slots, incidence, rising, falling, parts, fit):
    groups, tiles, share, width = parts[0].shape
    half = groups // 2
    return pl.pallas_call(
        functools.partial(final_kernel, half, groups - 1 - half),
        out_shape=[
            jax.ShapeDtypeStruct((tiles // slots, slots, share, width), jnp.bfloat16),
            jax.ShapeDtypeStruct((tiles // slots, incidence.shape[2]), jnp.float32),
        ],
        in_specs=[VMEM] * 8,
        out_specs=[VMEM] * 2,
        compiler_params=PARAMS,
        cost_estimate=pl.CostEstimate(flops=1_000_000, bytes_accessed=2_000_000, transcendentals=100_000),
    )(incidence, rising, falling, *parts, fit)


def local(soft, partners, incidence, edge_prob):
    shots, own_width = soft.shape
    blocks, slots = partners.shape
    width = own_width // blocks
    groups = lax.axis_size("shot")
    sides = lax.axis_size(("row", "col"))

    head, tail, cut = cut_call(soft, HALO * width)
    left = lax.ppermute(tail, ("row", "col"), [(i, (i + 1) % sides) for i in range(sides)])
    right = lax.ppermute(head, ("row", "col"), [((i + 1) % sides, i) for i in range(sides)])

    keys = incidence[1] * (width * width) + incidence[0] * width + incidence[2]
    fit, vals, hot, cov, early, own_sums, pick = ready_call(
        partners, soft, incidence, keys.T, edge_prob.T, cut, width, groups
    )
    cov, edges, sums, up, down = pair_call(partners, left, right, soft, vals, hot, early, own_sums, cov)
    parts = (cov, edges, sums, pick)

    half = groups // 2
    rise = [(i, (i + 1) % groups) for i in range(groups)]
    fall = [(b, a) for a, b in rise]
    rising = lax.ppermute(up, "shot", rise)
    falling = lax.ppermute(down, "shot", fall)
    order = down
    for step in range(1, half):
        order = hop_call(half - step, step, rising, parts, order)
        rising = lax.ppermute(order, "shot", rise)
        if step < half - 1:
            order = hop_call(half + 1 + step, step, falling, parts, order)
            falling = lax.ppermute(order, "shot", fall)
    return final_call(slots, incidence, rising, falling, parts, fit)


def solution(mesh):
    placed = (
        P("shot", ("row", "col")),
        P(("row", "col"), None),
        P(None, ("row", "col"), None),
        P(("row", "col"), None),
    )
    return jax.shard_map(
        local,
        mesh=mesh,
        in_specs=placed,
        out_specs=(P(("row", "col"), None, "shot", None), P(("row", "col"), None)),
        check_vma=False,
    )
```

```python
import functools

import jax
import jax.numpy as jnp
from jax import lax
from jax.experimental import pallas as pl
from jax.experimental.pallas import tpu as pltpu
from jax.sharding import PartitionSpec as P

HALO = 2
REACH = 8
NOISE_SPREAD = 0.05
SCALE = 131072.0
UNIT = 1600.0 / 65535.0
SHOTS = 768
TAIL = 32
ANY = pl.BlockSpec(memory_space=pl.ANY)
VMEM = pl.BlockSpec(memory_space=pltpu.VMEM)
SMEM = pl.BlockSpec(memory_space=pltpu.SMEM)
HBM = pl.BlockSpec(memory_space=pltpu.HBM)
PARAMS = pltpu.CompilerParams(vmem_limit_bytes=20 * 1024 * 1024)


def fixed(values):
    return jnp.floor(values * SCALE + 0.5).astype(jnp.int32)


def column_of(row, first, count):
    spot = lax.broadcasted_iota(jnp.int32, (count, row.shape[1]), 1) == (
        lax.broadcasted_iota(jnp.int32, (count, row.shape[1]), 0) + first
    )
    return jnp.sum(jnp.where(spot, row, 0.0), axis=1, keepdims=True)


def group_index():
    return lax.axis_index("row") * lax.axis_size("col") + lax.axis_index("col")


def row_sums(values):
    ones = jnp.ones((8, values.shape[0]), jnp.bfloat16)
    return jnp.dot(ones, values, preferred_element_type=jnp.float32)[0:1, :]


def sums_of(values):
    ones = jnp.ones((values.shape[0], 128), jnp.bfloat16)
    return lax.dot_general(values, ones, (((0,), (0,)), ((), ())), preferred_element_type=jnp.float32)[:, 0:1]


def cut_kernel(soft_ref, head_ref, tail_ref, done_ref, sems):
    width = soft_ref.shape[1]
    reach = head_ref.shape[1]
    copies = [
        pltpu.make_async_copy(soft_ref.at[:, pl.ds(width - reach, reach)], tail_ref, sems.at[0]),
        pltpu.make_async_copy(soft_ref.at[:, pl.ds(0, reach)], head_ref, sems.at[1]),
    ]
    for copy in copies:
        copy.start()
    done_ref[...] = jnp.zeros_like(done_ref)
    for copy in copies:
        copy.wait()


def cut_call(soft, reach):
    shape = jax.ShapeDtypeStruct((soft.shape[0], reach), soft.dtype)
    return pl.pallas_call(
        cut_kernel,
        out_shape=[shape, shape, jax.ShapeDtypeStruct((8, 128), jnp.float32)],
        in_specs=[HBM],
        out_specs=[VMEM, VMEM, VMEM],
        scratch_shapes=[pltpu.SemaphoreType.DMA((2,))],
        compiler_params=pltpu.CompilerParams(vmem_limit_bytes=50 * 1024 * 1024),
        cost_estimate=pl.CostEstimate(flops=0, bytes_accessed=3_000_000, transcendentals=0),
    )(soft)


def spread(cov_ref, slot, tile, me):
    groups, _, share, _ = cov_ref.shape
    for d in range(groups):
        at = lax.rem(d - me + groups, groups)
        cov_ref[at, slot] = tile[d * share : (d + 1) * share, :]


def rows_of(row, pieces):
    width = row.shape[1] // pieces
    return [row[:, p * width : (p + 1) * width] for p in range(pieces)]


def ready_kernel(
    width, partners_ref, soft_ref, inc_ref, keyt_ref, probt_ref, _,
    fit_ref, vals_ref, hot_ref, cov_ref, early_ref, sums_ref, pick_ref, own_ref, sem,
):
    blocks, slots = partners_ref.shape
    mine = blocks // 2
    shots = own_ref.shape[0]
    edges = inc_ref.shape[2]
    pieces = edges // width
    me = lax.axis_index("shot")
    base = group_index() * blocks
    fetch = pltpu.make_async_copy(soft_ref, own_ref, sem)
    fetch.start()
    for b in range(blocks):
        key = inc_ref[1, b : b + 1, :] * (width * width) + inc_ref[0, b : b + 1, :] * width + inc_ref[2, b : b + 1, :]
        same = keyt_ref[:, b : b + 1] == key
        fit_ref[b : b + 1, :] = jnp.sum(jnp.where(same, probt_ref[:, b : b + 1], 0.0), axis=0, keepdims=True)
    fetch.wait()
    lines = lax.broadcasted_iota(jnp.int32, (width, edges), 0)
    products, others = [], []
    for b in range(blocks):
        own = own_ref[:, b * width : (b + 1) * width]
        rows_x = inc_ref[0, b : b + 1, :]
        slot_x = inc_ref[1, b : b + 1, :]
        cols_x = inc_ref[2, b : b + 1, :]
        halo_first = base - HALO if b < mine else base + blocks
        chosen, hot = [], []
        far = [jnp.full((1, edges), -1, jnp.int32) for _ in range(HALO)]
        for k in range(slots):
            partner = partners_ref[b, k]
            tile = b * slots + k
            pick_ref[REACH, tile : tile + 1, :] = jnp.where(
                jnp.full((1, width), partner, jnp.int32) >= 0, 1.0, 0.0
            )
            partner = jnp.where(partner >= 0, partner, base + b)
            for w in range(REACH):
                pick_ref[w, tile : tile + 1, :] = jnp.where(
                    jnp.full((1, width), partner - base + HALO, jnp.int32) == w, 1.0, 0.0
                )
            inside = (partner >= base) & (partner < base + blocks)
            start = pl.multiple_of(jnp.where(inside, partner - base, b) * width, width)
            chosen.append(own_ref[:, pl.ds(start, width)])
            here = slot_x == k
            hot.append((lines == jnp.where(here & inside, cols_x, -1)).astype(jnp.bfloat16))
            for w in range(HALO):
                there = here & (partner == halo_first + w) & jnp.logical_not(inside)
                far[w] = jnp.where(there, cols_x, far[w])
        for w in range(HALO):
            hot_ref[b, w * width : (w + 1) * width, :] = (lines == far[w]).astype(jnp.bfloat16)
        chosen = jnp.concatenate(chosen, axis=1)
        tiles = lax.dot_general(own, chosen, (((0,), (0,)), ((), ())), preferred_element_type=jnp.float32)
        tiles = tiles - sums_of(own) * (row_sums(chosen) * (1.0 / shots))
        for k in range(slots):
            spread(cov_ref, b * slots + k, tiles[:, k * width : (k + 1) * width], me)
        vals = jnp.dot(own, (lines == rows_x).astype(jnp.bfloat16), preferred_element_type=jnp.float32)
        vals_ref[b] = vals.astype(jnp.bfloat16)
        other = jnp.dot(chosen, jnp.concatenate(hot, axis=0), preferred_element_type=jnp.float32)
        products += rows_of(jnp.sum(vals * other, axis=0, keepdims=True), pieces)
        others += rows_of(jnp.sum(other, axis=0, keepdims=True), pieces)
    early_ref[...] = jnp.concatenate(products + others, axis=0)
    sums_ref[...] = jnp.concatenate(rows_of(row_sums(own_ref[...]), blocks), axis=0)


def ready_call(partners, soft, incidence, keys_t, prob_t, after, width, groups):
    shots = soft.shape[0]
    blocks, slots = partners.shape
    edges = incidence.shape[2]
    return pl.pallas_call(
        functools.partial(ready_kernel, width),
        out_shape=[
            jax.ShapeDtypeStruct((blocks, edges), jnp.float32),
            jax.ShapeDtypeStruct((blocks, shots, edges), jnp.bfloat16),
            jax.ShapeDtypeStruct((blocks, HALO * width, edges), jnp.bfloat16),
            jax.ShapeDtypeStruct((groups, blocks * slots, width // groups, width), jnp.float32),
            jax.ShapeDtypeStruct((2 * blocks * edges // width, width), jnp.float32),
            jax.ShapeDtypeStruct((blocks, width), jnp.float32),
            jax.ShapeDtypeStruct((REACH + 1, blocks * slots, width), jnp.float32),
        ],
        in_specs=[SMEM, ANY] + [VMEM] * 3 + [ANY],
        out_specs=[VMEM] * 7,
        scratch_shapes=[pltpu.VMEM(soft.shape, soft.dtype), pltpu.SemaphoreType.DMA],
        compiler_params=PARAMS,
        cost_estimate=pl.CostEstimate(flops=20_000_000_000, bytes_accessed=12_000_000, transcendentals=0),
    )(partners, soft, incidence, keys_t, prob_t, after)


def factors_of(came_ref, words):
    scales = came_ref[came_ref.shape[0] - TAIL : came_ref.shape[0] - TAIL + words, :]
    step = UNIT / 32767.0
    low = (scales & 65535).astype(jnp.float32) * step
    return low, lax.shift_right_logical(scales, 16).astype(jnp.float32) * step


def words_of(came_ref, word, share, factors):
    words = came_ref[word * share : (word + 1) * share, :]
    low = lax.shift_right_arithmetic(words << 16, 16).astype(jnp.float32)
    high = lax.shift_right_arithmetic(words, 16).astype(jnp.float32)
    return low * factors[0][word : word + 1, :], high * factors[1][word : word + 1, :]


def encode(exact, sums, edges, out_ref):
    tiles, share, _ = exact.shape
    words = tiles // 2
    body = words * share
    out_ref[body + words : body + words + REACH, :] = sums
    out_ref[body + words + REACH :, :] = edges
    scales, steps = [], []
    for i in range(2):
        tops = [jnp.max(jnp.abs(exact[2 * word + i]), axis=0, keepdims=True) for word in range(words)]
        scale = jnp.floor(jnp.concatenate(tops, axis=0) * (1.0 / UNIT)).astype(jnp.int32) + 1
        scales.append(scale)
        steps.append(32767.0 / (scale.astype(jnp.float32) * UNIT))
    out_ref[body : body + words, :] = (scales[1] << 16) | scales[0]
    for word in range(words):
        low, high = [
            jnp.floor(exact[2 * word + i] * steps[i][word : word + 1, :] + 0.5).astype(jnp.int32) for i in range(2)
        ]
        out_ref[word * share : (word + 1) * share, :] = (high << 16) | (low & 65535)


def pair_kernel(
    partners_ref, left_ref, right_ref, own_ref, vals_ref, hot_ref, early_ref, own_sums_ref, _,
    cov_ref, edge_ref, sums_ref, up_ref, down_ref,
):
    blocks, slots = partners_ref.shape
    mine = blocks // 2
    shots = own_ref.shape[0]
    groups = cov_ref.shape[0]
    width = cov_ref.shape[3]
    pieces = hot_ref.shape[2] // width
    me = lax.axis_index("shot")
    base = group_index() * blocks
    halves = [ref[...] for ref in (left_ref, right_ref)]
    halo_sums = [row_sums(halo) for halo in halves]
    products, others = [], []
    for block in range(blocks):
        side = block // mine
        halo = halves[side]
        offsets = [w + (blocks if side else -HALO) for w in range(HALO)]
        own = own_ref[:, block * width : (block + 1) * width]
        reached = [w for w in range(HALO) if abs(block - offsets[w]) <= HALO]
        first, last = reached[0] * width, (reached[-1] + 1) * width
        tiles = lax.dot_general(
            own, halo[:, first:last], (((0,), (0,)), ((), ())), preferred_element_type=jnp.float32
        )
        tiles = tiles - sums_of(own) * (halo_sums[side][:, first:last] * (1.0 / shots))
        for n, w in enumerate(reached):
            for k in range(1, slots):
                partner = partners_ref[block, k]

                @pl.when((partner >= 0) & (partner == base + offsets[w]))
                def _():
                    spread(cov_ref, block * slots + k, tiles[:, n * width : (n + 1) * width], me)

        other = jnp.dot(halo[:, first:last], hot_ref[block, first:last, :], preferred_element_type=jnp.float32)
        product = jnp.sum(vals_ref[block].astype(jnp.float32) * other, axis=0, keepdims=True)
        products += rows_of(product, pieces)
        others += rows_of(jnp.sum(other, axis=0, keepdims=True), pieces)
    sums = fixed(
        jnp.concatenate(rows_of(halo_sums[0], HALO) + [own_sums_ref[...]] + rows_of(halo_sums[1], HALO), axis=0)
    )
    edges = early_ref[...] + jnp.concatenate(products + others, axis=0)
    edges = fixed(edges)
    sums_ref[...] = sums
    edge_ref[...] = edges
    encode(cov_ref.at[groups // 2], sums, edges, up_ref)
    encode(cov_ref.at[groups // 2 + 1], sums, edges, down_ref)


def pair_call(partners, left, right, soft, vals, hot, early, own_sums, cov):
    _, tiles, share, width = cov.shape
    message = jax.ShapeDtypeStruct((tiles // 2 * share + TAIL, width), jnp.int32)
    return pl.pallas_call(
        pair_kernel,
        out_shape=[
            jax.ShapeDtypeStruct(cov.shape, jnp.float32),
            jax.ShapeDtypeStruct(early.shape, jnp.int32),
            jax.ShapeDtypeStruct((REACH, width), jnp.int32),
            message,
            message,
        ],
        in_specs=[SMEM] + [VMEM] * 8,
        out_specs=[VMEM] * 5,
        input_output_aliases={8: 0},
        compiler_params=PARAMS,
        cost_estimate=pl.CostEstimate(flops=2_000_000_000, bytes_accessed=4_000_000, transcendentals=0),
    )(partners, left, right, soft, vals, hot, early, own_sums, cov)


def picked(pick_ref, rows):
    total = pick_ref[0] * rows[0:1, :]
    for w in range(1, REACH):
        total = total + pick_ref[w] * rows[w : w + 1, :]
    return total


def hop_kernel(at, seen, came_ref, cov_ref, edge_ref, sums_ref, pick_ref, _, out_ref, exact):
    groups, tiles, share, width = cov_ref.shape
    words = tiles // 2
    body = words * share
    blocks = REACH - 2 * HALO
    slots = tiles // blocks
    old = came_ref[body + words : body + words + REACH, :]
    sums = sums_ref[...]
    shift = old.astype(jnp.float32) * (1.0 / (SCALE * SHOTS * seen)) - sums.astype(jnp.float32) * (
        1.0 / (SCALE * SHOTS)
    )
    others = picked(pick_ref, shift)
    factors = factors_of(came_ref, words)
    dest = lax.rem(lax.axis_index("shot") + at, groups)
    for block in range(blocks):
        column = column_of(shift[block + HALO : block + HALO + 1, :], dest * share, share)
        column = column * (float(SHOTS) * seen / (seen + 1))
        for pair in range(slots // 2):
            word = block * (slots // 2) + pair
            came = words_of(came_ref, word, share, factors)
            for i in range(2):
                tile = 2 * word + i
                exact[tile] = cov_ref[at, tile] + came[i] + column * others[tile : tile + 1, :]
    encode(exact, sums + old, edge_ref[...] + came_ref[body + words + REACH :, :], out_ref)


def hop_call(at, seen, came, parts, after):
    tiles, share, width = parts[0].shape[1:]
    return pl.pallas_call(
        functools.partial(hop_kernel, at, seen),
        out_shape=jax.ShapeDtypeStruct(came.shape, jnp.int32),
        in_specs=[VMEM] * 5 + [ANY],
        out_specs=VMEM,
        scratch_shapes=[pltpu.VMEM((tiles, share, width), jnp.float32)],
        compiler_params=PARAMS,
        cost_estimate=pl.CostEstimate(flops=1_000_000, bytes_accessed=600_000, transcendentals=0),
    )(came, *parts, after)


def final_kernel(
    rises, falls, inc_ref, rising_ref, falling_ref, cov_ref, edge_ref, sums_ref, pick_ref, fit_ref,
    pair_ref, grad_ref,
):
    groups, tiles, share, width = cov_ref.shape
    words = tiles // 2
    body = words * share
    blocks, slots = pair_ref.shape[:2]
    pieces = inc_ref.shape[2] // width
    count = float(SHOTS * groups)
    start = lax.axis_index("shot") * share
    sums = sums_ref[...]
    rise_sums = rising_ref[body + words : body + words + REACH, :]
    fall_sums = falling_ref[body + words : body + words + REACH, :]

    def mean(values, sources):
        return values.astype(jnp.float32) * (1.0 / (SCALE * SHOTS * sources))

    first_shift = mean(rise_sums, rises) - mean(sums, 1)
    second_shift = mean(fall_sums, falls) - mean(sums + rise_sums, rises + 1)
    totals = (sums + rise_sums + fall_sums).astype(jnp.float32) * (1.0 / SCALE)
    firsts, seconds, alls = picked(pick_ref, first_shift), picked(pick_ref, second_shift), picked(pick_ref, totals)
    first_weight = float(SHOTS) * rises / (rises + 1)
    second_weight = float(SHOTS) * falls * (rises + 1) / (rises + 1 + falls)
    edges = edge_ref[...] + rising_ref[body + words + REACH :, :] + falling_ref[body + words + REACH :, :]
    edges = edges.astype(jnp.float32) * (1.0 / SCALE)
    risen_factors, fallen_factors = factors_of(rising_ref, words), factors_of(falling_ref, words)
    for block in range(blocks):
        own = slice(block + HALO, block + HALO + 1)
        first_column = column_of(first_shift[own, :], start, share) * first_weight
        second_column = column_of(second_shift[own, :], start, share) * second_weight
        total_column = column_of(totals[own, :], start, share) * (1.0 / count)
        for pair in range(slots // 2):
            word = block * (slots // 2) + pair
            risen = words_of(rising_ref, word, share, risen_factors)
            fallen = words_of(falling_ref, word, share, fallen_factors)
            for i in range(2):
                row = slice(2 * word + i, 2 * word + i + 1)
                cov = cov_ref[0, 2 * word + i] + risen[i] + first_column * firsts[row, :]
                cov = cov + fallen[i] + second_column * seconds[row, :]
                alone = total_column * alls[row, :]
                entry = 0.5 - 0.5 * jnp.sqrt(alone / (alone + cov))
                pair_ref[block, 2 * pair + i] = (entry * pick_ref[REACH, row, :]).astype(jnp.bfloat16)
        column = column_of(totals[own, :], 0, width)
        for p in range(pieces):
            n = block * pieces + p
            at = slice(p * width, (p + 1) * width)
            here = lax.broadcasted_iota(jnp.int32, (width, width), 0) == inc_ref[0, block : block + 1, at]
            first = jnp.sum(jnp.where(here, column, 0.0), axis=0, keepdims=True)
            slot_x = inc_ref[1, block : block + 1, at]
            live = jnp.zeros((1, width), jnp.float32)
            for k in range(slots):
                tile = block * slots + k
                live = live + jnp.where(slot_x == k, pick_ref[REACH, tile : tile + 1, :], 0.0)
            rows = blocks * pieces
            quotient = (first / count) * (
                edges[rows + n : rows + n + 1] / count
            ) * count / edges[n : n + 1]
            entry = (0.5 - 0.5 * jnp.sqrt(quotient)) * live
            residual = live * (entry - fit_ref[block : block + 1, at]) / NOISE_SPREAD
            grad_ref[block : block + 1, at] = -residual / NOISE_SPREAD


def final_call(slots, incidence, rising, falling, parts, fit):
    groups, tiles, share, width = parts[0].shape
    half = groups // 2
    return pl.pallas_call(
        functools.partial(final_kernel, half, groups - 1 - half),
        out_shape=[
            jax.ShapeDtypeStruct((tiles // slots, slots, share, width), jnp.bfloat16),
            jax.ShapeDtypeStruct((tiles // slots, incidence.shape[2]), jnp.float32),
        ],
        in_specs=[VMEM] * 8,
        out_specs=[VMEM] * 2,
        compiler_params=PARAMS,
        cost_estimate=pl.CostEstimate(flops=1_000_000, bytes_accessed=2_000_000, transcendentals=100_000),
    )(incidence, rising, falling, *parts, fit)


def local(soft, partners, incidence, edge_prob):
    shots, own_width = soft.shape
    blocks, slots = partners.shape
    width = own_width // blocks
    groups = lax.axis_size("shot")
    sides = lax.axis_size(("row", "col"))

    head, tail, cut = cut_call(soft, HALO * width)
    left = lax.ppermute(tail, ("row", "col"), [(i, (i + 1) % sides) for i in range(sides)])
    right = lax.ppermute(head, ("row", "col"), [((i + 1) % sides, i) for i in range(sides)])

    keys = incidence[1] * (width * width) + incidence[0] * width + incidence[2]
    fit, vals, hot, cov, early, own_sums, pick = ready_call(
        partners, soft, incidence, keys.T, edge_prob.T, cut, width, groups
    )
    cov, edges, sums, up, down = pair_call(partners, left, right, soft, vals, hot, early, own_sums, cov)
    parts = (cov, edges, sums, pick)

    half = groups // 2
    rise = [(i, (i + 1) % groups) for i in range(groups)]
    fall = [(b, a) for a, b in rise]
    rising = lax.ppermute(up, "shot", rise)
    falling = lax.ppermute(down, "shot", fall)
    order = down
    for step in range(1, half):
        order = hop_call(half - step, step, rising, parts, order)
        rising = lax.ppermute(order, "shot", rise)
        if step < half - 1:
            order = hop_call(half + 1 + step, step, falling, parts, order)
            falling = lax.ppermute(order, "shot", fall)
    return final_call(slots, incidence, rising, falling, parts, fit)


def solution(mesh):
    placed = (
        P("shot", ("row", "col")),
        P(("row", "col"), None),
        P(None, ("row", "col"), None),
        P(("row", "col"), None),
    )
    return jax.shard_map(
        local,
        mesh=mesh,
        in_specs=placed,
        out_specs=(P(("row", "col"), None, "shot", None), P(("row", "col"), None)),
        check_vma=False,
    )
```
